128 devices in a mesh: seq: 16 (over z, x_lo, core), fsdp: 8 (over y, x_hi).
Axes of the slice: x: 4 (x_hi: 2, x_lo: 2; x = x_hi * 2 + x_lo), y: 4, z: 4, core: 2. Of those that a mesh axis runs over, the one named last changes fastest.
Arguments:
- tokens: bfloat16 [8, 2048, 2048], P('fsdp', 'seq'), may hold values from -6 to 6
- positions: int32 [8, 2048], P('fsdp'), may hold values from 0 to 3071, as said below
- routes: int32 [8, 2048, 2], P('fsdp', 'seq'), may hold values from 0 to 15, all different within a row; in each aligned block of 128 rows (0 to 127, 128 to 255, ..., all dimensions but the last counted through in order) at most 20 rows name the same one
- first_gain: bfloat16 [2048], P(('seq', 'fsdp')), may hold values from 0.5 to 1.5
- query_weight: bfloat16 [2048, 3072], P(('seq', 'fsdp')), may hold values from -0.125 to 0.125
- latent_weight: bfloat16 [2048, 576], P(('seq', 'fsdp')), may hold values from -0.125 to 0.125
- latent_gain: bfloat16 [512], P(('seq', 'fsdp')), may hold values from 0.5 to 1.5
- expand_weight: bfloat16 [512, 4096], P(('seq', 'fsdp')), may hold values from -0.25 to 0.25
- output_weight: bfloat16 [2048, 2048], P(('seq', 'fsdp')), may hold values from -0.75 to 0.75
- second_gain: bfloat16 [2048], P(('seq', 'fsdp')), may hold values from 0.5 to 1.5
- router_weight: bfloat16 [2048, 16], P(('seq', 'fsdp')), may hold values from -0.0625 to 0.0625
- shared_gate: bfloat16 [2048, 2816], P(('seq', 'fsdp')), may hold values from -0.125 to 0.125
- shared_up: bfloat16 [2048, 2816], P(('seq', 'fsdp')), may hold values from -0.125 to 0.125
- shared_down: bfloat16 [2816, 2048], P(('seq', 'fsdp')), may hold values from -0.109375 to 0.109375
- expert_gate: bfloat16 [16, 2048, 1408], P('seq', 'fsdp'), may hold values from -0.125 to 0.125
- expert_up: bfloat16 [16, 2048, 1408], P('seq', 'fsdp'), may hold values from -0.125 to 0.125
- expert_down: bfloat16 [16, 1408, 2048], P('seq', None, 'fsdp'), may hold values from -0.15625 to 0.15625
- cotangent: bfloat16 [8, 2048, 2048], P('fsdp', 'seq'), may hold values from -6 to 6
Outputs:
- output: bfloat16 [8, 2048, 2048], P('fsdp', 'seq')
- grad_tokens: bfloat16 [8, 2048, 2048], P('fsdp', 'seq')
- grad_first_gain: float32 [2048], P(('seq', 'fsdp'))
- grad_query_weight: float32 [2048, 3072], P(('seq', 'fsdp'))
- grad_latent_weight: float32 [2048, 576], P(('seq', 'fsdp'))
- grad_latent_gain: float32 [512], P(('seq', 'fsdp'))
- grad_expand_weight: float32 [512, 4096], P(('seq', 'fsdp'))
- grad_output_weight: float32 [2048, 2048], P(('seq', 'fsdp'))
- grad_second_gain: float32 [2048], P(('seq', 'fsdp'))
- grad_router_weight: float32 [2048, 16], P(('seq', 'fsdp'))
- grad_shared_gate: float32 [2048, 2816], P(('seq', 'fsdp'))
- grad_shared_up: float32 [2048, 2816], P(('seq', 'fsdp'))
- grad_shared_down: float32 [2816, 2048], P(('seq', 'fsdp'))
- grad_expert_gate: float32 [16, 2048, 1408], P('seq', 'fsdp')
- grad_expert_up: float32 [16, 2048, 1408], P('seq', 'fsdp')
- grad_expert_down: float32 [16, 1408, 2048], P('seq', None, 'fsdp')
The draws below stay inside these ranges and needn't reach their ends.
Inputs may be any that keep to these rules, and one draw needn't show every extreme that they name: Each sequence's positions start at 0 and rise by 1 or 2 from one token to the next, by 2 at exactly 1024 of its steps. `routes`: each token names 2 different experts; among the 128 tokens of one device no expert is named more than 20 times, a bound that some block reaches.
All inputs are finite; a program needn't handle non-finite values.
Results may differ from the reference program's by a relative error of at most 0.035.
Values may be sent and summed in bfloat16 or wider, within the bound.
No kernel may reach another device: no remote copies, remote signals or barrier semaphores. Data moves between devices by JAX's collectives and lax.ppermute only.
A program may use at most 256 MiB of HBM per device.

```python
import math
import jax
import jax.numpy as jnp
import numpy as np
from jax import lax

D = 2048
HEADS = 16
NOPE = 128
ROPE = 64
VDIM = 128
KV_RANK = 512
FF = 1408
SHARED_FF = 2816
TOP = 2
TOK_DEV = 128
EXPERTS = 16
LENGTH = 2048
SEQS = 8
TOKENS = 16384
CAP = 20
BLOCK = 512


def draw_positions(key, part):
    key = jax.random.fold_in(key, 11)
    seq_keys = jax.random.split(key, SEQS)
    pattern = (jnp.arange(LENGTH - 1, dtype=jnp.int32) < LENGTH // 2).astype(jnp.int32)
    increments = jax.vmap(lambda one_key: jax.random.permutation(one_key, pattern))(seq_keys) + 1
    starts = jnp.zeros((SEQS, 1), jnp.int32)
    return jnp.concatenate([starts, jnp.cumsum(increments, axis=1).astype(jnp.int32)], axis=1).astype(jnp.int32)


def level_of(key, extent, cuts, smallest, top_value):
    level, own = 1.0, jax.random.fold_in(key, 6)
    for axis_at, blocks in cuts:
        draws = jnp.exp(jax.random.uniform(jax.random.fold_in(own, axis_at), (blocks,), jnp.float32, smallest / len(cuts), top_value / len(cuts)))
        level = level * jnp.repeat(draws, extent[axis_at] // blocks).reshape([-1 if axis == axis_at else 1 for axis in range(len(extent))])
    return level


def assign_block(stream_key, own, number, rows, amount, top, limit, skew):
    order = jax.random.permutation(stream_key, amount)
    packed, ordinary = load_shares(amount, rows * top, limit, skew, True), load_shares(amount, rows * top, limit, skew, False)
    places = jnp.arange(amount)

    def named(sizes, rotation):
        used = int((sizes > 0).sum())
        fixed = max(1, used // 4)
        moved = fixed + (places - fixed + rotation * (used - fixed)) % max(1, amount - fixed)
        return jnp.zeros((amount,), jnp.int32).at[order[jnp.where(places < fixed, places, moved)]].set(jnp.asarray(sizes, jnp.int32))

    sizes = jnp.where(number % 4 == 0, named(packed, number // 4), named(ordinary, number - number // 4 - 1))
    mixed = jax.random.permutation(jax.random.fold_in(own, 3), amount)
    donor, sink = mixed[0:amount // 2 * 2:2], mixed[1:amount // 2 * 2:2]
    slack = jnp.minimum(sizes[donor] - 1, limit - sizes[sink]) // 2
    slack = jnp.where((donor == order[0]) | (sink == order[0]) | (sizes[sink] == 0), 0, jnp.maximum(slack, 0))
    moved = jax.random.randint(jax.random.fold_in(own, 4), (amount // 2,), 0, 1 << 20) % (slack + 1)
    sizes = sizes.at[donor].add(-moved).at[sink].add(moved)
    labels = jnp.searchsorted(jnp.cumsum(sizes), jnp.arange(rows * top), side="right").astype(jnp.int32)
    table = labels.reshape(top, rows).T
    table = table[jax.random.permutation(jax.random.fold_in(own, 1), rows)]
    rotation = jax.random.randint(jax.random.fold_in(own, 2), (rows, 1), 0, top)
    return jnp.take_along_axis(table, (jnp.arange(top)[None, :] + rotation) % top, axis=1)


def load_shares(count, total, reach, skew, full):
    loads = [(1 << 20) // math.isqrt(rank ** skew) + 1 for rank in range(1, count + 1)]
    largest = reach if full else min(reach, max(-(-total // count), total * loads[0] // sum(loads)))
    least = 1 if total - largest >= count - 1 else 0
    holding, rest = [largest] + [least] * (count - 1), total - largest - least * (count - 1)
    while rest > 0:
        movable = [i for i in range(1, count) if holding[i] < largest] or [i for i in range(1, count) if holding[i] < reach]
        pool, budget = sum([loads[i] for i in movable]), rest
        for i in movable:
            addition = min(reach - holding[i], max(1, budget * loads[i] // pool), rest)
            holding[i] = holding[i] + addition
            rest = rest - addition
    return np.array(holding)


def noise(own_key, shape, scale, limit, pieces=(), kind=jnp.bfloat16):
    entries = jax.random.normal(own_key, shape, jnp.float32) * scale
    if len(pieces) > 0:
        entries = level_of(own_key, shape, pieces, -0.22, 0.18) * entries
    return jnp.clip(entries, min=-limit, max=limit).astype(kind)


def setup_inputs(seed: int = 0) -> dict:
    keys = jax.random.split(jax.random.key(seed), 19)
    tokens = noise(keys[0], (SEQS, LENGTH, D), 1.0, 6.0, ((0, 8), (1, 16)))
    positions = draw_positions(jax.random.fold_in(keys[18], 71), 0)
    routes_keys = jax.random.split(jax.random.fold_in(keys[2], 1), SEQS * LENGTH // TOK_DEV)
    routes_turns = jax.random.permutation(jax.random.fold_in(keys[2], 3), SEQS * LENGTH // TOK_DEV)
    routes = jax.vmap(lambda own, number: assign_block(jax.random.fold_in(keys[2], 2), own, number, TOK_DEV, EXPERTS, TOP, CAP, 1))(routes_keys, routes_turns).reshape((SEQS, LENGTH, TOP))
    first_gain = jnp.clip(1.0 + 0.1 * jax.random.normal(keys[3], (D,), jnp.float32), 0.5, 1.5).astype(jnp.bfloat16)
    query_weight = noise(keys[4], (D, HEADS * (NOPE + ROPE)), D ** -0.5, 0.125, ((0, 128),))
    latent_weight = noise(keys[5], (D, KV_RANK + ROPE), D ** -0.5, 0.125, ((0, 128),))
    latent_gain = jnp.clip(1.0 + 0.1 * jax.random.normal(keys[6], (KV_RANK,), jnp.float32), 0.5, 1.5).astype(jnp.bfloat16)
    expand_weight = noise(keys[7], (KV_RANK, HEADS * (NOPE + VDIM)), KV_RANK ** -0.5, 0.25, ((0, 128),))
    output_weight = noise(keys[8], (HEADS * VDIM, D), (HEADS * VDIM // 32) ** -0.5, 0.75, ((0, 128),))
    second_gain = jnp.clip(1.0 + 0.1 * jax.random.normal(keys[9], (D,), jnp.float32), 0.5, 1.5).astype(jnp.bfloat16)
    router_weight = noise(keys[10], (D, EXPERTS), (4 * D) ** -0.5, 0.0625, ((0, 128),))
    shared_gate = noise(keys[11], (D, SHARED_FF), D ** -0.5, 0.125, ((0, 128),))
    shared_up = noise(keys[12], (D, SHARED_FF), D ** -0.5, 0.125, ((0, 128),))
    shared_down = noise(keys[13], (SHARED_FF, D), SHARED_FF ** -0.5, 0.109375, ((0, 128),))
    expert_gate = noise(keys[14], (EXPERTS, D, FF), D ** -0.5, 0.125, ((0, 16), (1, 8)))
    expert_up = noise(keys[15], (EXPERTS, D, FF), D ** -0.5, 0.125, ((0, 16), (1, 8)))
    expert_down = noise(keys[16], (EXPERTS, FF, D), FF ** -0.5, 0.15625, ((0, 16), (2, 8)))
    cotangent = noise(keys[17], (SEQS, LENGTH, D), 1.0, 6.0, ((0, 8), (1, 16)))
    return {"tokens": tokens, "positions": positions, "routes": routes, "first_gain": first_gain, "query_weight": query_weight, "latent_weight": latent_weight, "latent_gain": latent_gain, "expand_weight": expand_weight, "output_weight": output_weight, "second_gain": second_gain, "router_weight": router_weight, "shared_gate": shared_gate, "shared_up": shared_up, "shared_down": shared_down, "expert_gate": expert_gate, "expert_up": expert_up, "expert_down": expert_down, "cotangent": cotangent}


EPSILON = 1e-06
HIGHEST = lax.Precision.HIGHEST

@jax.custom_vjp
def low(v):
    return lax.optimization_barrier(v.astype(jnp.bfloat16)).astype(jnp.float32)

@jax.custom_vjp
def low_back(v):
    return v

def low_keep(v):
    return (low(v), None)

def low_pass(kept, grad):
    return (grad,)

def back_keep(v):
    return (v, None)

def back_low(kept, grad):
    return (low(grad),)
low.defvjp(low_keep, low_pass)
low_back.defvjp(back_keep, back_low)

def matmul(left_side, right_side):
    return jnp.dot(left_side, right_side, precision=HIGHEST, preferred_element_type=jnp.float32)

def rms_norm(values, gain_vector):
    inverse = lax.rsqrt(lax.optimization_barrier(jnp.mean(values * values, axis=-1, keepdims=True)) + EPSILON)
    return values * inverse * gain_vector

def rotary_tables(position_list):
    half_rope = ROPE // 2
    frequency = jnp.exp(-(2.0 * jnp.arange(half_rope, dtype=jnp.float32) / ROPE) * math.log(10000.0))
    angles = position_list.astype(jnp.float32)[:, None] * frequency[None, :]
    return (jnp.cos(angles)[:, None, :], jnp.sin(angles)[:, None, :])

def rotate_forward(values, cosine_table, sine_table):
    half_rope = values.shape[-1] // 2
    first_part = values[..., :half_rope]
    second_part = values[..., half_rope:]
    return jnp.concatenate([first_part * cosine_table - second_part * sine_table, second_part * cosine_table + first_part * sine_table], axis=-1)

def attend_sequence(items):
    query_sent, key_sent, value_sent, position_list = items
    cosine_table, sine_table = rotary_tables(position_list)
    query_used = low(jnp.concatenate([query_sent[..., :NOPE], rotate_forward(query_sent[..., NOPE:], cosine_table, sine_table)], axis=-1))
    key_used = low(jnp.concatenate([key_sent[..., :NOPE], rotate_forward(key_sent[..., NOPE:], cosine_table, sine_table)], axis=-1))
    score_scale = (NOPE + ROPE) ** (-0.5)
    count_blocks = LENGTH // BLOCK
    query_blocks = query_used.reshape(count_blocks, BLOCK, HEADS, NOPE + ROPE)
    first_rows = jnp.arange(count_blocks, dtype=jnp.int32) * BLOCK

    def one_block(block_items):
        query_block, first_row = block_items
        scores = low_back(jnp.einsum('qhd,khd->hqk', query_block, key_used, precision=HIGHEST) * score_scale)
        row_index = first_row + jnp.arange(BLOCK, dtype=jnp.int32)
        col_index = jnp.arange(LENGTH, dtype=jnp.int32)
        allowed = col_index[None, :] <= row_index[:, None]
        scores = jnp.where(allowed[None], scores, -1e+30)
        row_top = lax.optimization_barrier(jnp.max(scores, axis=-1, keepdims=True))
        exponent = jnp.exp(scores - row_top)
        weights = low(exponent / lax.optimization_barrier(jnp.sum(exponent, axis=-1, keepdims=True)))
        return jnp.einsum('hqk,khd->qhd', weights, value_sent, precision=HIGHEST)
    attended = lax.map(jax.checkpoint(one_block), (query_blocks, first_rows))
    return attended.reshape(LENGTH, HEADS, VDIM)

def forward_function(input_rows, first_gain, query_weight, latent_weight, latent_gain, expand_weight, output_weight, second_gain, router_weight, shared_gate, shared_up, shared_down, expert_gate, expert_up, expert_down, positions, routes):
    flat_tokens = input_rows.reshape(TOKENS, D)
    normed_one = low(rms_norm(flat_tokens, first_gain))
    query_sent = low_back(low(matmul(normed_one, query_weight))).reshape(SEQS, LENGTH, HEADS, NOPE + ROPE)
    latent_all = low_back(matmul(normed_one, latent_weight))
    latent_normed = low(rms_norm(latent_all[:, :KV_RANK], latent_gain))
    expanded = matmul(latent_normed, expand_weight).reshape(TOKENS, HEADS, NOPE + VDIM)
    key_rope = jnp.broadcast_to(latent_all[:, None, KV_RANK:], (TOKENS, HEADS, ROPE))
    key_sent = low_back(low(jnp.concatenate([expanded[..., :NOPE], key_rope], axis=-1))).reshape(SEQS, LENGTH, HEADS, NOPE + ROPE)
    value_sent = low_back(low(expanded[..., NOPE:])).reshape(SEQS, LENGTH, HEADS, VDIM)
    attended = lax.map(jax.checkpoint(attend_sequence), (query_sent, key_sent, value_sent, positions))
    attended_flat = low_back(low(attended.reshape(TOKENS, HEADS * VDIM)))
    middle = flat_tokens + low_back(matmul(attended_flat, output_weight))
    normed_two = low(rms_norm(middle, second_gain))
    logits = matmul(normed_two, router_weight)
    flat_routes = routes.reshape(TOKENS, TOP)
    gate_values = jax.nn.softmax(jnp.take_along_axis(logits, flat_routes, axis=1), axis=-1)
    shared_pre = low_back(matmul(normed_two, shared_gate))
    shared_lin = low_back(matmul(normed_two, shared_up))
    shared_out = matmul(low(jax.nn.silu(shared_pre) * shared_lin), shared_down)
    route_list = flat_routes.reshape(TOKENS * TOP)
    route_hot = (route_list[:, None] == jnp.arange(EXPERTS, dtype=jnp.int32)[None, :]).astype(jnp.int32)
    slot_place = lax.optimization_barrier(jnp.sum((jnp.cumsum(route_hot, axis=0) - route_hot) * route_hot, axis=1)).astype(jnp.int32)
    room_rows = TOKENS // TOK_DEV * CAP
    repeated = jnp.repeat(normed_two, TOP, axis=0)
    buffers = low_back(jnp.zeros((EXPERTS, room_rows, D), jnp.float32).at[route_list, slot_place].set(repeated))

    def one_expert(items):
        rows_in, gate_matrix, up_matrix, down_matrix = items
        expert_pre = low_back(matmul(rows_in, gate_matrix))
        expert_linear_part = low_back(matmul(rows_in, up_matrix))
        expert_hidden = low(jax.nn.silu(expert_pre) * expert_linear_part)
        return low_back(low(matmul(expert_hidden, down_matrix)))
    results = lax.map(jax.checkpoint(one_expert), (buffers, expert_gate, expert_up, expert_down))
    picked = results[route_list, slot_place].reshape(TOKENS, TOP, D)
    routed = lax.optimization_barrier(jnp.sum(gate_values[:, :, None] * picked, axis=1))
    return (middle + shared_out + routed).reshape(SEQS, LENGTH, D)

def reference(tokens, positions, routes, first_gain, query_weight, latent_weight, latent_gain, expand_weight, output_weight, second_gain, router_weight, shared_gate, shared_up, shared_down, expert_gate, expert_up, expert_down, cotangent):

    def complete_layer(input_rows, first_norm_gain, query_projection_weight, latent_projection_weight, latent_norm_gain, expansion_weight, output_projection_weight, second_norm_gain, routing_weight, shared_gate_weight, shared_up_weight, shared_down_weight, expert_gate_weight, expert_up_weight, expert_down_weight):
        return forward_function(input_rows, first_norm_gain, query_projection_weight, latent_projection_weight, latent_norm_gain, expansion_weight, output_projection_weight, second_norm_gain, routing_weight, shared_gate_weight, shared_up_weight, shared_down_weight, expert_gate_weight, expert_up_weight, expert_down_weight, positions, routes)
    result, pullback = jax.vjp(complete_layer, tokens.astype(jnp.float32), first_gain.astype(jnp.float32), query_weight.astype(jnp.float32), latent_weight.astype(jnp.float32), latent_gain.astype(jnp.float32), expand_weight.astype(jnp.float32), output_weight.astype(jnp.float32), second_gain.astype(jnp.float32), router_weight.astype(jnp.float32), shared_gate.astype(jnp.float32), shared_up.astype(jnp.float32), shared_down.astype(jnp.float32), expert_gate.astype(jnp.float32), expert_up.astype(jnp.float32), expert_down.astype(jnp.float32))
    gradients = pullback(cotangent.astype(jnp.float32))
    return (result.astype(jnp.bfloat16), gradients[0].astype(jnp.bfloat16), gradients[1], gradients[2], gradients[3], gradients[4], gradients[5], gradients[6], gradients[7], gradients[8], gradients[9], gradients[10], gradients[11], gradients[12], gradients[13], gradients[14])
```

```python
import math

import jax
import jax.numpy as jnp
from jax import lax
from jax.experimental import pallas as pl
from jax.experimental.pallas import tpu as pltpu
from jax.sharding import Mesh
from jax.sharding import PartitionSpec as P

NOPE = 128
ROPE = 64
VDIM = 128
KV_RANK = 512
TOP = 2
UNIT_PAD = 384
SLOTS = 24
HALF = 768
EPSILON = 1e-06

SEQ = ("z", "xl", "c")
FSDP = ("y", "xh")
ZC = ("z", "c")
XYX = ("xl", "y", "xh")
ZXX = ("z", "xl", "xh")
ALL = ("z", "xl", "c", "y", "xh")
BF = jnp.bfloat16
F32 = jnp.float32


def matmul(left_side, right_side):
    return jnp.dot(left_side, right_side, preferred_element_type=F32)


def contract_rows(left_side, right_side):
    return lax.dot_general(
        left_side, right_side, (((0,), (0,)), ((), ())), preferred_element_type=F32
    )


def contract_cols(left_side, right_side):
    return lax.dot_general(
        left_side, right_side, (((1,), (1,)), ((), ())), preferred_element_type=F32
    )


def normalize(values):
    inverse = lax.rsqrt(jnp.mean(values * values, axis=-1, keepdims=True) + EPSILON)
    return (values * inverse, inverse)


def norm_back(grad_normed, gain_vector, scaled, inverse):
    grad_scaled = grad_normed * gain_vector
    grad_gain = jnp.sum(grad_normed * scaled, axis=0)
    grad_input = inverse * (
        grad_scaled - scaled * jnp.mean(grad_scaled * scaled, axis=-1, keepdims=True)
    )
    return (grad_input, grad_gain)


def rotary_tables(position_list):
    half_rope = ROPE // 2
    frequency = jnp.exp(-(2.0 * jnp.arange(half_rope, dtype=F32) / ROPE) * math.log(10000.0))
    angles = position_list.astype(F32)[:, None] * frequency[None, :]
    return (jnp.cos(angles), jnp.sin(angles))


def rotate_forward(values, cosine_table, sine_table):
    half_rope = values.shape[-1] // 2
    first_part = values[..., :half_rope]
    second_part = values[..., half_rope:]
    return jnp.concatenate(
        [
            first_part * cosine_table - second_part * sine_table,
            second_part * cosine_table + first_part * sine_table,
        ],
        axis=-1,
    )


def rotate_back(grads, cosine_table, sine_table):
    half_rope = grads.shape[-1] // 2
    first_part = grads[..., :half_rope]
    second_part = grads[..., half_rope:]
    return jnp.concatenate(
        [
            first_part * cosine_table + second_part * sine_table,
            second_part * cosine_table - first_part * sine_table,
        ],
        axis=-1,
    )


def shift(values, axis_name, step):
    count = lax.axis_size(axis_name)
    return lax.ppermute(values, axis_name, [((i + step) % count, i) for i in range(count)])


def block_scores(query_block, key_used, first_row, score_scale):
    scores = contract_cols(query_block, key_used) * score_scale
    row_index = first_row + lax.broadcasted_iota(jnp.int32, scores.shape, 0)
    col_index = lax.broadcasted_iota(jnp.int32, scores.shape, 1)
    return jnp.where(col_index <= row_index, scores, -1e30)


def group_columns(weight):
    rows, width = weight.shape[0], weight.shape[1] // 16
    return weight.reshape(rows, 4, 2, 2, width).transpose(1, 3, 0, 2, 4).reshape(8, rows, 2, width)


def ungroup_columns(parts):
    rows, width = parts.shape[1], parts.shape[3]
    return parts.reshape(4, 2, rows, 2, width).transpose(2, 0, 3, 1, 4).reshape(rows, 16 * width)


def to_replicas(rows):
    count, width = rows.shape
    blocks = jnp.broadcast_to(rows[None], (16, count, width)).reshape(16 * count, width)
    return lax.all_to_all(blocks, XYX, split_axis=0, concat_axis=0, tiled=True)


def in_row_order(rows):
    width = rows.shape[-1]
    blocks = rows.reshape(2, 8, 4, 2, 16, width).transpose(2, 0, 3, 1, 4, 5)
    return blocks.reshape(-1, width)


def exchange_all(blocks):
    return lax.all_to_all(blocks, ALL, split_axis=0, concat_axis=0, tiled=True)


def tie(*values):
    return lax.optimization_barrier(values)


def halves(gate, up, down):
    turned = down.T
    units = gate.shape[1]
    first = [part[:, :HALF] for part in (gate, up, turned)]
    second = [part[:, units - HALF :] for part in (gate, up, turned)]
    repeated = 2 * HALF - units
    keep = lax.broadcasted_iota(jnp.int32, second[0].shape, 1) >= repeated
    second = [jnp.where(keep, second[0], 0), jnp.where(keep, second[1], 0), second[2]]
    return jnp.concatenate(first, axis=-1), jnp.concatenate(second, axis=-1)


def meet(values, turn):
    pairs = [(2 * c + xh, 2 * (xh ^ turn) + c) for c in range(2) for xh in range(2)]
    return lax.ppermute(values, ("c", "xh"), pairs)


def part(values, turn):
    pairs = [(2 * c + xh, 2 * xh + (c ^ turn)) for c in range(2) for xh in range(2)]
    return lax.ppermute(values, ("c", "xh"), pairs)


def total(*terms):
    return sum(term.astype(F32) for term in terms).astype(BF)


def expert_body(at_ref, *refs):
    pieces, (own_ref, other_ref) = refs[:8], refs[8:10]
    own_out, other_out, own_kept, other_kept = refs[10:14]
    weights, sem = refs[14:]
    copies = [
        pltpu.make_async_copy(
            pieces[i], weights.at[pl.ds(pl.multiple_of(at_ref[i] * 256, 256), 256)], sem.at[i]
        )
        for i in range(8)
    ]
    for copy in copies:
        copy.start()
    for copy in copies:
        copy.wait()
    width = own_ref.shape[1] // 2
    for given, result, kept in (
        (own_ref, own_out, own_kept),
        (other_ref, other_out, other_kept),
    ):

        @pl.loop(0, HALF // 256)
        def _(n, given=given, kept=kept):
            def columns(k):
                return pl.ds(pl.multiple_of(k * HALF + n * 256, 256), 256)

            rows, grads = given[:, :width], given[:, width:]
            pre = matmul(rows, weights[:, columns(0)])
            lin = matmul(rows, weights[:, columns(1)])
            grad = matmul(grads, weights[:, columns(2)])
            sigmoid = jax.nn.sigmoid(pre)
            silu = pre * sigmoid
            kept[:, columns(0)] = (grad * lin * sigmoid * (1.0 + pre * (1.0 - sigmoid))).astype(BF)
            kept[:, columns(1)] = (grad * silu).astype(BF)
            kept[:, columns(2)] = (silu * lin).astype(BF)

        @pl.loop(0, width // 256)
        def _(f, kept=kept, result=result):
            block = weights[pl.ds(pl.multiple_of(f * 256, 256), 256), :]
            out = contract_cols(kept[:, 2 * HALF :], block[:, 2 * HALF :])
            back = contract_cols(kept[:, : 2 * HALF], block[:, : 2 * HALF])
            result[:, pl.ds(pl.multiple_of(f * 256, 256), 256)] = out.astype(BF)
            result[:, pl.ds(pl.multiple_of(width + f * 256, 256), 256)] = back.astype(BF)


def expert_rows(order, pieces, own, other):
    rows, width = own.shape
    kept = jax.ShapeDtypeStruct((rows, 3 * HALF), BF)
    result = jax.ShapeDtypeStruct((rows, width), BF)
    whole = pl.BlockSpec(memory_space=pltpu.VMEM)
    return pl.pallas_call(
        expert_body,
        out_shape=(result, result, kept, kept),
        in_specs=[pl.BlockSpec(memory_space=pltpu.SMEM)]
        + [pl.BlockSpec(memory_space=pl.ANY)] * 8
        + [whole] * 2,
        out_specs=(whole,) * 4,
        scratch_shapes=[pltpu.VMEM((width // 2, 3 * HALF), BF), pltpu.SemaphoreType.DMA((8,))],
        compiler_params=pltpu.CompilerParams(vmem_limit_bytes=56 * 2**20),
        cost_estimate=pl.CostEstimate(
            flops=2 * 2 * rows * 6 * HALF * (width // 2),
            bytes_accessed=40 * 2**20,
            transcendentals=2 * rows * HALF,
        ),
    )(order, *pieces, own, other)


def expert_grad_body(at_ref, own_rows, own_grads, other_rows, other_grads, own_kept, other_kept, out):
    out[0, :, : 2 * HALF] = (
        contract_rows(own_rows[...], own_kept[:, : 2 * HALF])
        + contract_rows(other_rows[...], other_kept[:, : 2 * HALF])
    ).astype(BF)
    out[0, :, 2 * HALF :] = (
        contract_rows(own_grads[...], own_kept[:, 2 * HALF :])
        + contract_rows(other_grads[...], other_kept[:, 2 * HALF :])
    ).astype(BF)


def expert_grads(order, own, other, own_kept, other_kept):
    rows, width = own.shape
    blocks = width // 512
    row_spec = pl.BlockSpec((rows, 256), lambda i, at: (0, at[i]))
    grad_spec = pl.BlockSpec((rows, 256), lambda i, at: (0, blocks + at[i]))
    kept_spec = pl.BlockSpec((rows, 3 * HALF), lambda i, at: (0, 0))
    return pl.pallas_call(
        expert_grad_body,
        out_shape=jax.ShapeDtypeStruct((8, 256, 3 * HALF), BF),
        grid_spec=pltpu.PrefetchScalarGridSpec(
            num_scalar_prefetch=1,
            grid=(8,),
            in_specs=[row_spec, grad_spec, row_spec, grad_spec, kept_spec, kept_spec],
            out_specs=pl.BlockSpec((1, 256, 3 * HALF), lambda i, at: (i, 0, 0)),
        ),
        compiler_params=pltpu.CompilerParams(vmem_limit_bytes=48 * 2**20),
        cost_estimate=pl.CostEstimate(
            flops=2 * 2 * rows * 3 * HALF * (width // 2),
            bytes_accessed=26 * 2**20,
            transcendentals=0,
        ),
    )(order, own, own, other, other, own_kept, other_kept)


def shared_body(rows_ref, grads_ref, gate_up_ref, down_ref, back_ref, out_ref, kept_ref):
    both = matmul(rows_ref[...], gate_up_ref[...])
    pre, lin = both[:, :UNIT_PAD], both[:, UNIT_PAD:]
    grad = contract_cols(grads_ref[...], down_ref[...])
    sigmoid = jax.nn.sigmoid(pre)
    silu = pre * sigmoid
    hidden = (silu * lin).astype(BF)
    grad_pre = (grad * lin * sigmoid * (1.0 + pre * (1.0 - sigmoid))).astype(BF)
    grad_lin = (grad * silu).astype(BF)
    kept_ref[:, :UNIT_PAD] = grad_pre
    kept_ref[:, UNIT_PAD : 2 * UNIT_PAD] = grad_lin
    kept_ref[:, 2 * UNIT_PAD :] = hidden
    back_ref[...] = contract_cols(kept_ref[:, : 2 * UNIT_PAD], gate_up_ref[...]).astype(BF)
    out_ref[...] = matmul(hidden, down_ref[...]).astype(BF)


def shared_rows(rows, grads, gate_up, down):
    count, width = rows.shape
    tile = 256
    row_spec = pl.BlockSpec((tile, width), lambda i: (i, 0))
    return pl.pallas_call(
        shared_body,
        grid=(count // tile,),
        out_shape=(
            jax.ShapeDtypeStruct((count, width), BF),
            jax.ShapeDtypeStruct((count, width), BF),
            jax.ShapeDtypeStruct((count, 3 * UNIT_PAD), BF),
        ),
        in_specs=[
            row_spec,
            row_spec,
            pl.BlockSpec(gate_up.shape, lambda i: (0, 0)),
            pl.BlockSpec(down.shape, lambda i: (0, 0)),
        ],
        out_specs=(row_spec, row_spec, pl.BlockSpec((tile, 3 * UNIT_PAD), lambda i: (i, 0))),
        compiler_params=pltpu.CompilerParams(vmem_limit_bytes=48 * 2**20),
        cost_estimate=pl.CostEstimate(
            flops=2 * count * width * 6 * UNIT_PAD,
            bytes_accessed=24 * 2**20,
            transcendentals=count * UNIT_PAD,
        ),
    )(rows, grads, gate_up, down)


def unit_columns_out(weight):
    runs = group_columns(weight).reshape(8, 16, 16, -1)
    return jnp.pad(runs, ((0, 0), (0, 0), (0, 0), (0, 24 - runs.shape[-1]))).reshape(8, 16, -1)


def unit_columns_back(parts, units):
    runs = parts.reshape(8, 16, 16, 24)[..., : units // 8]
    return ungroup_columns(runs.reshape(8, 16, 2, units))


def on_device(
    tokens,
    positions,
    routes,
    first_gain,
    query_weight,
    latent_weight,
    latent_gain,
    expand_weight,
    output_weight,
    second_gain,
    router_weight,
    shared_gate,
    shared_up,
    shared_down,
    expert_gate,
    expert_up,
    expert_down,
    cotangent,
):
    z_at, xl_at, c_at = lax.axis_index("z"), lax.axis_index("xl"), lax.axis_index("c")
    y_at, xh_at = lax.axis_index("y"), lax.axis_index("xh")
    own_tokens = tokens[0]
    row_count, width = own_tokens.shape
    length = 16 * row_count
    expert_count = router_weight.shape[1]
    units = shared_gate.shape[1] // 16

    seq_tokens = lax.all_gather(own_tokens, SEQ, axis=0, tiled=True)

    query_group = group_columns(query_weight)
    expand_group = group_columns(expand_weight).reshape(8, 16, 128)
    head_group = jnp.concatenate(
        [
            query_group[..., :NOPE].reshape(8, 16, 2 * NOPE),
            query_group[..., NOPE:].reshape(8, 16, 2 * ROPE),
            expand_group,
        ],
        axis=-1,
    )
    common = jnp.concatenate(
        [
            latent_weight,
            router_weight,
            first_gain[:, None],
            second_gain[:, None],
            jnp.pad(latent_gain, (0, 12))[:, None],
            jnp.zeros((16, 45), BF),
        ],
        axis=-1,
    )
    unit_group = jnp.concatenate(
        [unit_columns_out(weight) for weight in (shared_gate, shared_up)], axis=-1
    )
    grouped = jnp.concatenate(
        [jnp.broadcast_to(common[None], (8,) + common.shape), head_group, unit_group], axis=-1
    ).reshape(128, 1920)
    grouped = lax.all_to_all(grouped, ZC, split_axis=0, concat_axis=0, tiled=True)
    common_in = to_replicas(grouped[:, :640])

    first_half, second_half = halves(expert_gate[0], expert_up[0], expert_down[0])
    met = [
        meet(jnp.where((xh_at ^ turn) == 0, first_half, second_half), turn) for turn in range(2)
    ]
    seq_tokens, met[0], met[1], common_in = tie(seq_tokens, met[0], met[1], common_in)
    own_grad, seq_tokens = tie(cotangent[0], seq_tokens)
    seq_grad = lax.all_gather(own_grad, ZC, axis=0, tiled=True)
    head_columns, common_in = tie(grouped[:, 640:1152], common_in)
    head_in = to_replicas(head_columns)

    down_rows = jnp.concatenate(
        [output_weight, jnp.pad(shared_down, ((0, 24 - shared_down.shape[0]), (0, 0)))], axis=0
    )
    down_rows, met[0], head_in = tie(down_rows, met[0], head_in)
    down_all = to_replicas(down_rows)
    above, below = [None, None], [None, None]
    above[0], below[0] = shift(met[0], "y", 1), shift(met[0], "y", -1)

    common_in = in_row_order(common_in)
    latent_full = common_in[:, :576]
    router_full = common_in[:, 576:592]
    first_norm_gain = common_in[:, 592].astype(F32)
    second_norm_gain = common_in[:, 593].astype(F32)
    latent_norm_gain = common_in[:, 594].reshape(128, 16)[:, :4].reshape(KV_RANK).astype(F32)
    head_in = in_row_order(head_in)
    query_own = head_in[:, :384]
    expand_own = head_in[:, 384:].reshape(KV_RANK, 512)

    scaled_all, _ = normalize(seq_tokens.astype(F32))
    normed_all = (scaled_all * first_norm_gain).astype(BF)
    latent_all = matmul(normed_all, latent_full)
    scaled_latent_all, _ = normalize(latent_all[:, :KV_RANK])
    latent_normed = (scaled_latent_all * latent_norm_gain).astype(BF)
    key_rope_low = latent_all[:, KV_RANK:].astype(BF)
    normed_half = lax.dynamic_index_in_dim(
        normed_all.reshape(4, 2, 2 * row_count, width), xl_at, axis=1, keepdims=False
    ).reshape(length // 2, width)
    query_flat = matmul(normed_half, query_own).astype(BF)
    expanded = matmul(latent_normed, expand_own).astype(BF)
    cosine_table, sine_table = rotary_tables(positions[0])

    def half_rows(table):
        return lax.dynamic_index_in_dim(
            table.reshape(4, 2, 2 * row_count, -1), xl_at, axis=1, keepdims=False
        ).reshape(length // 2, -1)

    cosine_half, sine_half = half_rows(cosine_table), half_rows(sine_table)
    key_rope = rotate_forward(key_rope_low.astype(F32), cosine_table, sine_table).astype(BF)
    score_scale = (NOPE + ROPE) ** (-0.5)
    queries, keys, values = [], [], []
    for head in range(2):
        rope_at = 2 * NOPE + head * ROPE
        turned = rotate_forward(
            query_flat[:, rope_at : rope_at + ROPE].astype(F32), cosine_half, sine_half
        ).astype(BF)
        queries.append(
            jnp.concatenate([query_flat[:, head * NOPE : (head + 1) * NOPE], turned], axis=-1)
        )
        keys.append(jnp.concatenate([expanded[:, head * 256 : head * 256 + NOPE], key_rope], axis=-1))
        values.append(expanded[:, head * 256 + NOPE : (head + 1) * 256])
    block_rows = 2 * row_count
    tops, totals, attended = {}, {}, []
    for head in range(2):
        parts = []
        for block in range(4):
            final_row = 2 * block_rows * (block + 1)
            first_row = 2 * block_rows * block + block_rows * xl_at
            query_block = queries[head][block * block_rows : (block + 1) * block_rows]
            scores = block_scores(query_block, keys[head][:final_row], first_row, score_scale)
            row_top = jnp.max(scores, axis=-1, keepdims=True)
            exponent = jnp.exp(scores - row_top)
            row_total = jnp.sum(exponent, axis=-1, keepdims=True)
            probs_low = (exponent / row_total).astype(BF)
            parts.append(matmul(probs_low, values[head][:final_row]).astype(BF))
            tops[head, block], totals[head, block] = row_top, row_total
        attended.append(jnp.concatenate(parts, axis=0))
    attended_own = jnp.concatenate(attended, axis=-1)
    attended_own, above[0], below[0], seq_grad, down_all = tie(
        attended_own, above[0], below[0], seq_grad, down_all
    )
    down_all = down_all.reshape(16, 40, width)
    output_own = down_all[:, :16].reshape(256, width)
    sdown_own = down_all[:, 16:].reshape(UNIT_PAD, width)
    unit_columns, attended_own = tie(grouped[:, 1152:], attended_own)
    unit_columns = to_replicas(unit_columns)
    attended_sum = lax.psum_scatter(
        matmul(attended_own, output_own).astype(BF), ZC, scatter_dimension=0, tiled=True
    )

    attended_sum, unit_columns = tie(attended_sum, unit_columns)
    unit_columns = in_row_order(unit_columns)
    met[1], attended_sum = tie(met[1], attended_sum)
    above[1], below[1] = shift(met[1], "y", 1), shift(met[1], "y", -1)
    far = [shift(above[0], "y", 1), shift(below[1], "y", -1)]

    input_rows = own_tokens.astype(F32)
    middle = input_rows + attended_sum.astype(F32)
    scaled_two, inverse_two = normalize(middle)
    normed_two = (scaled_two * second_norm_gain).astype(BF)
    seq_normed_two = lax.all_gather(normed_two, ZC, axis=0, tiled=True)

    logits = matmul(normed_two, router_full)
    route_ids = routes[0]
    route_hot = (
        route_ids[:, :, None] == jnp.arange(expert_count, dtype=jnp.int32)[None, None, :]
    ).astype(F32)
    chosen = jnp.sum(route_hot * logits[:, None, :], axis=-1)
    gate_values = jax.nn.softmax(chosen, axis=-1)
    grad_result = cotangent[0]
    grad_float = grad_result.astype(F32)
    route_total = row_count * TOP
    flat_hot = route_hot.reshape(route_total, expert_count).astype(BF)
    earlier = (
        jnp.arange(route_total, dtype=jnp.int32)[:, None]
        > jnp.arange(route_total, dtype=jnp.int32)[None, :]
    ).astype(BF)
    before = matmul(earlier, flat_hot)
    slot_place = jnp.sum(before * flat_hot.astype(F32), axis=-1).astype(jnp.int32)
    slot_ids = (route_ids.reshape(route_total) * SLOTS + slot_place).reshape(row_count, TOP)
    slot_match = (
        jnp.arange(expert_count * SLOTS, dtype=jnp.int32)[:, None, None] == slot_ids[None, :, :]
    )
    dispatch = jnp.any(slot_match, axis=-1).astype(BF)
    slot_gates = jnp.sum(jnp.where(slot_match, gate_values[None], 0.0), axis=(1, 2))
    sent_rows = matmul(dispatch, normed_two).astype(BF)
    sent_grads = (matmul(dispatch, grad_result) * slot_gates[:, None]).astype(BF)
    sent = jnp.concatenate([sent_rows, sent_grads], axis=-1)
    own_in = lax.all_to_all(sent, ZXX, split_axis=0, concat_axis=0, tiled=True)
    other_in = shift(own_in, "c", 1)
    own_in, other_in, seq_normed_two, above[1], below[1] = tie(
        own_in, other_in, seq_normed_two, above[1], below[1]
    )

    back_part, out_part, shared_kept = shared_rows(
        seq_normed_two, seq_grad, unit_columns, sdown_own
    )
    far[0], far[1], back_part, out_part = tie(far[0], far[1], back_part, out_part)
    shared_back = lax.psum_scatter(back_part, ZC, scatter_dimension=0, tiled=True).astype(F32)
    shared_out = lax.psum_scatter(out_part, ZC, scatter_dimension=0, tiled=True).astype(F32)

    pieces = [met[0], met[1], above[0], above[1], far[0], far[1], below[0], below[1]]
    order = jnp.stack(
        [((y_at + step) % 4) * 2 + (c_at ^ turn) for step in range(4) for turn in range(2)]
    ).astype(jnp.int32)
    own_back, other_back, own_kept, other_kept = expert_rows(order, pieces, own_in, other_in)
    back = total(own_back, shift(other_back, "c", 1))
    returned = lax.all_to_all(back, ZXX, split_axis=0, concat_axis=0, tiled=True)
    wide_grads = expert_grads(order, own_in, other_in, own_kept, other_kept)
    returned, wide_grads = tie(returned, wide_grads)
    picks = (
        jnp.arange(expert_count * SLOTS, dtype=jnp.int32)[None, :] == slot_ids.T.reshape(-1)[:, None]
    ).astype(BF)
    picked = matmul(picks, returned).reshape(TOP, row_count, 2 * width)
    picked_out = picked[:, :, :width]
    grad_normed_routed = picked[0, :, width:] + picked[1, :, width:]
    routed = gate_values[:, :1] * picked_out[0] + gate_values[:, 1:] * picked_out[1]
    result = middle + shared_out + routed
    grad_gates = jnp.stack(
        [jnp.sum(grad_float * picked_out[k], axis=-1) for k in range(TOP)], axis=-1
    )
    centered_gates = grad_gates - jnp.sum(gate_values * grad_gates, axis=-1, keepdims=True)
    grad_chosen = gate_values * centered_gates
    grad_logits = jnp.sum(route_hot * grad_chosen[:, :, None], axis=1).astype(BF)
    grad_router = contract_rows(normed_two, grad_logits)
    grad_normed_router = contract_cols(grad_logits, router_full)
    grad_normed_two = shared_back + grad_normed_routed + grad_normed_router
    grad_from_norm, grad_gain_second = norm_back(
        grad_normed_two, second_norm_gain, scaled_two, inverse_two
    )
    grad_middle = grad_float + grad_from_norm
    blocks = wide_grads.reshape(4, 2, 256, 3 * HALF)
    from_below = shift(blocks[2, 0], "y", -1)
    from_above = shift(blocks[2, 1], "y", 1)
    grad_middle, from_below, from_above = tie(grad_middle, from_below, from_above)
    upward = [total(blocks[1, 0], from_below), blocks[1, 1]]
    downward = [blocks[3, 0], total(blocks[3, 1], from_above)]
    upward = [shift(block, "y", -1) for block in upward]
    downward = [shift(block, "y", 1) for block in downward]
    seq_grad_middle = lax.all_gather(grad_middle.astype(BF), ZC, axis=0, tiled=True)

    grad_units = contract_rows(seq_normed_two, shared_kept[:, : 2 * UNIT_PAD]).astype(BF)
    grad_sdown = contract_rows(shared_kept[:, 2 * UNIT_PAD :], seq_grad).astype(BF)
    seq_grad_middle, grad_units, grad_sdown = tie(seq_grad_middle, grad_units, grad_sdown)
    units_in = exchange_all(grad_units)

    grad_output = contract_rows(attended_own, seq_grad_middle)
    grad_heads = contract_cols(seq_grad_middle, output_own).astype(BF)
    grad_queries_nope, grad_queries_rope, grad_expanded_parts, rope_parts = [], [], [], []
    for head in range(2):
        grad_query_parts = []
        grad_key = jnp.zeros((length, NOPE + ROPE), F32)
        grad_value = jnp.zeros((length, VDIM), F32)
        for block in range(4):
            final_row = 2 * block_rows * (block + 1)
            first_row = 2 * block_rows * block + block_rows * xl_at
            rows = slice(block * block_rows, (block + 1) * block_rows)
            query_block = queries[head][rows]
            scores = block_scores(query_block, keys[head][:final_row], first_row, score_scale)
            probs = jnp.exp(scores - tops[head, block]) / totals[head, block]
            grad_block = grad_heads[rows, head * VDIM : (head + 1) * VDIM]
            grad_probs = contract_cols(grad_block, values[head][:final_row])
            centered = jnp.sum(probs * grad_probs, axis=-1, keepdims=True)
            grad_scores = (probs * (grad_probs - centered)).astype(BF)
            grad_query_parts.append(matmul(grad_scores, keys[head][:final_row]) * score_scale)
            grad_key = grad_key.at[:final_row].add(
                contract_rows(grad_scores, query_block) * score_scale
            )
            grad_value = grad_value.at[:final_row].add(
                contract_rows(probs.astype(BF), grad_block)
            )
        grad_query = jnp.concatenate(grad_query_parts, axis=0)
        grad_queries_nope.append(grad_query[:, :NOPE].astype(BF))
        grad_queries_rope.append(
            rotate_back(grad_query[:, NOPE:], cosine_half, sine_half).astype(BF)
        )
        grad_expanded_parts += [grad_key[:, :NOPE].astype(BF), grad_value.astype(BF)]
        rope_parts.append(rotate_back(grad_key[:, NOPE:], cosine_table, sine_table).astype(BF))
    grad_expanded = jnp.concatenate(grad_expanded_parts, axis=-1)
    grad_expanded, upward[0], upward[1], downward[0], downward[1], units_in = tie(
        grad_expanded, upward[0], upward[1], downward[0], downward[1], units_in
    )
    summed = [total(blocks[0, turn], upward[turn], downward[turn]) for turn in range(2)]
    parted = [part(summed[turn], turn) for turn in range(2)]
    grad_query_flat = jnp.concatenate(grad_queries_nope + grad_queries_rope, axis=-1)
    rope_part = rope_parts[0].astype(F32) + rope_parts[1].astype(F32)
    latent_part = jnp.concatenate(
        [contract_cols(grad_expanded, expand_own).astype(BF), rope_part.astype(BF)], axis=-1
    )
    latent_part = latent_part.reshape(8, 2, row_count, -1)
    latent_kept = lax.dynamic_index_in_dim(latent_part, c_at, axis=1, keepdims=False)
    latent_given = lax.dynamic_index_in_dim(latent_part, 1 - c_at, axis=1, keepdims=False)
    latent_pair = total(latent_kept, shift(latent_given, "c", 1))
    latent_in = lax.all_to_all(latent_pair, ("z", "xl"), split_axis=0, concat_axis=0, tiled=True)
    grad_latent_sum = jnp.sum(latent_in.astype(F32), axis=0)
    grad_normed_part = lax.psum_scatter(
        contract_cols(grad_query_flat, query_own).astype(BF), ZC, scatter_dimension=0, tiled=True
    ).astype(F32)
    grad_expand = contract_rows(latent_normed, grad_expanded)
    grad_query_w = contract_rows(normed_half, grad_query_flat)

    down_grads = jnp.concatenate(
        [grad_output.astype(BF).reshape(16, 16, width), grad_sdown.reshape(16, 24, width)], axis=1
    ).reshape(640, width)
    down_in = lax.all_to_all(down_grads, XYX, split_axis=0, concat_axis=0, tiled=True)
    grad_latent_sum, down_in, parted[0], parted[1] = tie(
        grad_latent_sum, down_in, parted[0], parted[1]
    )

    scaled_one, inverse_one = normalize(input_rows)
    normed_one = (scaled_one * first_norm_gain).astype(BF)
    seq_at = (z_at * 2 + xl_at) * 2 + c_at
    latent_own = lax.dynamic_slice_in_dim(latent_all, seq_at * row_count, row_count, axis=0)
    scaled_latent, inverse_latent = normalize(latent_own[:, :KV_RANK])
    grad_latent, grad_gain_latent = norm_back(
        grad_latent_sum[:, :KV_RANK], latent_norm_gain, scaled_latent, inverse_latent
    )
    grad_latent_all = jnp.concatenate([grad_latent, grad_latent_sum[:, KV_RANK:]], axis=-1).astype(BF)
    grad_latent_w = contract_rows(normed_one, grad_latent_all)
    grad_normed_one = grad_normed_part + contract_cols(grad_latent_all, latent_full)
    grad_input_norm, grad_gain_first = norm_back(
        grad_normed_one, first_norm_gain, scaled_one, inverse_one
    )
    grad_inputs = grad_middle + grad_input_norm

    first_half = jnp.where(xh_at == 0, parted[0], parted[1])
    second_half = jnp.where(xh_at == 0, parted[1], parted[0])
    repeated = 2 * HALF - expert_gate.shape[2]
    grad_egate, grad_eup, grad_edown = [
        jnp.concatenate(
            [
                first_half[:, k * HALF : (k + 1) * HALF],
                second_half[:, k * HALF + repeated : (k + 1) * HALF],
            ],
            axis=-1,
        ).astype(F32)
        for k in range(3)
    ]
    grad_edown = grad_edown.T
    down_final = jnp.sum(down_in.reshape(16, 40, width).astype(F32), axis=0)
    grad_output_w = down_final[:16]
    grad_sdown_w = down_final[16 : 16 + shared_down.shape[0]]
    units_sum = jnp.sum(
        units_in.reshape(4, 2, 2, 8, 16, 2 * UNIT_PAD).astype(F32), axis=(1, 3)
    ).reshape(8, 16, 2 * UNIT_PAD)
    grad_sgate = unit_columns_back(units_sum[..., :UNIT_PAD], units)
    grad_sup = unit_columns_back(units_sum[..., UNIT_PAD:], units)

    gain_latent_rows = jnp.pad(grad_gain_latent.reshape(128, 4), ((0, 0), (0, 12))).reshape(-1, 1)
    final_out = jnp.concatenate(
        [
            grad_query_w.astype(BF),
            grad_expand.astype(BF).reshape(length, 128),
            grad_latent_w.astype(BF),
            grad_router.astype(BF),
            grad_gain_first.astype(BF)[:, None],
            grad_gain_second.astype(BF)[:, None],
            gain_latent_rows.astype(BF),
            jnp.zeros((length, 45), BF),
        ],
        axis=-1,
    )
    final_in = exchange_all(final_out).reshape(4, 2, 2, 8, 16, 1152)
    group_sum = jnp.sum(final_in[..., :512].astype(F32), axis=(1, 3)).reshape(8, 16, 512)
    common_sum = jnp.sum(final_in[..., 512:].astype(F32), axis=(0, 1, 2, 3))
    grad_query_weight = ungroup_columns(
        jnp.concatenate(
            [
                group_sum[..., :256].reshape(8, 16, 2, NOPE),
                group_sum[..., 256:384].reshape(8, 16, 2, ROPE),
            ],
            axis=-1,
        )
    )
    grad_expand_weight = ungroup_columns(group_sum[..., 384:].reshape(8, 4, 2, 256))
    return (
        result.astype(BF)[None],
        grad_inputs.astype(BF)[None],
        common_sum[:, 592],
        grad_query_weight,
        common_sum[:, :576],
        common_sum[:4, 594],
        grad_expand_weight,
        grad_output_w,
        common_sum[:, 593],
        common_sum[:, 576:592],
        grad_sgate,
        grad_sup,
        grad_sdown_w,
        grad_egate[None],
        grad_eup[None],
        grad_edown[None],
    )


def solution(mesh):
    fine = Mesh(mesh.devices.reshape(4, 2, 2, 4, 2), ALL)
    return jax.shard_map(
        on_device,
        mesh=fine,
        in_specs=(
            P(FSDP, SEQ, None),
            P(FSDP, None),
            P(FSDP, SEQ, None),
            P(ALL),
            P(ALL, None),
            P(ALL, None),
            P(ALL),
            P(ALL, None),
            P(ALL, None),
            P(ALL),
            P(ALL, None),
            P(ALL, None),
            P(ALL, None),
            P(ALL, None),
            P(SEQ, FSDP, None),
            P(SEQ, FSDP, None),
            P(SEQ, None, FSDP),
            P(FSDP, SEQ, None),
        ),
        out_specs=(
            P(FSDP, SEQ, None),
            P(FSDP, SEQ, None),
            P(ALL),
            P(ALL, None),
            P(ALL, None),
            P(ALL),
            P(ALL, None),
            P(ALL, None),
            P(ALL),
            P(ALL, None),
            P(ALL, None),
            P(ALL, None),
            P(ALL, None),
            P(SEQ, FSDP, None),
            P(SEQ, FSDP, None),
            P(SEQ, None, FSDP),
        ),
        check_vma=False,
    )
```

```python
import math

import jax
import jax.numpy as jnp
from jax import lax
from jax.experimental import pallas as pl
from jax.experimental.pallas import tpu as pltpu
from jax.sharding import Mesh
from jax.sharding import PartitionSpec as P

NOPE = 128
ROPE = 64
VDIM = 128
KV_RANK = 512
TOP = 2
UNIT_PAD = 384
SLOTS = 24
HALF = 768
PACKED = 640
EPSILON = 1e-06
VMEM_BYTES = 60 * 2**20
LESS_VMEM = 40 * 2**20
SMALL = pl.CostEstimate(flops=1024, bytes_accessed=2**18, transcendentals=0)

SEQ = ("z", "xl", "c")
FSDP = ("y", "xh")
ZC = ("z", "c")
XYX = ("xl", "y", "xh")
ZXX = ("z", "xl", "xh")
ALL = ("z", "xl", "c", "y", "xh")
BF = jnp.bfloat16
F32 = jnp.float32


def matmul(left_side, right_side):
    return jnp.dot(left_side, right_side, preferred_element_type=F32)


def contract_rows(left_side, right_side):
    return lax.dot_general(
        left_side, right_side, (((0,), (0,)), ((), ())), preferred_element_type=F32
    )


def contract_cols(left_side, right_side):
    return lax.dot_general(
        left_side, right_side, (((1,), (1,)), ((), ())), preferred_element_type=F32
    )


def normalize(values):
    inverse = lax.rsqrt(jnp.mean(values * values, axis=-1, keepdims=True) + EPSILON)
    return (values * inverse, inverse)


def norm_back(grad_normed, gain_vector, scaled, inverse):
    grad_scaled = grad_normed * gain_vector
    grad_input = inverse * (
        grad_scaled - scaled * jnp.mean(grad_scaled * scaled, axis=-1, keepdims=True)
    )
    return (grad_input, grad_normed * scaled)


def rotary_tables(position_list):
    half_rope = ROPE // 2
    frequency = jnp.exp(-(2.0 * jnp.arange(half_rope, dtype=F32) / ROPE) * math.log(10000.0))
    angles = position_list.astype(F32)[:, None] * frequency[None, :]
    return (jnp.cos(angles), jnp.sin(angles))


def wide_tables(cosine_table, sine_table):
    return (
        jnp.concatenate([cosine_table, cosine_table], axis=-1),
        jnp.concatenate([-sine_table, sine_table], axis=-1),
    )


def places(kind, rows, head, swapped):
    row = lax.broadcasted_iota(jnp.int32, (rows, ROPE), 0)
    col = lax.broadcasted_iota(jnp.int32, (rows, ROPE), 1)
    if swapped:
        col = (col + ROPE // 2) % ROPE
    return (row == col + head * ROPE).astype(kind)


def shift(values, axis_name, step):
    count = lax.axis_size(axis_name)
    return lax.ppermute(values, axis_name, [((i + step) % count, i) for i in range(count)])


def front_body(
    rows_ref, gain_ref, weight_ref, latent_gain_ref, packed_ref, normed_ref, latent_ref
):
    scaled, _ = normalize(rows_ref[...].astype(F32))
    normed = (scaled * gain_ref[...]).astype(BF)
    latent = matmul(normed, weight_ref[...])
    normed_ref[...] = normed
    latent_ref[...] = latent
    scaled_latent, _ = normalize(latent[:, :KV_RANK])
    packed_ref[:, :KV_RANK] = (scaled_latent * latent_gain_ref[...]).astype(BF)
    packed_ref[:, KV_RANK : KV_RANK + ROPE] = latent[:, KV_RANK:].astype(BF)
    packed_ref[:, KV_RANK + ROPE :] = jnp.zeros((latent.shape[0], PACKED - KV_RANK - ROPE), BF)


def front(rows, gain, weight, latent_gain):
    count, width = rows.shape
    columns, tile = weight.shape[1], 256
    outs = (
        jax.ShapeDtypeStruct((count, PACKED), BF),
        jax.ShapeDtypeStruct((count, width), BF),
        jax.ShapeDtypeStruct((count, columns), F32),
    )
    return pl.pallas_call(
        front_body,
        grid=(count // tile,),
        out_shape=outs,
        in_specs=[
            row_tiles(rows.shape, tile),
            whole_block((1, width)),
            whole_block(weight.shape),
            whole_block((1, KV_RANK)),
        ],
        out_specs=tuple(row_tiles(out.shape, tile) for out in outs),
        compiler_params=pltpu.CompilerParams(vmem_limit_bytes=LESS_VMEM),
        cost_estimate=SMALL,
    )(rows, gain[None], weight, latent_gain[None])


def key_values(packed_ref, expand_ref, cosine, sine, keys_ref, values_ref):
    expanded = matmul(packed_ref[:, :KV_RANK], expand_ref[...]).astype(BF)
    rope = packed_ref[:, KV_RANK : KV_RANK + ROPE]
    turned = (
        rope.astype(F32) * cosine + matmul(rope, places(BF, ROPE, 0, True)) * sine
    ).astype(BF)
    for head in range(2):
        at = head * (NOPE + VDIM)
        keys_ref[head, :, :NOPE] = expanded[:, at : at + NOPE]
        keys_ref[head, :, NOPE:] = turned
        values_ref[head] = expanded[:, at + NOPE : at + NOPE + VDIM]


def own_heads_body(
    normed_ref, query_weight_ref, packed_ref, expand_ref, cosine_ref, sine_ref,
    queries_ref, keys_ref, values_ref,
):
    cosine, sine = cosine_ref[...], sine_ref[...]
    flat = matmul(normed_ref[...], query_weight_ref[...]).astype(BF)
    for head in range(2):
        queries_ref[head, :, :NOPE] = flat[:, head * NOPE : (head + 1) * NOPE]
        ropes = flat[:, 2 * NOPE :]
        queries_ref[head, :, NOPE:] = (
            matmul(ropes, places(BF, 2 * ROPE, head, False)) * cosine
            + matmul(ropes, places(BF, 2 * ROPE, head, True)) * sine
        ).astype(BF)
    key_values(packed_ref, expand_ref, cosine, sine, keys_ref, values_ref)


def other_heads_body(packed_ref, expand_ref, cosine_ref, sine_ref, keys_ref, values_ref):
    key_values(packed_ref, expand_ref, cosine_ref[...], sine_ref[...], keys_ref, values_ref)


def row_tiles(shape, tile):
    if len(shape) == 2:
        return pl.BlockSpec((tile, shape[1]), lambda i: (i, 0))
    return pl.BlockSpec((shape[0], tile, shape[2]), lambda i: (0, i, 0))


def whole_block(shape):
    return pl.BlockSpec(shape, lambda i: (0,) * len(shape))


def heads_of(packed, expand_own, tables, normed=None, query_own=None):
    rows, tile = packed.shape[0], 256
    keys = jax.ShapeDtypeStruct((2, rows, NOPE + ROPE), BF)
    values = jax.ShapeDtypeStruct((2, rows, VDIM), BF)
    outs = (keys, values) if normed is None else (keys, keys, values)
    args, specs = [packed, expand_own, *tables], []
    specs = [
        row_tiles(packed.shape, tile),
        whole_block(expand_own.shape),
        row_tiles(tables[0].shape, tile),
        row_tiles(tables[1].shape, tile),
    ]
    if normed is not None:
        args = [normed, query_own] + args
        specs = [row_tiles(normed.shape, tile), whole_block(query_own.shape)] + specs
    return pl.pallas_call(
        other_heads_body if normed is None else own_heads_body,
        grid=(rows // tile,),
        out_shape=outs,
        in_specs=specs,
        out_specs=tuple(row_tiles(out.shape, tile) for out in outs),
        compiler_params=pltpu.CompilerParams(vmem_limit_bytes=LESS_VMEM),
        cost_estimate=SMALL,
    )(*args)


def back_rows_body(
    at_ref, nope_ref, rope_ref, pair_ref, pair_other_ref, key_rope_ref, key_rope_other_ref,
    cosine_ref, sine_ref, cosine_other_ref, sine_other_ref, query_weight_ref, expand_ref,
    flat_ref, part_ref, kept_ref, given_ref, terms_ref,
):
    swap = places(F32, ROPE, 0, True)

    def turned_back(values, cosine, sine):
        swapped = jnp.dot(
            values, swap, precision=lax.Precision.HIGHEST, preferred_element_type=F32
        )
        return (values * cosine - swapped * sine).astype(BF)

    cosine, sine = cosine_ref[...], sine_ref[...]
    flat_ref[:, : 2 * NOPE] = nope_ref[...]
    for head in range(2):
        at = 2 * NOPE + head * ROPE
        flat_ref[:, at : at + ROPE] = turned_back(rope_ref[head], cosine, sine)
    part_ref[...] = contract_cols(flat_ref[...], query_weight_ref[...]).astype(BF)
    rows = nope_ref.shape[0] // 2
    core = at_ref[1]
    for i, (pairs, ropes, cosine, sine) in enumerate(
        (
            (pair_ref, key_rope_ref, cosine, sine),
            (pair_other_ref, key_rope_other_ref, cosine_other_ref[...], sine_other_ref[...]),
        )
    ):
        terms = contract_cols(pairs[...], expand_ref[...]).astype(BF)
        rope = (
            turned_back(ropes[0], cosine, sine).astype(F32)
            + turned_back(ropes[1], cosine, sine).astype(F32)
        ).astype(BF)
        for c in range(2):
            terms_ref[c, :, :KV_RANK] = terms[c * rows : (c + 1) * rows]
            terms_ref[c, :, KV_RANK : KV_RANK + ROPE] = rope[c * rows : (c + 1) * rows]
            terms_ref[c, :, KV_RANK + ROPE :] = jnp.zeros((rows, PACKED - KV_RANK - ROPE), BF)
        place = pl.ds(at_ref[0] if i == 0 else 1 - at_ref[0], 1)
        kept_ref[place] = terms_ref[pl.ds(core, 1)]
        given_ref[place] = terms_ref[pl.ds(1 - core, 1)]


def back_rows(at, grads, tables, query_own, expand_own):
    nope, rope, pair, pair_other, key_rope, key_rope_other = grads
    rows, tile = nope.shape[0], 256
    args = [nope, rope, pair, pair_other, key_rope, key_rope_other, *tables]
    terms = jax.ShapeDtypeStruct((8, tile // 2, PACKED), BF)
    terms_spec = pl.BlockSpec((2, tile // 2, PACKED), lambda i: (i, 0, 0))
    outs = (
        jax.ShapeDtypeStruct((rows, query_own.shape[1]), BF),
        jax.ShapeDtypeStruct((rows, query_own.shape[0]), BF),
    )
    return pl.pallas_call(
        back_rows_body,
        grid=(rows // tile,),
        out_shape=outs + (terms, terms),
        in_specs=[pl.BlockSpec(memory_space=pltpu.SMEM)]
        + [row_tiles(arg.shape, tile) for arg in args]
        + [whole_block(query_own.shape), whole_block(expand_own.shape)],
        out_specs=tuple(row_tiles(out.shape, tile) for out in outs) + (terms_spec, terms_spec),
        scratch_shapes=[pltpu.VMEM((2, tile // 2, PACKED), BF)],
        compiler_params=pltpu.CompilerParams(vmem_limit_bytes=VMEM_BYTES),
        cost_estimate=SMALL,
    )(at, *args, query_own, expand_own)


def scores_of(query, keys, own, other_first, t, block):
    scores = contract_cols(query, keys) * (NOPE + ROPE) ** (-0.5)
    count = scores.shape[0]
    row = lax.broadcasted_iota(jnp.int32, scores.shape, 0)
    col = lax.broadcasted_iota(jnp.int32, scores.shape, 1)
    if own:
        reach = jnp.where(t < block, count, 0)
    else:
        reach = jnp.where((t < block) | other_first, count, -count)
    return jnp.where(col <= row + reach, scores, -1e30)


def attend_body(
    at_ref, query_ref, key_ref, key_other_ref, value_ref, value_other_ref, out_ref, lse_ref, scores_ref
):
    count = query_ref.shape[1]
    block = pl.program_id(1)
    query = query_ref[0]
    other_first = at_ref[0] == 1
    sets = ((key_ref, value_ref, True, 0), (key_other_ref, value_other_ref, False, count))

    def score(t, top):
        at = pl.ds(pl.multiple_of(t * count, count), count)
        for keys, _, own, place in sets:
            scores = scores_of(query, keys[0, at, :], own, other_first, t, block)
            scores_ref[:, pl.ds(pl.multiple_of(2 * t * count + place, count), count)] = scores
            top = jnp.maximum(top, jnp.max(scores, axis=-1, keepdims=True))
        return top

    top = lax.fori_loop(0, block + 1, score, jnp.full((count, 1), -1e30, F32))

    def weigh(t, carry):
        row_total, summed = carry
        at = pl.ds(pl.multiple_of(t * count, count), count)
        for _, values, _, place in sets:
            scores = scores_ref[:, pl.ds(pl.multiple_of(2 * t * count + place, count), count)]
            exponent = jnp.exp(scores - top)
            row_total = row_total + jnp.sum(exponent, axis=-1, keepdims=True)
            summed = summed + matmul(exponent.astype(BF), values[0, at, :])
        return row_total, summed

    row_total, summed = lax.fori_loop(
        0, block + 1, weigh, (jnp.zeros((count, 1), F32), jnp.zeros((count, VDIM), F32))
    )
    out_ref[...] = (summed / row_total).astype(BF)
    lse_ref[0] = top + jnp.log(row_total)


def attend(xl_at, queries, keys, keys_other, values, values_other):
    heads, rows, depth = queries.shape
    count = rows // 4
    key_spec = pl.BlockSpec((1, rows, depth), lambda h, j: (h, 0, 0))
    value_spec = pl.BlockSpec((1, rows, VDIM), lambda h, j: (h, 0, 0))
    return pl.pallas_call(
        attend_body,
        grid=(heads, 4),
        out_shape=(
            jax.ShapeDtypeStruct((rows, heads * VDIM), BF),
            jax.ShapeDtypeStruct((heads, rows, 1), F32),
        ),
        in_specs=[
            pl.BlockSpec(memory_space=pltpu.SMEM),
            pl.BlockSpec((1, count, depth), lambda h, j: (h, j, 0)),
            key_spec,
            key_spec,
            value_spec,
            value_spec,
        ],
        out_specs=(
            pl.BlockSpec((count, VDIM), lambda h, j: (j, h)),
            pl.BlockSpec((1, count, 1), lambda h, j: (h, j, 0)),
        ),
        scratch_shapes=[pltpu.VMEM((count, 2 * rows), F32)],
        compiler_params=pltpu.CompilerParams(vmem_limit_bytes=LESS_VMEM),
        cost_estimate=SMALL,
    )(xl_at.reshape(1), queries, keys, keys_other, values, values_other)


def attend_back_body(
    at_ref, query_ref, key_ref, key_other_ref, value_ref, value_other_ref, grad_ref, lse_ref,
    nope_ref, rope_ref, pair_ref, pair_other_ref, key_rope_ref, key_rope_other_ref,
    probs_ref, grad_probs_ref, key_sum, key_other_sum, value_sum, value_other_sum,
):
    count = query_ref.shape[1]
    block = pl.program_id(1)
    query, grad = query_ref[0], grad_ref[...]
    other_first = at_ref[0] == 1
    scale = (NOPE + ROPE) ** (-0.5)
    sets = (
        (key_ref, value_ref, key_sum, value_sum, True, 0),
        (key_other_ref, value_other_ref, key_other_sum, value_other_sum, False, count),
    )

    @pl.when(block == 0)
    def _():
        for _, _, keys_to, values_to, _, _ in sets:
            keys_to[...] = jnp.zeros_like(keys_to)
            values_to[...] = jnp.zeros_like(values_to)

    def score(t, centered):
        at = pl.ds(pl.multiple_of(t * count, count), count)
        for keys, values, _, _, own, place in sets:
            to = pl.ds(pl.multiple_of(2 * t * count + place, count), count)
            scores = scores_of(query, keys[0, at, :], own, other_first, t, block)
            probs = jnp.exp(scores - lse_ref[0])
            grad_probs = contract_cols(grad, values[0, at, :])
            probs_ref[:, to] = probs
            grad_probs_ref[:, to] = grad_probs
            centered = centered + jnp.sum(probs * grad_probs, axis=-1, keepdims=True)
        return centered

    centered = lax.fori_loop(0, block + 1, score, jnp.zeros((count, 1), F32))

    def give(t, summed):
        at = pl.ds(pl.multiple_of(t * count, count), count)
        for keys, _, keys_to, values_to, _, place in sets:
            to = pl.ds(pl.multiple_of(2 * t * count + place, count), count)
            probs = probs_ref[:, to]
            grad_scores = (probs * (grad_probs_ref[:, to] - centered)).astype(BF)
            keys_to[at, :] += contract_rows(grad_scores, query)
            values_to[at, :] += contract_rows(probs.astype(BF), grad)
            summed = summed + matmul(grad_scores, keys[0, at, :])
        return summed

    grad_query = scale * lax.fori_loop(0, block + 1, give, jnp.zeros(query.shape, F32))
    nope_ref[...] = grad_query[:, :NOPE].astype(BF)
    rope_ref[0] = grad_query[:, NOPE:]

    @pl.when(block == 3)
    def _():
        for keys_from, values_from, to, rope_to in (
            (key_sum, value_sum, pair_ref, key_rope_ref),
            (key_other_sum, value_other_sum, pair_other_ref, key_rope_other_ref),
        ):
            to[:, :NOPE] = (scale * keys_from[:, :NOPE]).astype(BF)
            to[:, NOPE:] = values_from[...].astype(BF)
            rope_to[0] = scale * keys_from[:, NOPE:]


def attend_back(xl_at, queries, keys, keys_other, values, values_other, grads, lse):
    heads, rows, depth = queries.shape
    count = rows // 4
    key_spec = pl.BlockSpec((1, rows, depth), lambda h, j: (h, 0, 0))
    value_spec = pl.BlockSpec((1, rows, VDIM), lambda h, j: (h, 0, 0))
    pair = jax.ShapeDtypeStruct((rows, heads * (NOPE + VDIM)), BF)
    rope = jax.ShapeDtypeStruct((heads, rows, ROPE), F32)
    pair_spec = pl.BlockSpec((rows, NOPE + VDIM), lambda h, j: (0, h))
    rope_spec = pl.BlockSpec((1, rows, ROPE), lambda h, j: (h, 0, 0))
    return pl.pallas_call(
        attend_back_body,
        grid=(heads, 4),
        out_shape=(
            jax.ShapeDtypeStruct((rows, heads * NOPE), BF),
            rope,
            pair,
            pair,
            rope,
            rope,
        ),
        in_specs=[
            pl.BlockSpec(memory_space=pltpu.SMEM),
            pl.BlockSpec((1, count, depth), lambda h, j: (h, j, 0)),
            key_spec,
            key_spec,
            value_spec,
            value_spec,
            pl.BlockSpec((count, VDIM), lambda h, j: (j, h)),
            pl.BlockSpec((1, count, 1), lambda h, j: (h, j, 0)),
        ],
        out_specs=(
            pl.BlockSpec((count, NOPE), lambda h, j: (j, h)),
            pl.BlockSpec((1, count, ROPE), lambda h, j: (h, j, 0)),
            pair_spec,
            pair_spec,
            rope_spec,
            rope_spec,
        ),
        scratch_shapes=[pltpu.VMEM((count, 2 * rows), F32)] * 2
        + [pltpu.VMEM((rows, depth), F32)] * 2
        + [pltpu.VMEM((rows, VDIM), F32)] * 2,
        compiler_params=pltpu.CompilerParams(vmem_limit_bytes=VMEM_BYTES),
        cost_estimate=SMALL,
    )(xl_at.reshape(1), queries, keys, keys_other, values, values_other, grads, lse)


def group_columns(weight):
    rows, width = weight.shape[0], weight.shape[1] // 16
    return weight.reshape(rows, 4, 2, 2, width).transpose(1, 3, 0, 2, 4).reshape(8, rows, 2, width)


def ungroup_columns(parts):
    rows, width = parts.shape[1], parts.shape[3]
    return parts.reshape(4, 2, rows, 2, width).transpose(2, 0, 3, 1, 4).reshape(rows, 16 * width)


def spread_groups(parts):
    rows, width = parts.shape[1:]
    blocks = jnp.broadcast_to(
        parts.reshape(4, 1, 2, 1, 1, rows, width), (4, 2, 2, 4, 2, rows, width)
    )
    return blocks.reshape(128 * rows, width)


def to_replicas(rows):
    count, width = rows.shape
    blocks = jnp.broadcast_to(rows[None], (16, count, width)).reshape(16 * count, width)
    return lax.all_to_all(blocks, XYX, split_axis=0, concat_axis=0, tiled=True)


def in_row_order(rows):
    width = rows.shape[-1]
    blocks = rows.reshape(2, 8, 4, 2, 16, width).transpose(2, 0, 3, 1, 4, 5)
    return blocks.reshape(-1, width)


def exchange_all(blocks):
    return lax.all_to_all(blocks, ALL, split_axis=0, concat_axis=0, tiled=True)


def tie(*values):
    return lax.optimization_barrier(values)


def halves(gate, up, down):
    turned = down.T
    units = gate.shape[1]
    first = [part[:, :HALF] for part in (gate, up, turned)]
    second = [part[:, units - HALF :] for part in (gate, up, turned)]
    repeated = 2 * HALF - units
    keep = lax.broadcasted_iota(jnp.int32, second[0].shape, 1) >= repeated
    second = [jnp.where(keep, second[0], 0), jnp.where(keep, second[1], 0), second[2]]
    return jnp.concatenate(first, axis=-1), jnp.concatenate(second, axis=-1)


def meet(values, turn):
    pairs = [(2 * c + xh, 2 * (xh ^ turn) + c) for c in range(2) for xh in range(2)]
    return lax.ppermute(values, ("c", "xh"), pairs)


def part(values, turn):
    pairs = [(2 * c + xh, 2 * xh + (c ^ turn)) for c in range(2) for xh in range(2)]
    return lax.ppermute(values, ("c", "xh"), pairs)


def total(*terms):
    return sum(term.astype(F32) for term in terms).astype(BF)


def expert_body(at_ref, *refs):
    pieces, (own_ref, other_ref) = refs[:8], refs[8:10]
    own_out, other_out, own_kept, other_kept = refs[10:14]
    weights, sem = refs[14:]
    copies = [
        pltpu.make_async_copy(
            pieces[i], weights.at[pl.ds(pl.multiple_of(at_ref[i] * 256, 256), 256)], sem.at[i]
        )
        for i in range(8)
    ]
    for copy in copies:
        copy.start()
    for copy in copies:
        copy.wait()
    width = own_ref.shape[1] // 2
    for given, result, kept in (
        (own_ref, own_out, own_kept),
        (other_ref, other_out, other_kept),
    ):

        @pl.loop(0, HALF // 256)
        def _(n, given=given, kept=kept):
            def columns(k):
                return pl.ds(pl.multiple_of(k * HALF + n * 256, 256), 256)

            rows, grads = given[:, :width], given[:, width:]
            pre = matmul(rows, weights[:, columns(0)])
            lin = matmul(rows, weights[:, columns(1)])
            grad = matmul(grads, weights[:, columns(2)])
            sigmoid = jax.nn.sigmoid(pre)
            silu = pre * sigmoid
            kept[:, columns(0)] = (grad * lin * sigmoid * (1.0 + pre * (1.0 - sigmoid))).astype(BF)
            kept[:, columns(1)] = (grad * silu).astype(BF)
            kept[:, columns(2)] = (silu * lin).astype(BF)

        @pl.loop(0, width // 256)
        def _(f, kept=kept, result=result):
            block = weights[pl.ds(pl.multiple_of(f * 256, 256), 256), :]
            out = contract_cols(kept[:, 2 * HALF :], block[:, 2 * HALF :])
            back = contract_cols(kept[:, : 2 * HALF], block[:, : 2 * HALF])
            result[:, pl.ds(pl.multiple_of(f * 256, 256), 256)] = out.astype(BF)
            result[:, pl.ds(pl.multiple_of(width + f * 256, 256), 256)] = back.astype(BF)


def expert_rows(order, pieces, own, other):
    rows, width = own.shape
    kept = jax.ShapeDtypeStruct((rows, 3 * HALF), BF)
    result = jax.ShapeDtypeStruct((rows, width), BF)
    whole = pl.BlockSpec(memory_space=pltpu.VMEM)
    return pl.pallas_call(
        expert_body,
        out_shape=(result, result, kept, kept),
        in_specs=[pl.BlockSpec(memory_space=pltpu.SMEM)]
        + [pl.BlockSpec(memory_space=pl.ANY)] * 8
        + [whole] * 2,
        out_specs=(whole,) * 4,
        scratch_shapes=[pltpu.VMEM((width // 2, 3 * HALF), BF), pltpu.SemaphoreType.DMA((8,))],
        compiler_params=pltpu.CompilerParams(vmem_limit_bytes=VMEM_BYTES),
        cost_estimate=SMALL,
    )(order, *pieces, own, other)


def expert_grad_body(
    at_ref, own_rows, own_grads, other_rows, other_grads, own_kept, other_kept, *outs
):
    first = contract_rows(own_rows[...], own_kept[:, : 2 * HALF]) + contract_rows(
        other_rows[...], other_kept[:, : 2 * HALF]
    )
    last = contract_rows(own_grads[...], own_kept[:, 2 * HALF :]) + contract_rows(
        other_grads[...], other_kept[:, 2 * HALF :]
    )
    for i, out in enumerate(outs):

        @pl.when(pl.program_id(0) == i)
        def _(out=out):
            out[:, : 2 * HALF] = first.astype(BF)
            out[:, 2 * HALF :] = last.astype(BF)


def expert_grads(order, own, other, own_kept, other_kept):
    rows, width = own.shape
    blocks, count = width // 512, order.shape[0]
    row_spec = pl.BlockSpec((rows, 256), lambda i, at: (0, at[i]))
    grad_spec = pl.BlockSpec((rows, 256), lambda i, at: (0, blocks + at[i]))
    kept_spec = pl.BlockSpec((rows, 3 * HALF), lambda i, at: (0, 0))
    return pl.pallas_call(
        expert_grad_body,
        out_shape=(jax.ShapeDtypeStruct((256, 3 * HALF), BF),) * count,
        grid_spec=pltpu.PrefetchScalarGridSpec(
            num_scalar_prefetch=1,
            grid=(count,),
            in_specs=[row_spec, grad_spec, row_spec, grad_spec, kept_spec, kept_spec],
            out_specs=(pl.BlockSpec((256, 3 * HALF), lambda i, at: (0, 0)),) * count,
        ),
        compiler_params=pltpu.CompilerParams(vmem_limit_bytes=LESS_VMEM),
        cost_estimate=SMALL,
    )(order, own, own, other, other, own_kept, other_kept)


def shared_body(rows_ref, grads_ref, gate_up_ref, down_ref, back_ref, out_ref, kept_ref):
    both = matmul(rows_ref[...], gate_up_ref[...])
    pre, lin = both[:, :UNIT_PAD], both[:, UNIT_PAD:]
    grad = contract_cols(grads_ref[...], down_ref[...])
    sigmoid = jax.nn.sigmoid(pre)
    silu = pre * sigmoid
    hidden = (silu * lin).astype(BF)
    grad_pre = (grad * lin * sigmoid * (1.0 + pre * (1.0 - sigmoid))).astype(BF)
    grad_lin = (grad * silu).astype(BF)
    kept_ref[:, :UNIT_PAD] = grad_pre
    kept_ref[:, UNIT_PAD : 2 * UNIT_PAD] = grad_lin
    kept_ref[:, 2 * UNIT_PAD :] = hidden
    back_ref[...] = contract_cols(kept_ref[:, : 2 * UNIT_PAD], gate_up_ref[...]).astype(BF)
    out_ref[...] = matmul(hidden, down_ref[...]).astype(BF)


def shared_rows(rows, grads, gate_up, down):
    count, width = rows.shape
    tile = 256
    row_spec = pl.BlockSpec((tile, width), lambda i: (i, 0))
    return pl.pallas_call(
        shared_body,
        grid=(count // tile,),
        out_shape=(
            jax.ShapeDtypeStruct((count, width), BF),
            jax.ShapeDtypeStruct((count, width), BF),
            jax.ShapeDtypeStruct((count, 3 * UNIT_PAD), BF),
        ),
        in_specs=[
            row_spec,
            row_spec,
            pl.BlockSpec(gate_up.shape, lambda i: (0, 0)),
            pl.BlockSpec(down.shape, lambda i: (0, 0)),
        ],
        out_specs=(row_spec, row_spec, pl.BlockSpec((tile, 3 * UNIT_PAD), lambda i: (i, 0))),
        compiler_params=pltpu.CompilerParams(vmem_limit_bytes=VMEM_BYTES),
        cost_estimate=SMALL,
    )(rows, grads, gate_up, down)


def last_rows_body(
    one_ref, two_ref, first_terms_ref, second_terms_ref, latent_ref, logits_ref, extra_ref, out_ref
):
    column = lax.broadcasted_iota(jnp.int32, logits_ref.shape, 1)
    latent = contract_rows(one_ref[...], latent_ref[...])
    out_ref[:, :KV_RANK] = latent[:, :KV_RANK].astype(BF)
    last = latent[:, KV_RANK:] + contract_rows(two_ref[...], logits_ref[...])
    last = last + contract_rows(first_terms_ref[...], (column == 80).astype(BF))
    last = last + contract_rows(second_terms_ref[...], (column == 81).astype(BF))
    out_ref[:, KV_RANK:] = (last + extra_ref[...]).astype(BF)


def last_rows(normed_one, normed_two, first_terms, second_terms, latent, logits, extra):
    rows, length = normed_one.shape
    tile = 256
    column_spec = pl.BlockSpec((rows, tile), lambda i: (0, i))
    out = jax.ShapeDtypeStruct((length, PACKED), BF)
    return pl.pallas_call(
        last_rows_body,
        grid=(length // tile,),
        out_shape=out,
        in_specs=[column_spec] * 4
        + [whole_block(latent.shape), whole_block(logits.shape), row_tiles(extra.shape, tile)],
        out_specs=row_tiles(out.shape, tile),
        compiler_params=pltpu.CompilerParams(vmem_limit_bytes=VMEM_BYTES),
        cost_estimate=SMALL,
    )(normed_one, normed_two, first_terms, second_terms, latent, logits, extra)


def head_sums_body(in_ref, query_ref, expand_ref):
    for z in range(4):
        for c in range(2):

            def add(f, summed, z=z, c=c):
                for xl in range(2):
                    summed = summed + in_ref[((z * 2 + xl) * 2 + c) * 8 + f].astype(F32)
                return summed

            summed = lax.fori_loop(0, 8, add, jnp.zeros(in_ref.shape[1:], F32))
            for xl in range(2):
                part = z * 4 + xl * 2 + c
                at = part * (NOPE + ROPE)
                query_ref[:, at : at + NOPE] = summed[:, xl * NOPE : (xl + 1) * NOPE]
                rope_at = 2 * NOPE + xl * ROPE
                query_ref[:, at + NOPE : at + NOPE + ROPE] = summed[:, rope_at : rope_at + ROPE]
                for half in range(2):
                    j = 2 * xl + half
                    at = part * 256 + half * 128
                    expand_ref[:, at : at + 128] = summed[4 * j : 4 * j + 4, 384:]


def head_sums(arrived):
    whole = pl.BlockSpec(memory_space=pltpu.VMEM)
    return pl.pallas_call(
        head_sums_body,
        out_shape=(
            jax.ShapeDtypeStruct((16, 16 * (NOPE + ROPE)), F32),
            jax.ShapeDtypeStruct((4, 4096), F32),
        ),
        in_specs=[whole],
        out_specs=(whole,) * 2,
        compiler_params=pltpu.CompilerParams(vmem_limit_bytes=LESS_VMEM),
        cost_estimate=SMALL,
    )(arrived)


def unit_columns_out(weight):
    runs = group_columns(weight).reshape(8, 16, 16, -1)
    return jnp.pad(runs, ((0, 0), (0, 0), (0, 0), (0, 24 - runs.shape[-1]))).reshape(8, 16, -1)


def unit_columns_back(parts, units):
    runs = parts.reshape(8, 16, 16, 24)[..., : units // 8]
    return ungroup_columns(runs.reshape(8, 16, 2, units))


def on_device(
    tokens,
    positions,
    routes,
    first_gain,
    query_weight,
    latent_weight,
    latent_gain,
    expand_weight,
    output_weight,
    second_gain,
    router_weight,
    shared_gate,
    shared_up,
    shared_down,
    expert_gate,
    expert_up,
    expert_down,
    cotangent,
):
    z_at, xl_at, c_at = lax.axis_index("z"), lax.axis_index("xl"), lax.axis_index("c")
    y_at, xh_at = lax.axis_index("y"), lax.axis_index("xh")
    own_tokens = tokens[0]
    row_count, width = own_tokens.shape
    length = 16 * row_count
    expert_count = router_weight.shape[1]
    units = shared_gate.shape[1] // 16

    half_tokens = lax.all_gather(own_tokens, ZC, axis=0, tiled=True)

    cosine_table, sine_table = rotary_tables(positions[0])

    def half_rows(table, at):
        return lax.dynamic_index_in_dim(
            table.reshape(4, 2, 2 * row_count, -1), at, axis=1, keepdims=False
        ).reshape(length // 2, -1)

    wide = wide_tables(cosine_table, sine_table)
    tables = [half_rows(table, at) for at in (xl_at, 1 - xl_at) for table in wide]
    route_ids = routes[0]
    route_hot = (
        route_ids[:, :, None] == jnp.arange(expert_count, dtype=jnp.int32)[None, None, :]
    ).astype(F32)
    grad_result = cotangent[0]
    grad_float = grad_result.astype(F32)
    route_total = row_count * TOP
    flat_hot = route_hot.reshape(route_total, expert_count).astype(BF)
    earlier = (
        jnp.arange(route_total, dtype=jnp.int32)[:, None]
        > jnp.arange(route_total, dtype=jnp.int32)[None, :]
    ).astype(BF)
    before = matmul(earlier, flat_hot)
    slot_place = jnp.sum(before * flat_hot.astype(F32), axis=-1).astype(jnp.int32)
    slot_ids = (route_ids.reshape(route_total) * SLOTS + slot_place).reshape(row_count, TOP)
    slot_match = (
        jnp.arange(expert_count * SLOTS, dtype=jnp.int32)[:, None, None] == slot_ids[None, :, :]
    )
    dispatch = jnp.any(slot_match, axis=-1).astype(BF)
    picks = (
        jnp.arange(expert_count * SLOTS, dtype=jnp.int32)[None, :]
        == slot_ids.T.reshape(-1)[:, None]
    ).astype(BF)
    dispatch_grads = matmul(dispatch, grad_result)
    first_half, second_half = halves(expert_gate[0], expert_up[0], expert_down[0])
    met = [jnp.where((xh_at ^ turn) == 0, first_half, second_half) for turn in range(2)]

    query_group = group_columns(query_weight)
    expand_group = group_columns(expand_weight).reshape(8, 16, 128)
    head_group = jnp.concatenate(
        [
            query_group[..., :NOPE].reshape(8, 16, 2 * NOPE),
            query_group[..., NOPE:].reshape(8, 16, 2 * ROPE),
            expand_group,
        ],
        axis=-1,
    )
    common = jnp.concatenate(
        [
            latent_weight,
            router_weight,
            first_gain[:, None],
            second_gain[:, None],
            jnp.pad(latent_gain, (0, 12))[:, None],
            jnp.zeros((16, 45), BF),
        ],
        axis=-1,
    )
    unit_group = jnp.concatenate(
        [unit_columns_out(weight) for weight in (shared_gate, shared_up)], axis=-1
    ).reshape(128, 768)
    common_in = exchange_all(jnp.broadcast_to(common[None], (128, 16, 640)).reshape(2048, 640))
    met[0] = meet(met[0], 0)
    head_group = spread_groups(head_group)
    unit_group, common_in = tie(unit_group, common_in)
    unit_group = lax.all_to_all(unit_group, ZC, split_axis=0, concat_axis=0, tiled=True)

    half_tokens, common_in, met, head_group = tie(half_tokens, common_in, met, head_group)
    above, below = [None, None], [None, None]
    above[0], below[0] = shift(met[0], "y", 1), shift(met[0], "y", -1)
    head_in = exchange_all(head_group)
    gains = common_in[:, 512:640].T.astype(F32)
    first_norm_gain, second_norm_gain = gains[80], gains[81]
    latent_norm_gain = gains[82].reshape(128, 16)[:, :4].reshape(KV_RANK)
    latent_full = common_in[:, :576]
    router_full = common_in[:, 576:592]
    latent_mine, normed_half, latent_half = front(
        half_tokens, first_norm_gain, latent_full, latent_norm_gain
    )
    latent_other = shift(latent_mine, "xl", 1)

    down_count = shared_down.shape[0]
    down_rows = jnp.concatenate(
        [output_weight, jnp.pad(shared_down, ((0, 24 - down_count), (0, 0)))], axis=0
    )
    latent_other, latent_mine, normed_half, head_in, met, down_rows, grad_result, tables, unit_group, above[0], below[0] = tie(
        latent_other, latent_mine, normed_half, head_in, met, down_rows, grad_result, tables, unit_group, above[0], below[0]
    )
    down_all = to_replicas(down_rows).reshape(16, 40, width)
    seq_grad = lax.all_gather(grad_result, ZC, axis=0, tiled=True)
    met[1] = meet(met[1], 1)
    query_own = head_in[:, :384]
    expand_own = head_in[:, 384:].reshape(KV_RANK, 512)
    queries, keys, values = heads_of(latent_mine, expand_own, tables[:2], normed_half, query_own)

    keys_other, values_other = heads_of(latent_other, expand_own, tables[2:])

    attended_own, row_lse = attend(xl_at, queries, keys, keys_other, values, values_other)

    attended_own, row_lse, seq_grad, unit_group, down_all, met[1], dispatch, dispatch_grads, picks = tie(
        attended_own, row_lse, seq_grad, unit_group, down_all, met[1], dispatch, dispatch_grads, picks
    )
    output_own = down_all[:, :16].reshape(256, width)
    attended_part = matmul(attended_own, output_own).astype(BF)
    attended_sum = lax.psum_scatter(attended_part, ZC, scatter_dimension=0, tiled=True)
    unit_columns = to_replicas(unit_group)

    attended_sum, unit_columns, met[1], above[0], down_all = tie(
        attended_sum, unit_columns, met[1], above[0], down_all
    )
    unit_columns = in_row_order(unit_columns)
    sdown_own = down_all[:, 16:].reshape(UNIT_PAD, width)
    above[1], below[1] = shift(met[1], "y", 1), shift(met[1], "y", -1)
    input_rows = own_tokens.astype(F32)
    middle = input_rows + attended_sum.astype(F32)
    scaled_two, inverse_two = normalize(middle)
    normed_two = (scaled_two * second_norm_gain).astype(BF)
    seq_normed_two = lax.all_gather(normed_two, ZC, axis=0, tiled=True)
    logits = matmul(normed_two, router_full)
    chosen = jnp.sum(route_hot * logits[:, None, :], axis=-1)
    gate_values = jax.nn.softmax(chosen, axis=-1)
    slot_gates = jnp.sum(jnp.where(slot_match, gate_values[None], 0.0), axis=(1, 2))
    sent_rows = matmul(dispatch, normed_two).astype(BF)
    sent_grads = (dispatch_grads * slot_gates[:, None]).astype(BF)
    sent = jnp.concatenate([sent_rows, sent_grads], axis=-1)

    sent, seq_normed_two, above[0], above[1], below[1], unit_columns, sdown_own = tie(
        sent, seq_normed_two, above[0], above[1], below[1], unit_columns, sdown_own
    )
    own_in = lax.all_to_all(sent, ZXX, split_axis=0, concat_axis=0, tiled=True)
    far = [shift(above[0], "y", 1), shift(below[1], "y", -1)]

    back_part, out_part, shared_kept = shared_rows(
        seq_normed_two, seq_grad, unit_columns, sdown_own
    )
    grad_units = contract_rows(seq_normed_two, shared_kept[:, : 2 * UNIT_PAD]).astype(BF)
    grad_sdown = contract_rows(shared_kept[:, 2 * UNIT_PAD :], seq_grad).astype(BF)

    own_in, back_part, out_part, grad_units, grad_sdown, far = tie(
        own_in, back_part, out_part, grad_units, grad_sdown, far
    )
    shared_back = lax.psum_scatter(back_part, ZC, scatter_dimension=0, tiled=True)
    units_in = exchange_all(grad_units)
    other_in = shift(own_in, "c", 1)
    pieces = [met[0], met[1], above[0], above[1], far[0], far[1], below[0], below[1]]
    order = jnp.stack(
        [((y_at + step) % 4) * 2 + (c_at ^ turn) for step in range(4) for turn in range(2)]
    ).astype(jnp.int32)
    own_back, other_back, own_kept, other_kept = expert_rows(order, pieces, own_in, other_in)
    other_back, units_in = tie(other_back, units_in)
    back = total(own_back, shift(other_back, "c", 1))

    back, own_kept, other_kept = tie(back, own_kept, other_kept)
    returned = lax.all_to_all(back, ZXX, split_axis=0, concat_axis=0, tiled=True)
    blocks = [None] * 8
    blocks[4], blocks[5] = expert_grads(
        jnp.stack([order[4], order[5]]), own_in, other_in, own_kept, other_kept
    )
    from_below = shift(blocks[4], "y", -1)
    from_above = shift(blocks[5], "y", 1)
    own_kept, blocks[4] = tie(own_kept, blocks[4])
    blocks[3], blocks[6] = expert_grads(
        jnp.stack([order[3], order[6]]), own_in, other_in, own_kept, other_kept
    )
    upward_free, downward_free = shift(blocks[3], "y", -1), shift(blocks[6], "y", 1)
    own_kept, blocks[3] = tie(own_kept, blocks[3])
    blocks[2], blocks[7], blocks[0], blocks[1] = expert_grads(
        jnp.stack([order[2], order[7], order[0], order[1]]), own_in, other_in, own_kept, other_kept
    )

    returned, shared_back, from_below, from_above, blocks[0], blocks[2], blocks[7] = tie(
        returned, shared_back, from_below, from_above, blocks[0], blocks[2], blocks[7]
    )
    upward_last = total(blocks[2], from_below)
    downward_last = total(blocks[7], from_above)
    picked = matmul(picks, returned).reshape(TOP, row_count, 2 * width)
    picked_out = picked[:, :, :width]
    grad_normed_routed = picked[0, :, width:] + picked[1, :, width:]
    routed = gate_values[:, :1] * picked_out[0] + gate_values[:, 1:] * picked_out[1]
    grad_gates = jnp.stack(
        [jnp.sum(grad_float * picked_out[k], axis=-1) for k in range(TOP)], axis=-1
    )
    centered_gates = grad_gates - jnp.sum(gate_values * grad_gates, axis=-1, keepdims=True)
    grad_chosen = gate_values * centered_gates
    grad_logits = jnp.sum(route_hot * grad_chosen[:, :, None], axis=1).astype(BF)
    grad_normed_router = contract_cols(grad_logits, router_full)
    grad_normed_two = shared_back.astype(F32) + grad_normed_routed + grad_normed_router
    grad_from_norm, gain_second_terms = norm_back(
        grad_normed_two, second_norm_gain, scaled_two, inverse_two
    )
    grad_middle = grad_float + grad_from_norm

    grad_middle, upward_last, downward_last, upward_free, downward_free = tie(
        grad_middle, upward_last, downward_last, upward_free, downward_free
    )
    seq_grad_middle = lax.all_gather(grad_middle.astype(BF), ZC, axis=0, tiled=True)
    upward_last = shift(upward_last, "y", -1)
    downward_last = shift(downward_last, "y", 1)

    seq_grad_middle, upward_last, downward_last, out_part = tie(
        seq_grad_middle, upward_last, downward_last, out_part
    )
    shared_out = lax.psum_scatter(out_part, ZC, scatter_dimension=0, tiled=True)
    grad_output = contract_rows(attended_own, seq_grad_middle).astype(BF)
    down_grads = jnp.concatenate(
        [grad_output.reshape(16, 16, width), grad_sdown.reshape(16, 24, width)], axis=1
    ).reshape(640, width)
    down_in = lax.all_to_all(down_grads, XYX, split_axis=0, concat_axis=0, tiled=True)
    grad_heads = contract_cols(seq_grad_middle, output_own).astype(BF)
    attention_grads = attend_back(
        xl_at, queries, keys, keys_other, values, values_other, grad_heads, row_lse
    )

    attention_grads, shared_out = tie(attention_grads, shared_out)
    _, _, pair, pair_other, _, _ = attention_grads
    grad_query_flat, normed_part, latent_kept, latent_given = back_rows(
        jnp.stack([xl_at, c_at]), attention_grads, tables, query_own, expand_own
    )
    grad_query_flat, normed_part, latent_kept, latent_given, down_in = tie(
        grad_query_flat, normed_part, latent_kept, latent_given, down_in
    )
    latent_sums = total(latent_kept, shift(latent_given, "c", 1)).reshape(8 * row_count, -1)
    latent_sums, upward_last, downward_last = tie(latent_sums, upward_last, downward_last)
    parted = [
        part(total(blocks[0], upward_last, downward_free), 0),
        part(total(blocks[1], upward_free, downward_last), 1),
    ]
    latent_in = lax.all_to_all(latent_sums, ("z", "xl"), split_axis=0, concat_axis=0, tiled=True)
    grad_normed_part = lax.psum_scatter(normed_part, ZC, scatter_dimension=0, tiled=True)
    grad_expand = (
        contract_rows(latent_mine[:, :KV_RANK], pair)
        + contract_rows(latent_other[:, :KV_RANK], pair_other)
    ).astype(BF)
    grad_query_w = contract_rows(normed_half, grad_query_flat).astype(BF)
    grad_expand = grad_expand.reshape(128, 4, 4, 128).transpose(0, 2, 1, 3).reshape(length, 128)
    head_grads = jnp.concatenate([grad_query_w, grad_expand], axis=-1)

    latent_in, head_grads = tie(latent_in, head_grads)
    heads_in = exchange_all(head_grads)
    grad_latent_sum = jnp.sum(latent_in.reshape(8, row_count, -1).astype(F32), axis=0)
    scaled_one, inverse_one = normalize(input_rows)
    normed_one = (scaled_one * first_norm_gain).astype(BF)
    latent_own = lax.dynamic_slice_in_dim(
        latent_half, (z_at * 2 + c_at) * row_count, row_count, axis=0
    )
    scaled_latent, inverse_latent = normalize(latent_own[:, :KV_RANK])
    grad_latent, gain_latent_terms = norm_back(
        grad_latent_sum[:, :KV_RANK], latent_norm_gain, scaled_latent, inverse_latent
    )
    grad_latent_all = jnp.concatenate(
        [grad_latent, grad_latent_sum[:, KV_RANK : KV_RANK + ROPE]], axis=-1
    ).astype(BF)
    grad_normed_one = grad_normed_part.astype(F32) + contract_cols(grad_latent_all, latent_full)
    grad_input_norm, gain_first_terms = norm_back(
        grad_normed_one, first_norm_gain, scaled_one, inverse_one
    )

    gain_latent = jnp.sum(gain_latent_terms, axis=0).reshape(128, 1, 4)
    final_out = last_rows(
        normed_one,
        normed_two,
        gain_first_terms.astype(BF),
        gain_second_terms.astype(BF),
        jnp.pad(grad_latent_all, ((0, 0), (0, PACKED - KV_RANK - ROPE))),
        jnp.pad(grad_logits, ((0, 0), (64, 48))),
        jnp.pad(gain_latent, ((0, 0), (0, 15), (96, 28))).reshape(length, 128),
    )

    final_out, units_in, down_in, heads_in, parted = tie(
        final_out, units_in, down_in, heads_in, parted
    )
    final_in = exchange_all(final_out)

    grad_inputs = grad_middle + grad_input_norm
    result = middle + shared_out.astype(F32) + routed
    first_half = jnp.where(xh_at == 0, parted[0], parted[1])
    second_half = jnp.where(xh_at == 0, parted[1], parted[0])
    repeated = 2 * HALF - expert_gate.shape[2]
    expert_results = [
        jnp.concatenate(
            [
                first_half[:, k * HALF : (k + 1) * HALF],
                second_half[:, k * HALF + repeated : (k + 1) * HALF],
            ],
            axis=-1,
        ).astype(F32)
        for k in range(3)
    ]
    expert_results[2] = expert_results[2].T
    down_in = down_in.reshape(16, 40, width)
    grad_output_w = jnp.sum(down_in[:, :16].astype(F32), axis=0)
    grad_sdown_w = jnp.sum(down_in[:, 16 : 16 + down_count].astype(F32), axis=0)
    grad_query_weight, grad_expand_weight = head_sums(heads_in.reshape(128, 16, 512))
    units_sum = jnp.sum(
        units_in.reshape(4, 2, 2, 8, 16, 2 * UNIT_PAD).astype(F32), axis=(1, 3)
    ).reshape(8, 16, 2 * UNIT_PAD)
    unit_results = [
        unit_columns_back(units_sum[..., :UNIT_PAD], units),
        unit_columns_back(units_sum[..., UNIT_PAD:], units),
    ]
    beside = (
        grad_inputs, result, expert_results, grad_output_w, grad_sdown_w, unit_results,
        grad_query_weight, grad_expand_weight,
    )
    final_in, beside = tie(final_in, beside)
    (
        grad_inputs, result, expert_results, grad_output_w, grad_sdown_w, unit_results,
        grad_query_weight, grad_expand_weight,
    ) = beside
    common_sum = jnp.sum(final_in.reshape(128, 16, PACKED).astype(F32), axis=0)
    return (
        result.astype(BF)[None],
        grad_inputs.astype(BF)[None],
        common_sum[:, 592],
        grad_query_weight,
        common_sum[:, :576],
        common_sum[0, 608:612],
        grad_expand_weight,
        grad_output_w,
        common_sum[:, 593],
        common_sum[:, 576:592],
        unit_results[0],
        unit_results[1],
        grad_sdown_w,
        expert_results[0][None],
        expert_results[1][None],
        expert_results[2][None],
    )


def solution(mesh):
    fine = Mesh(mesh.devices.reshape(4, 2, 2, 4, 2), ALL)
    return jax.shard_map(
        on_device,
        mesh=fine,
        in_specs=(
            P(FSDP, SEQ, None),
            P(FSDP, None),
            P(FSDP, SEQ, None),
            P(ALL),
            P(ALL, None),
            P(ALL, None),
            P(ALL),
            P(ALL, None),
            P(ALL, None),
            P(ALL),
            P(ALL, None),
            P(ALL, None),
            P(ALL, None),
            P(ALL, None),
            P(SEQ, FSDP, None),
            P(SEQ, FSDP, None),
            P(SEQ, None, FSDP),
            P(FSDP, SEQ, None),
        ),
        out_specs=(
            P(FSDP, SEQ, None),
            P(FSDP, SEQ, None),
            P(ALL),
            P(ALL, None),
            P(ALL, None),
            P(ALL),
            P(ALL, None),
            P(ALL, None),
            P(ALL),
            P(ALL, None),
            P(ALL, None),
            P(ALL, None),
            P(ALL, None),
            P(SEQ, FSDP, None),
            P(SEQ, FSDP, None),
            P(SEQ, None, FSDP),
        ),
        check_vma=False,
    )
```

```python
import math

import jax
import jax.numpy as jnp
from jax import lax
from jax.experimental import pallas as pl
from jax.experimental.pallas import tpu as pltpu
from jax.sharding import Mesh
from jax.sharding import PartitionSpec as P

NOPE = 128
ROPE = 64
VDIM = 128
KV_RANK = 512
TOP = 2
UNIT_PAD = 384
SLOTS = 24
HALF = 768
PACKED = 640
QUERY = 384
EPSILON = 1e-06
VMEM_BYTES = 60 * 2**20
LESS_VMEM = 40 * 2**20
SMALL = pl.CostEstimate(flops=1024, bytes_accessed=2**18, transcendentals=0)

SEQ = ("z", "xl", "c")
FSDP = ("y", "xh")
ZC = ("z", "c")
XYX = ("xl", "y", "xh")
ZXX = ("z", "xl", "xh")
ALL = ("z", "xl", "c", "y", "xh")
BF = jnp.bfloat16
F32 = jnp.float32


def matmul(left_side, right_side):
    return jnp.dot(left_side, right_side, preferred_element_type=F32)


def contract_rows(left_side, right_side):
    return lax.dot_general(
        left_side, right_side, (((0,), (0,)), ((), ())), preferred_element_type=F32
    )


def contract_cols(left_side, right_side):
    return lax.dot_general(
        left_side, right_side, (((1,), (1,)), ((), ())), preferred_element_type=F32
    )


def normalize(values):
    inverse = lax.rsqrt(jnp.mean(values * values, axis=-1, keepdims=True) + EPSILON)
    return (values * inverse, inverse)


def norm_back(grad_normed, gain_vector, scaled, inverse):
    grad_scaled = grad_normed * gain_vector
    grad_input = inverse * (
        grad_scaled - scaled * jnp.mean(grad_scaled * scaled, axis=-1, keepdims=True)
    )
    return (grad_input, grad_normed * scaled)


def rotary_tables(position_list):
    half_rope = ROPE // 2
    frequency = jnp.exp(-(2.0 * jnp.arange(half_rope, dtype=F32) / ROPE) * math.log(10000.0))
    angles = position_list.astype(F32)[:, None] * frequency[None, :]
    return (jnp.cos(angles), jnp.sin(angles))


def wide_tables(cosine_table, sine_table):
    return (
        jnp.concatenate([cosine_table, cosine_table], axis=-1),
        jnp.concatenate([-sine_table, sine_table], axis=-1),
    )


def places(kind, rows, head, swapped):
    row = lax.broadcasted_iota(jnp.int32, (rows, ROPE), 0)
    col = lax.broadcasted_iota(jnp.int32, (rows, ROPE), 1)
    if swapped:
        col = (col + ROPE // 2) % ROPE
    return (row == col + head * ROPE).astype(kind)


def shift(values, axis_name, step):
    count = lax.axis_size(axis_name)
    return lax.ppermute(values, axis_name, [((i + step) % count, i) for i in range(count)])


def front_body(
    rows_ref, gain_ref, weight_ref, latent_gain_ref, packed_ref, normed_ref, latent_ref
):
    scaled, _ = normalize(rows_ref[...].astype(F32))
    normed = (scaled * gain_ref[...]).astype(BF)
    latent = matmul(normed, weight_ref[...])
    normed_ref[...] = normed
    latent_ref[...] = latent
    scaled_latent, _ = normalize(latent[:, :KV_RANK])
    packed_ref[:, :KV_RANK] = (scaled_latent * latent_gain_ref[...]).astype(BF)
    packed_ref[:, KV_RANK : KV_RANK + ROPE] = latent[:, KV_RANK:].astype(BF)
    packed_ref[:, KV_RANK + ROPE :] = jnp.zeros((latent.shape[0], PACKED - KV_RANK - ROPE), BF)


def front(rows, gain, weight, latent_gain):
    count, width = rows.shape
    columns, tile = weight.shape[1], 256
    outs = (
        jax.ShapeDtypeStruct((count, PACKED), BF),
        jax.ShapeDtypeStruct((count, width), BF),
        jax.ShapeDtypeStruct((count, columns), F32),
    )
    return pl.pallas_call(
        front_body,
        grid=(count // tile,),
        out_shape=outs,
        in_specs=[
            row_tiles(rows.shape, tile),
            whole_block((1, width)),
            whole_block(weight.shape),
            whole_block((1, KV_RANK)),
        ],
        out_specs=tuple(row_tiles(out.shape, tile) for out in outs),
        compiler_params=pltpu.CompilerParams(vmem_limit_bytes=LESS_VMEM),
        cost_estimate=SMALL,
    )(rows, gain[None], weight, latent_gain[None])


def key_values(packed_ref, expand_ref, cosine, sine, keys_ref, values_ref):
    expanded = matmul(packed_ref[:, :KV_RANK], expand_ref[...]).astype(BF)
    rope = packed_ref[:, KV_RANK : KV_RANK + ROPE]
    turned = (
        rope.astype(F32) * cosine + matmul(rope, places(BF, ROPE, 0, True)) * sine
    ).astype(BF)
    for head in range(2):
        at = head * (NOPE + VDIM)
        keys_ref[head, :, :NOPE] = expanded[:, at : at + NOPE]
        keys_ref[head, :, NOPE:] = turned
        values_ref[head] = expanded[:, at + NOPE : at + NOPE + VDIM]


def own_heads_body(
    normed_ref, query_weight_ref, packed_ref, expand_ref, cosine_ref, sine_ref,
    queries_ref, keys_ref, values_ref,
):
    cosine, sine = cosine_ref[...], sine_ref[...]
    flat = matmul(normed_ref[...], query_weight_ref[...]).astype(BF)
    for head in range(2):
        queries_ref[head, :, :NOPE] = flat[:, head * NOPE : (head + 1) * NOPE]
        ropes = flat[:, 2 * NOPE :]
        queries_ref[head, :, NOPE:] = (
            matmul(ropes, places(BF, 2 * ROPE, head, False)) * cosine
            + matmul(ropes, places(BF, 2 * ROPE, head, True)) * sine
        ).astype(BF)
    key_values(packed_ref, expand_ref, cosine, sine, keys_ref, values_ref)


def other_heads_body(packed_ref, expand_ref, cosine_ref, sine_ref, keys_ref, values_ref):
    key_values(packed_ref, expand_ref, cosine_ref[...], sine_ref[...], keys_ref, values_ref)


def row_tiles(shape, tile):
    if len(shape) == 2:
        return pl.BlockSpec((tile, shape[1]), lambda i: (i, 0))
    return pl.BlockSpec((shape[0], tile, shape[2]), lambda i: (0, i, 0))


def whole_block(shape):
    return pl.BlockSpec(shape, lambda i: (0,) * len(shape))


def heads_of(packed, expand_own, tables, normed=None, query_own=None):
    rows, tile = packed.shape[0], 256
    keys = jax.ShapeDtypeStruct((2, rows, NOPE + ROPE), BF)
    values = jax.ShapeDtypeStruct((2, rows, VDIM), BF)
    outs = (keys, values) if normed is None else (keys, keys, values)
    args, specs = [packed, expand_own, *tables], []
    specs = [
        row_tiles(packed.shape, tile),
        whole_block(expand_own.shape),
        row_tiles(tables[0].shape, tile),
        row_tiles(tables[1].shape, tile),
    ]
    if normed is not None:
        args = [normed, query_own] + args
        specs = [row_tiles(normed.shape, tile), whole_block((normed.shape[1], QUERY))] + specs
    return pl.pallas_call(
        other_heads_body if normed is None else own_heads_body,
        grid=(rows // tile,),
        out_shape=outs,
        in_specs=specs,
        out_specs=tuple(row_tiles(out.shape, tile) for out in outs),
        compiler_params=pltpu.CompilerParams(vmem_limit_bytes=LESS_VMEM),
        cost_estimate=SMALL,
    )(*args)


def back_rows_body(
    at_ref, nope_ref, rope_ref, pair_ref, pair_other_ref, key_rope_ref, key_rope_other_ref,
    cosine_ref, sine_ref, cosine_other_ref, sine_other_ref, query_weight_ref, expand_ref,
    flat_ref, part_ref, kept_ref, given_ref, terms_ref,
):
    swap = places(F32, ROPE, 0, True)

    def turned_back(values, cosine, sine):
        swapped = jnp.dot(
            values, swap, precision=lax.Precision.HIGHEST, preferred_element_type=F32
        )
        return (values * cosine - swapped * sine).astype(BF)

    cosine, sine = cosine_ref[...], sine_ref[...]
    flat_ref[:, : 2 * NOPE] = nope_ref[...]
    for head in range(2):
        at = 2 * NOPE + head * ROPE
        flat_ref[:, at : at + ROPE] = turned_back(rope_ref[head], cosine, sine)
    part_ref[...] = contract_cols(flat_ref[...], query_weight_ref[...]).astype(BF)
    rows = nope_ref.shape[0] // 2
    core = at_ref[1]
    for i, (pairs, ropes, cosine, sine) in enumerate(
        (
            (pair_ref, key_rope_ref, cosine, sine),
            (pair_other_ref, key_rope_other_ref, cosine_other_ref[...], sine_other_ref[...]),
        )
    ):
        terms = contract_cols(pairs[...], expand_ref[...]).astype(BF)
        rope = (
            turned_back(ropes[0], cosine, sine).astype(F32)
            + turned_back(ropes[1], cosine, sine).astype(F32)
        ).astype(BF)
        for c in range(2):
            terms_ref[c, :, :KV_RANK] = terms[c * rows : (c + 1) * rows]
            terms_ref[c, :, KV_RANK : KV_RANK + ROPE] = rope[c * rows : (c + 1) * rows]
            terms_ref[c, :, KV_RANK + ROPE :] = jnp.zeros((rows, PACKED - KV_RANK - ROPE), BF)
        place = pl.ds(at_ref[0] if i == 0 else 1 - at_ref[0], 1)
        kept_ref[place] = terms_ref[pl.ds(core, 1)]
        given_ref[place] = terms_ref[pl.ds(1 - core, 1)]


def back_rows(at, grads, tables, query_own, expand_own):
    nope, rope, pair, pair_other, key_rope, key_rope_other = grads
    rows, tile = nope.shape[0], 256
    args = [nope, rope, pair, pair_other, key_rope, key_rope_other, *tables]
    terms = jax.ShapeDtypeStruct((8, tile // 2, PACKED), BF)
    terms_spec = pl.BlockSpec((2, tile // 2, PACKED), lambda i: (i, 0, 0))
    outs = (
        jax.ShapeDtypeStruct((rows, QUERY), BF),
        jax.ShapeDtypeStruct((rows, query_own.shape[0]), BF),
    )
    return pl.pallas_call(
        back_rows_body,
        grid=(rows // tile,),
        out_shape=outs + (terms, terms),
        in_specs=[pl.BlockSpec(memory_space=pltpu.SMEM)]
        + [row_tiles(arg.shape, tile) for arg in args]
        + [whole_block((query_own.shape[0], QUERY)), whole_block(expand_own.shape)],
        out_specs=tuple(row_tiles(out.shape, tile) for out in outs) + (terms_spec, terms_spec),
        scratch_shapes=[pltpu.VMEM((2, tile // 2, PACKED), BF)],
        compiler_params=pltpu.CompilerParams(vmem_limit_bytes=VMEM_BYTES),
        cost_estimate=SMALL,
    )(at, *args, query_own, expand_own)


def scores_of(query, keys, own, other_first, t, block):
    scores = contract_cols(query, keys) * (NOPE + ROPE) ** (-0.5)
    count = scores.shape[0]
    row = lax.broadcasted_iota(jnp.int32, scores.shape, 0)
    col = lax.broadcasted_iota(jnp.int32, scores.shape, 1)
    if own:
        reach = jnp.where(t < block, count, 0)
    else:
        reach = jnp.where((t < block) | other_first, count, -count)
    return jnp.where(col <= row + reach, scores, -1e30)


def attend_body(
    at_ref, query_ref, key_ref, key_other_ref, value_ref, value_other_ref, out_ref, lse_ref, scores_ref
):
    count = query_ref.shape[1]
    block = pl.program_id(1)
    query = query_ref[0]
    other_first = at_ref[0] == 1
    sets = ((key_ref, value_ref, True, 0), (key_other_ref, value_other_ref, False, count))

    def score(t, top):
        at = pl.ds(pl.multiple_of(t * count, count), count)
        for keys, _, own, place in sets:
            scores = scores_of(query, keys[0, at, :], own, other_first, t, block)
            scores_ref[:, pl.ds(pl.multiple_of(2 * t * count + place, count), count)] = scores
            top = jnp.maximum(top, jnp.max(scores, axis=-1, keepdims=True))
        return top

    top = lax.fori_loop(0, block + 1, score, jnp.full((count, 1), -1e30, F32))

    def weigh(t, carry):
        row_total, summed = carry
        at = pl.ds(pl.multiple_of(t * count, count), count)
        for _, values, _, place in sets:
            scores = scores_ref[:, pl.ds(pl.multiple_of(2 * t * count + place, count), count)]
            exponent = jnp.exp(scores - top)
            row_total = row_total + jnp.sum(exponent, axis=-1, keepdims=True)
            summed = summed + matmul(exponent.astype(BF), values[0, at, :])
        return row_total, summed

    row_total, summed = lax.fori_loop(
        0, block + 1, weigh, (jnp.zeros((count, 1), F32), jnp.zeros((count, VDIM), F32))
    )
    out_ref[...] = (summed / row_total).astype(BF)
    lse_ref[0] = top + jnp.log(row_total)


def attend(xl_at, queries, keys, keys_other, values, values_other):
    heads, rows, depth = queries.shape
    count = rows // 4
    key_spec = pl.BlockSpec((1, rows, depth), lambda h, j: (h, 0, 0))
    value_spec = pl.BlockSpec((1, rows, VDIM), lambda h, j: (h, 0, 0))
    return pl.pallas_call(
        attend_body,
        grid=(heads, 4),
        out_shape=(
            jax.ShapeDtypeStruct((rows, heads * VDIM), BF),
            jax.ShapeDtypeStruct((heads, rows, 1), F32),
        ),
        in_specs=[
            pl.BlockSpec(memory_space=pltpu.SMEM),
            pl.BlockSpec((1, count, depth), lambda h, j: (h, j, 0)),
            key_spec,
            key_spec,
            value_spec,
            value_spec,
        ],
        out_specs=(
            pl.BlockSpec((count, VDIM), lambda h, j: (j, h)),
            pl.BlockSpec((1, count, 1), lambda h, j: (h, j, 0)),
        ),
        scratch_shapes=[pltpu.VMEM((count, 2 * rows), F32)],
        compiler_params=pltpu.CompilerParams(vmem_limit_bytes=LESS_VMEM),
        cost_estimate=SMALL,
    )(xl_at.reshape(1), queries, keys, keys_other, values, values_other)


def attend_back_body(
    at_ref, query_ref, key_ref, key_other_ref, value_ref, value_other_ref, grad_ref, lse_ref,
    nope_ref, rope_ref, pair_ref, pair_other_ref, key_rope_ref, key_rope_other_ref,
    probs_ref, grad_probs_ref, key_sum, key_other_sum, value_sum, value_other_sum,
):
    count = query_ref.shape[1]
    block = pl.program_id(1)
    query, grad = query_ref[0], grad_ref[...]
    other_first = at_ref[0] == 1
    scale = (NOPE + ROPE) ** (-0.5)
    sets = (
        (key_ref, value_ref, key_sum, value_sum, True, 0),
        (key_other_ref, value_other_ref, key_other_sum, value_other_sum, False, count),
    )

    @pl.when(block == 0)
    def _():
        for _, _, keys_to, values_to, _, _ in sets:
            keys_to[...] = jnp.zeros_like(keys_to)
            values_to[...] = jnp.zeros_like(values_to)

    def score(t, centered):
        at = pl.ds(pl.multiple_of(t * count, count), count)
        for keys, values, _, _, own, place in sets:
            to = pl.ds(pl.multiple_of(2 * t * count + place, count), count)
            scores = scores_of(query, keys[0, at, :], own, other_first, t, block)
            probs = jnp.exp(scores - lse_ref[0])
            grad_probs = contract_cols(grad, values[0, at, :])
            probs_ref[:, to] = probs
            grad_probs_ref[:, to] = grad_probs
            centered = centered + jnp.sum(probs * grad_probs, axis=-1, keepdims=True)
        return centered

    centered = lax.fori_loop(0, block + 1, score, jnp.zeros((count, 1), F32))

    def give(t, summed):
        at = pl.ds(pl.multiple_of(t * count, count), count)
        for keys, _, keys_to, values_to, _, place in sets:
            to = pl.ds(pl.multiple_of(2 * t * count + place, count), count)
            probs = probs_ref[:, to]
            grad_scores = (probs * (grad_probs_ref[:, to] - centered)).astype(BF)
            keys_to[at, :] += contract_rows(grad_scores, query)
            values_to[at, :] += contract_rows(probs.astype(BF), grad)
            summed = summed + matmul(grad_scores, keys[0, at, :])
        return summed

    grad_query = scale * lax.fori_loop(0, block + 1, give, jnp.zeros(query.shape, F32))
    nope_ref[...] = grad_query[:, :NOPE].astype(BF)
    rope_ref[0] = grad_query[:, NOPE:]

    @pl.when(block == 3)
    def _():
        for keys_from, values_from, to, rope_to in (
            (key_sum, value_sum, pair_ref, key_rope_ref),
            (key_other_sum, value_other_sum, pair_other_ref, key_rope_other_ref),
        ):
            to[:, :NOPE] = (scale * keys_from[:, :NOPE]).astype(BF)
            to[:, NOPE:] = values_from[...].astype(BF)
            rope_to[0] = scale * keys_from[:, NOPE:]


def attend_back(xl_at, queries, keys, keys_other, values, values_other, grads, lse):
    heads, rows, depth = queries.shape
    count = rows // 4
    key_spec = pl.BlockSpec((1, rows, depth), lambda h, j: (h, 0, 0))
    value_spec = pl.BlockSpec((1, rows, VDIM), lambda h, j: (h, 0, 0))
    pair = jax.ShapeDtypeStruct((rows, heads * (NOPE + VDIM)), BF)
    rope = jax.ShapeDtypeStruct((heads, rows, ROPE), F32)
    pair_spec = pl.BlockSpec((rows, NOPE + VDIM), lambda h, j: (0, h))
    rope_spec = pl.BlockSpec((1, rows, ROPE), lambda h, j: (h, 0, 0))
    return pl.pallas_call(
        attend_back_body,
        grid=(heads, 4),
        out_shape=(
            jax.ShapeDtypeStruct((rows, heads * NOPE), BF),
            rope,
            pair,
            pair,
            rope,
            rope,
        ),
        in_specs=[
            pl.BlockSpec(memory_space=pltpu.SMEM),
            pl.BlockSpec((1, count, depth), lambda h, j: (h, j, 0)),
            key_spec,
            key_spec,
            value_spec,
            value_spec,
            pl.BlockSpec((count, VDIM), lambda h, j: (j, h)),
            pl.BlockSpec((1, count, 1), lambda h, j: (h, j, 0)),
        ],
        out_specs=(
            pl.BlockSpec((count, NOPE), lambda h, j: (j, h)),
            pl.BlockSpec((1, count, ROPE), lambda h, j: (h, j, 0)),
            pair_spec,
            pair_spec,
            rope_spec,
            rope_spec,
        ),
        scratch_shapes=[pltpu.VMEM((count, 2 * rows), F32)] * 2
        + [pltpu.VMEM((rows, depth), F32)] * 2
        + [pltpu.VMEM((rows, VDIM), F32)] * 2,
        compiler_params=pltpu.CompilerParams(vmem_limit_bytes=VMEM_BYTES),
        cost_estimate=SMALL,
    )(xl_at.reshape(1), queries, keys, keys_other, values, values_other, grads, lse)


def group_columns(weight):
    rows, width = weight.shape[0], weight.shape[1] // 16
    return weight.reshape(rows, 4, 2, 2, width).transpose(1, 3, 0, 2, 4).reshape(8, rows, 2, width)


def ungroup_columns(parts):
    rows, width = parts.shape[1], parts.shape[3]
    return parts.reshape(4, 2, rows, 2, width).transpose(2, 0, 3, 1, 4).reshape(rows, 16 * width)


def spread_groups(parts):
    rows, width = parts.shape[1:]
    blocks = jnp.broadcast_to(
        parts.reshape(4, 1, 2, 1, 1, rows, width), (4, 2, 2, 4, 2, rows, width)
    )
    return blocks.reshape(128 * rows, width)


def to_replicas(rows):
    count, width = rows.shape
    blocks = jnp.broadcast_to(rows[None], (16, count, width)).reshape(16 * count, width)
    return lax.all_to_all(blocks, XYX, split_axis=0, concat_axis=0, tiled=True)


def in_row_order(rows):
    width = rows.shape[-1]
    blocks = rows.reshape(2, 8, 4, 2, 16, width).transpose(2, 0, 3, 1, 4, 5)
    return blocks.reshape(-1, width)


def exchange_all(blocks):
    return lax.all_to_all(blocks, ALL, split_axis=0, concat_axis=0, tiled=True)


def tie(*values):
    return lax.optimization_barrier(values)


def halves(gate, up, down):
    turned = down.T
    units = gate.shape[1]
    first = [part[:, :HALF] for part in (gate, up, turned)]
    second = [part[:, units - HALF :] for part in (gate, up, turned)]
    repeated = 2 * HALF - units
    keep = lax.broadcasted_iota(jnp.int32, second[0].shape, 1) >= repeated
    second = [jnp.where(keep, second[0], 0), jnp.where(keep, second[1], 0), second[2]]
    return jnp.concatenate(first, axis=-1), jnp.concatenate(second, axis=-1)


def meet(values, turn):
    pairs = [(2 * c + xh, 2 * (xh ^ turn) + c) for c in range(2) for xh in range(2)]
    return lax.ppermute(values, ("c", "xh"), pairs)


def part(values, turn):
    pairs = [(2 * c + xh, 2 * xh + (c ^ turn)) for c in range(2) for xh in range(2)]
    return lax.ppermute(values, ("c", "xh"), pairs)


def total(*terms):
    return sum(term.astype(F32) for term in terms).astype(BF)


def expert_body(at_ref, *refs):
    pieces, (own_ref, other_ref) = refs[:8], refs[8:10]
    own_out, other_out, own_kept, other_kept = refs[10:14]
    weights, sem = refs[14:]
    copies = [
        pltpu.make_async_copy(
            pieces[i], weights.at[pl.ds(pl.multiple_of(at_ref[i] * 256, 256), 256)], sem.at[i]
        )
        for i in range(8)
    ]
    for copy in copies:
        copy.start()
    for copy in copies:
        copy.wait()
    width = own_ref.shape[1] // 2
    for given, result, kept in (
        (own_ref, own_out, own_kept),
        (other_ref, other_out, other_kept),
    ):

        @pl.loop(0, HALF // 256)
        def _(n, given=given, kept=kept):
            def columns(k):
                return pl.ds(pl.multiple_of(k * HALF + n * 256, 256), 256)

            rows, grads = given[:, :width], given[:, width:]
            pre = matmul(rows, weights[:, columns(0)])
            lin = matmul(rows, weights[:, columns(1)])
            grad = matmul(grads, weights[:, columns(2)])
            sigmoid = jax.nn.sigmoid(pre)
            silu = pre * sigmoid
            kept[:, columns(0)] = (grad * lin * sigmoid * (1.0 + pre * (1.0 - sigmoid))).astype(BF)
            kept[:, columns(1)] = (grad * silu).astype(BF)
            kept[:, columns(2)] = (silu * lin).astype(BF)

        @pl.loop(0, width // 256)
        def _(f, kept=kept, result=result):
            block = weights[pl.ds(pl.multiple_of(f * 256, 256), 256), :]
            out = contract_cols(kept[:, 2 * HALF :], block[:, 2 * HALF :])
            back = contract_cols(kept[:, : 2 * HALF], block[:, : 2 * HALF])
            result[:, pl.ds(pl.multiple_of(f * 256, 256), 256)] = out.astype(BF)
            result[:, pl.ds(pl.multiple_of(width + f * 256, 256), 256)] = back.astype(BF)


def expert_rows(order, pieces, own, other):
    rows, width = own.shape
    kept = jax.ShapeDtypeStruct((rows, 3 * HALF), BF)
    result = jax.ShapeDtypeStruct((rows, width), BF)
    whole = pl.BlockSpec(memory_space=pltpu.VMEM)
    return pl.pallas_call(
        expert_body,
        out_shape=(result, result, kept, kept),
        in_specs=[pl.BlockSpec(memory_space=pltpu.SMEM)]
        + [pl.BlockSpec(memory_space=pl.ANY)] * 8
        + [whole] * 2,
        out_specs=(whole,) * 4,
        scratch_shapes=[pltpu.VMEM((width // 2, 3 * HALF), BF), pltpu.SemaphoreType.DMA((8,))],
        compiler_params=pltpu.CompilerParams(vmem_limit_bytes=VMEM_BYTES),
        cost_estimate=SMALL,
    )(order, *pieces, own, other)


def expert_grad_body(
    at_ref, own_rows, own_grads, other_rows, other_grads, own_kept, other_kept, *outs
):
    first = contract_rows(own_rows[...], own_kept[:, : 2 * HALF]) + contract_rows(
        other_rows[...], other_kept[:, : 2 * HALF]
    )
    last = contract_rows(own_grads[...], own_kept[:, 2 * HALF :]) + contract_rows(
        other_grads[...], other_kept[:, 2 * HALF :]
    )
    for i, out in enumerate(outs):

        @pl.when(pl.program_id(0) == i)
        def _(out=out):
            out[:, : 2 * HALF] = first.astype(BF)
            out[:, 2 * HALF :] = last.astype(BF)


def expert_grads(order, own, other, own_kept, other_kept):
    rows, width = own.shape
    blocks, count = width // 512, order.shape[0]
    row_spec = pl.BlockSpec((rows, 256), lambda i, at: (0, at[i]))
    grad_spec = pl.BlockSpec((rows, 256), lambda i, at: (0, blocks + at[i]))
    kept_spec = pl.BlockSpec((rows, 3 * HALF), lambda i, at: (0, 0))
    return pl.pallas_call(
        expert_grad_body,
        out_shape=(jax.ShapeDtypeStruct((256, 3 * HALF), BF),) * count,
        grid_spec=pltpu.PrefetchScalarGridSpec(
            num_scalar_prefetch=1,
            grid=(count,),
            in_specs=[row_spec, grad_spec, row_spec, grad_spec, kept_spec, kept_spec],
            out_specs=(pl.BlockSpec((256, 3 * HALF), lambda i, at: (0, 0)),) * count,
        ),
        compiler_params=pltpu.CompilerParams(vmem_limit_bytes=LESS_VMEM),
        cost_estimate=SMALL,
    )(order, own, own, other, other, own_kept, other_kept)


def shared_body(rows_ref, grads_ref, gate_up_ref, down_ref, back_ref, out_ref, kept_ref):
    both = matmul(rows_ref[...], gate_up_ref[...])
    pre, lin = both[:, :UNIT_PAD], both[:, UNIT_PAD:]
    grad = contract_cols(grads_ref[...], down_ref[...])
    sigmoid = jax.nn.sigmoid(pre)
    silu = pre * sigmoid
    hidden = (silu * lin).astype(BF)
    grad_pre = (grad * lin * sigmoid * (1.0 + pre * (1.0 - sigmoid))).astype(BF)
    grad_lin = (grad * silu).astype(BF)
    kept_ref[:, :UNIT_PAD] = grad_pre
    kept_ref[:, UNIT_PAD : 2 * UNIT_PAD] = grad_lin
    kept_ref[:, 2 * UNIT_PAD :] = hidden
    back_ref[...] = contract_cols(kept_ref[:, : 2 * UNIT_PAD], gate_up_ref[...]).astype(BF)
    out_ref[...] = matmul(hidden, down_ref[...]).astype(BF)


def shared_rows(rows, grads, gate_up, down):
    count, width = rows.shape
    tile = 256
    row_spec = pl.BlockSpec((tile, width), lambda i: (i, 0))
    return pl.pallas_call(
        shared_body,
        grid=(count // tile,),
        out_shape=(
            jax.ShapeDtypeStruct((count, width), BF),
            jax.ShapeDtypeStruct((count, width), BF),
            jax.ShapeDtypeStruct((count, 3 * UNIT_PAD), BF),
        ),
        in_specs=[
            row_spec,
            row_spec,
            pl.BlockSpec(gate_up.shape, lambda i: (0, 0)),
            pl.BlockSpec(down.shape, lambda i: (0, 0)),
        ],
        out_specs=(row_spec, row_spec, pl.BlockSpec((tile, 3 * UNIT_PAD), lambda i: (i, 0))),
        compiler_params=pltpu.CompilerParams(vmem_limit_bytes=VMEM_BYTES),
        cost_estimate=SMALL,
    )(rows, grads, gate_up, down)


def by_replica_spec(width):
    return pl.BlockSpec((1, 8, 2, 16, width), lambda i: (i % 2, 0, i // 2, 0, 0))


def put_by_replica(out_ref, values, at):
    for c in range(2):
        for f in range(8):
            row = (c * 8 + f) * 16
            out_ref[0, f, c, :, at : at + values.shape[1]] = values[row : row + 16]


def last_rows_body(
    one_ref, two_ref, first_terms_ref, second_terms_ref, latent_ref, logits_ref, extra_ref, out_ref
):
    column = lax.broadcasted_iota(jnp.int32, logits_ref.shape, 1)
    latent = contract_rows(one_ref[...], latent_ref[...])
    put_by_replica(out_ref, latent[:, :KV_RANK].astype(BF), 0)
    last = latent[:, KV_RANK:] + contract_rows(two_ref[...], logits_ref[...])
    last = last + contract_rows(first_terms_ref[...], (column == 80).astype(BF))
    last = last + contract_rows(second_terms_ref[...], (column == 81).astype(BF))
    put_by_replica(out_ref, (last + extra_ref[...]).astype(BF), KV_RANK)


def last_rows(normed_one, normed_two, first_terms, second_terms, latent, logits, extra):
    rows, length = normed_one.shape
    tile = 256
    column_spec = pl.BlockSpec((rows, tile), lambda i: (0, i))
    out = jax.ShapeDtypeStruct((2, 8, 8, 16, PACKED), BF)
    return pl.pallas_call(
        last_rows_body,
        grid=(length // tile,),
        out_shape=out,
        in_specs=[column_spec] * 4
        + [whole_block(latent.shape), whole_block(logits.shape), row_tiles(extra.shape, tile)],
        out_specs=by_replica_spec(PACKED),
        compiler_params=pltpu.CompilerParams(vmem_limit_bytes=VMEM_BYTES),
        cost_estimate=SMALL,
    )(normed_one, normed_two, first_terms, second_terms, latent, logits, extra)


def head_sums_body(in_ref, query_ref, expand_ref):
    for z in range(4):
        for c in range(2):

            summed = in_ref[z * 2 + c].astype(F32)
            for xl in range(2):
                part = z * 4 + xl * 2 + c
                at = part * (NOPE + ROPE)
                query_ref[:, at : at + NOPE] = summed[:, xl * NOPE : (xl + 1) * NOPE]
                rope_at = 2 * NOPE + xl * ROPE
                query_ref[:, at + NOPE : at + NOPE + ROPE] = summed[:, rope_at : rope_at + ROPE]
                for half in range(2):
                    j = 2 * xl + half
                    at = part * 256 + half * 128
                    expand_ref[:, at : at + 128] = summed[4 * j : 4 * j + 4, 384:]


def head_sums(arrived):
    whole = pl.BlockSpec(memory_space=pltpu.VMEM)
    return pl.pallas_call(
        head_sums_body,
        out_shape=(
            jax.ShapeDtypeStruct((16, 16 * (NOPE + ROPE)), F32),
            jax.ShapeDtypeStruct((4, 4096), F32),
        ),
        in_specs=[whole],
        out_specs=(whole,) * 2,
        compiler_params=pltpu.CompilerParams(vmem_limit_bytes=LESS_VMEM),
        cost_estimate=SMALL,
    )(arrived)


def query_grads_body(normed_ref, flat_ref, out_ref):
    put_by_replica(out_ref, contract_rows(normed_ref[...], flat_ref[...]).astype(BF), 0)


def query_grads(normed, flat):
    tile = 256
    return pl.pallas_call(
        query_grads_body,
        grid=(normed.shape[1] // tile,),
        out_shape=jax.ShapeDtypeStruct((2, 8, 8, 16, flat.shape[1]), BF),
        in_specs=[
            pl.BlockSpec((normed.shape[0], tile), lambda i: (0, i)),
            whole_block(flat.shape),
        ],
        out_specs=by_replica_spec(flat.shape[1]),
        compiler_params=pltpu.CompilerParams(vmem_limit_bytes=LESS_VMEM),
        cost_estimate=SMALL,
    )(normed, flat)


def unit_columns_out(weight):
    runs = group_columns(weight).reshape(8, 16, 16, -1)
    return jnp.pad(runs, ((0, 0), (0, 0), (0, 0), (0, 24 - runs.shape[-1]))).reshape(8, 16, -1)


def unit_columns_back(parts, units):
    runs = parts.reshape(8, 16, 16, 24)[..., : units // 8]
    return ungroup_columns(runs.reshape(8, 16, 2, units))


def on_device(
    tokens,
    positions,
    routes,
    first_gain,
    query_weight,
    latent_weight,
    latent_gain,
    expand_weight,
    output_weight,
    second_gain,
    router_weight,
    shared_gate,
    shared_up,
    shared_down,
    expert_gate,
    expert_up,
    expert_down,
    cotangent,
):
    z_at, xl_at, c_at = lax.axis_index("z"), lax.axis_index("xl"), lax.axis_index("c")
    y_at, xh_at = lax.axis_index("y"), lax.axis_index("xh")
    own_tokens = tokens[0]
    row_count, width = own_tokens.shape
    length = 16 * row_count
    expert_count = router_weight.shape[1]
    units = shared_gate.shape[1] // 16

    half_tokens = lax.all_gather(own_tokens, ZC, axis=0, tiled=True)

    cosine_table, sine_table = rotary_tables(positions[0])

    def half_rows(table, at):
        return lax.dynamic_index_in_dim(
            table.reshape(4, 2, 2 * row_count, -1), at, axis=1, keepdims=False
        ).reshape(length // 2, -1)

    wide = wide_tables(cosine_table, sine_table)
    tables = [half_rows(table, at) for at in (xl_at, 1 - xl_at) for table in wide]
    route_ids = routes[0]
    route_hot = (
        route_ids[:, :, None] == jnp.arange(expert_count, dtype=jnp.int32)[None, None, :]
    ).astype(F32)
    grad_result = cotangent[0]
    grad_float = grad_result.astype(F32)
    route_total = row_count * TOP
    flat_hot = route_hot.reshape(route_total, expert_count).astype(BF)
    earlier = (
        jnp.arange(route_total, dtype=jnp.int32)[:, None]
        > jnp.arange(route_total, dtype=jnp.int32)[None, :]
    ).astype(BF)
    before = matmul(earlier, flat_hot)
    slot_place = jnp.sum(before * flat_hot.astype(F32), axis=-1).astype(jnp.int32)
    slot_ids = (route_ids.reshape(route_total) * SLOTS + slot_place).reshape(row_count, TOP)
    slot_match = (
        jnp.arange(expert_count * SLOTS, dtype=jnp.int32)[:, None, None] == slot_ids[None, :, :]
    )
    dispatch = jnp.any(slot_match, axis=-1).astype(BF)
    picks = (
        jnp.arange(expert_count * SLOTS, dtype=jnp.int32)[None, :]
        == slot_ids.T.reshape(-1)[:, None]
    ).astype(BF)
    dispatch_grads = matmul(dispatch, grad_result)
    first_half, second_half = halves(expert_gate[0], expert_up[0], expert_down[0])
    met = [jnp.where((xh_at ^ turn) == 0, first_half, second_half) for turn in range(2)]

    query_group = group_columns(query_weight)
    expand_group = group_columns(expand_weight).reshape(8, 16, 128)
    head_group = jnp.concatenate(
        [
            query_group[..., :NOPE].reshape(8, 16, 2 * NOPE),
            query_group[..., NOPE:].reshape(8, 16, 2 * ROPE),
            expand_group,
        ],
        axis=-1,
    )
    common = jnp.concatenate(
        [
            latent_weight,
            router_weight,
            first_gain[:, None],
            second_gain[:, None],
            jnp.pad(latent_gain, (0, 12))[:, None],
            jnp.zeros((16, 45), BF),
        ],
        axis=-1,
    )
    unit_group = jnp.concatenate(
        [unit_columns_out(weight) for weight in (shared_gate, shared_up)], axis=-1
    ).reshape(128, 768)
    common_in = exchange_all(jnp.broadcast_to(common[None], (128, 16, 640)).reshape(2048, 640))
    met = [meet(met[turn], turn) for turn in range(2)]
    head_group = spread_groups(head_group)
    unit_group, common_in = tie(unit_group, common_in)
    unit_group = lax.all_to_all(unit_group, ZC, split_axis=0, concat_axis=0, tiled=True)

    half_tokens, common_in, met, head_group = tie(half_tokens, common_in, met, head_group)
    above, below = [None, None], [None, None]
    above[0], below[0] = shift(met[0], "y", 1), shift(met[0], "y", -1)
    head_in = exchange_all(head_group)
    gains = common_in[:, 512:640].T.astype(F32)
    first_norm_gain, second_norm_gain = gains[80], gains[81]
    latent_norm_gain = gains[82].reshape(128, 16)[:, :4].reshape(KV_RANK)
    latent_full = common_in[:, :576]
    router_full = common_in[:, 576:592]
    latent_mine, normed_half, latent_half = front(
        half_tokens, first_norm_gain, latent_full, latent_norm_gain
    )
    latent_other = shift(latent_mine, "xl", 1)

    down_count = shared_down.shape[0]
    down_rows = jnp.concatenate(
        [output_weight, jnp.pad(shared_down, ((0, 24 - down_count), (0, 0)))], axis=0
    )
    latent_other, latent_mine, normed_half, head_in, met, down_rows, grad_result, tables, unit_group, above[0], below[0], dispatch, dispatch_grads, picks = tie(
        latent_other, latent_mine, normed_half, head_in, met, down_rows, grad_result, tables, unit_group, above[0], below[0], dispatch, dispatch_grads, picks
    )
    down_all = to_replicas(down_rows).reshape(16, 40, width)
    seq_grad = lax.all_gather(grad_result, ZC, axis=0, tiled=True)
    expand_own = head_in[:, 384:].reshape(KV_RANK, 512)
    queries, keys, values = heads_of(latent_mine, expand_own, tables[:2], normed_half, head_in)

    keys_other, values_other = heads_of(latent_other, expand_own, tables[2:])

    attended_own, row_lse = attend(xl_at, queries, keys, keys_other, values, values_other)

    attended_own, row_lse, seq_grad, unit_group, down_all = tie(
        attended_own, row_lse, seq_grad, unit_group, down_all
    )
    output_own = down_all[:, :16].reshape(256, width)
    attended_part = matmul(attended_own, output_own).astype(BF)
    attended_sum = lax.psum_scatter(attended_part, ZC, scatter_dimension=0, tiled=True)
    unit_columns = to_replicas(unit_group)

    attended_sum, unit_columns, met[1], above[0], down_all = tie(
        attended_sum, unit_columns, met[1], above[0], down_all
    )
    unit_columns = in_row_order(unit_columns)
    sdown_own = down_all[:, 16:].reshape(UNIT_PAD, width)
    above[1], below[1] = shift(met[1], "y", 1), shift(met[1], "y", -1)
    input_rows = own_tokens.astype(F32)
    middle = input_rows + attended_sum.astype(F32)
    scaled_two, inverse_two = normalize(middle)
    normed_two = (scaled_two * second_norm_gain).astype(BF)
    seq_normed_two = lax.all_gather(normed_two, ZC, axis=0, tiled=True)
    logits = matmul(normed_two, router_full)
    chosen = jnp.sum(route_hot * logits[:, None, :], axis=-1)
    gate_values = jax.nn.softmax(chosen, axis=-1)
    slot_gates = jnp.sum(jnp.where(slot_match, gate_values[None], 0.0), axis=(1, 2))
    sent_rows = matmul(dispatch, normed_two).astype(BF)
    sent_grads = (dispatch_grads * slot_gates[:, None]).astype(BF)
    sent = jnp.concatenate([sent_rows, sent_grads], axis=-1)

    sent, seq_normed_two, above[0], above[1], below[1], unit_columns, sdown_own = tie(
        sent, seq_normed_two, above[0], above[1], below[1], unit_columns, sdown_own
    )
    own_in = lax.all_to_all(sent, ZXX, split_axis=0, concat_axis=0, tiled=True)
    far = [shift(above[0], "y", 1), shift(below[1], "y", -1)]

    back_part, out_part, shared_kept = shared_rows(
        seq_normed_two, seq_grad, unit_columns, sdown_own
    )
    grad_units = contract_rows(seq_normed_two, shared_kept[:, : 2 * UNIT_PAD]).astype(BF)
    grad_sdown = contract_rows(shared_kept[:, 2 * UNIT_PAD :], seq_grad).astype(BF)

    own_in, back_part, out_part, grad_units, grad_sdown, far = tie(
        own_in, back_part, out_part, grad_units, grad_sdown, far
    )
    shared_back = lax.psum_scatter(back_part, ZC, scatter_dimension=0, tiled=True)
    units_in = exchange_all(grad_units)
    other_in = shift(own_in, "c", 1)
    pieces = [met[0], met[1], above[0], above[1], far[0], far[1], below[0], below[1]]
    order = jnp.stack(
        [((y_at + step) % 4) * 2 + (c_at ^ turn) for step in range(4) for turn in range(2)]
    ).astype(jnp.int32)
    own_back, other_back, own_kept, other_kept = expert_rows(order, pieces, own_in, other_in)
    other_back, units_in = tie(other_back, units_in)
    back = total(own_back, shift(other_back, "c", 1))

    back, own_kept, other_kept = tie(back, own_kept, other_kept)
    returned = lax.all_to_all(back, ZXX, split_axis=0, concat_axis=0, tiled=True)
    blocks = [None] * 8
    blocks[4], blocks[5] = expert_grads(
        jnp.stack([order[4], order[5]]), own_in, other_in, own_kept, other_kept
    )
    from_below = shift(blocks[4], "y", -1)
    from_above = shift(blocks[5], "y", 1)
    own_kept, blocks[4] = tie(own_kept, blocks[4])
    blocks[3], blocks[6] = expert_grads(
        jnp.stack([order[3], order[6]]), own_in, other_in, own_kept, other_kept
    )
    upward_free, downward_free = shift(blocks[3], "y", -1), shift(blocks[6], "y", 1)
    own_kept, blocks[3] = tie(own_kept, blocks[3])
    blocks[2], blocks[7], blocks[0], blocks[1] = expert_grads(
        jnp.stack([order[2], order[7], order[0], order[1]]), own_in, other_in, own_kept, other_kept
    )

    returned, shared_back, from_below, from_above, blocks[0], blocks[2], blocks[7] = tie(
        returned, shared_back, from_below, from_above, blocks[0], blocks[2], blocks[7]
    )
    upward_last = total(blocks[2], from_below)
    downward_last = total(blocks[7], from_above)
    picked = matmul(picks, returned).reshape(TOP, row_count, 2 * width)
    picked_out = picked[:, :, :width]
    grad_normed_routed = picked[0, :, width:] + picked[1, :, width:]
    routed = gate_values[:, :1] * picked_out[0] + gate_values[:, 1:] * picked_out[1]
    grad_gates = jnp.stack(
        [jnp.sum(grad_float * picked_out[k], axis=-1) for k in range(TOP)], axis=-1
    )
    centered_gates = grad_gates - jnp.sum(gate_values * grad_gates, axis=-1, keepdims=True)
    grad_chosen = gate_values * centered_gates
    grad_logits = jnp.sum(route_hot * grad_chosen[:, :, None], axis=1).astype(BF)
    grad_normed_router = contract_cols(grad_logits, router_full)
    grad_normed_two = shared_back.astype(F32) + grad_normed_routed + grad_normed_router
    grad_from_norm, gain_second_terms = norm_back(
        grad_normed_two, second_norm_gain, scaled_two, inverse_two
    )
    grad_middle = grad_float + grad_from_norm

    grad_middle, upward_last, downward_last, upward_free, downward_free, units_in = tie(
        grad_middle, upward_last, downward_last, upward_free, downward_free, units_in
    )
    seq_grad_middle = lax.all_gather(grad_middle.astype(BF), ZC, axis=0, tiled=True)
    upward_last = shift(upward_last, "y", -1)
    downward_last = shift(downward_last, "y", 1)

    units_sum = jnp.sum(
        units_in.reshape(4, 2, 2, 8, 16, 2 * UNIT_PAD).astype(F32), axis=(1, 3)
    ).reshape(8, 16, 2 * UNIT_PAD)
    unit_results = [
        unit_columns_back(units_sum[..., :UNIT_PAD], units),
        unit_columns_back(units_sum[..., UNIT_PAD:], units),
    ]
    seq_grad_middle, upward_last, downward_last, out_part, unit_results = tie(
        seq_grad_middle, upward_last, downward_last, out_part, unit_results
    )
    shared_out = lax.psum_scatter(out_part, ZC, scatter_dimension=0, tiled=True)
    grad_output = contract_rows(attended_own, seq_grad_middle).astype(BF)
    down_grads = jnp.concatenate(
        [grad_output.reshape(16, 16, width), grad_sdown.reshape(16, 24, width)], axis=1
    ).reshape(640, width)
    down_in = lax.all_to_all(down_grads, XYX, split_axis=0, concat_axis=0, tiled=True)
    grad_heads = contract_cols(seq_grad_middle, output_own).astype(BF)
    attention_grads = attend_back(
        xl_at, queries, keys, keys_other, values, values_other, grad_heads, row_lse
    )

    attention_grads, shared_out = tie(attention_grads, shared_out)
    _, _, pair, pair_other, _, _ = attention_grads
    grad_query_flat, normed_part, latent_kept, latent_given = back_rows(
        jnp.stack([xl_at, c_at]), attention_grads, tables, head_in, expand_own
    )
    grad_query_flat, normed_part, latent_kept, latent_given, down_in = tie(
        grad_query_flat, normed_part, latent_kept, latent_given, down_in
    )
    latent_sums = total(latent_kept, shift(latent_given, "c", 1)).reshape(8 * row_count, -1)
    latent_in = lax.all_to_all(latent_sums, ("z", "xl"), split_axis=0, concat_axis=0, tiled=True)
    grad_normed_part = lax.psum_scatter(normed_part, ZC, scatter_dimension=0, tiled=True)
    grad_expand = (
        contract_rows(latent_mine[:, :KV_RANK], pair)
        + contract_rows(latent_other[:, :KV_RANK], pair_other)
    ).astype(BF)
    grad_query_w = query_grads(normed_half, grad_query_flat)
    grad_expand = grad_expand.reshape(4, 2, 2, 8, 4, 4, 128).transpose(1, 3, 0, 2, 5, 4, 6)
    head_grads = jnp.concatenate(
        [grad_query_w.reshape(length, QUERY), grad_expand.reshape(length, 128)], axis=-1
    )

    summed = [
        total(blocks[0], upward_last, downward_free),
        total(blocks[1], upward_free, downward_last),
    ]
    latent_in, head_grads, summed = tie(latent_in, head_grads, summed)
    heads_in = lax.all_to_all(head_grads, XYX, split_axis=0, concat_axis=0, tiled=True)
    parted = [part(summed[turn], turn) for turn in range(2)]
    grad_latent_sum = jnp.sum(latent_in.reshape(8, row_count, -1).astype(F32), axis=0)
    scaled_one, inverse_one = normalize(input_rows)
    normed_one = (scaled_one * first_norm_gain).astype(BF)
    latent_own = lax.dynamic_slice_in_dim(
        latent_half, (z_at * 2 + c_at) * row_count, row_count, axis=0
    )
    scaled_latent, inverse_latent = normalize(latent_own[:, :KV_RANK])
    grad_latent, gain_latent_terms = norm_back(
        grad_latent_sum[:, :KV_RANK], latent_norm_gain, scaled_latent, inverse_latent
    )
    grad_latent_all = jnp.concatenate(
        [grad_latent, grad_latent_sum[:, KV_RANK : KV_RANK + ROPE]], axis=-1
    ).astype(BF)
    grad_normed_one = grad_normed_part.astype(F32) + contract_cols(grad_latent_all, latent_full)
    grad_input_norm, gain_first_terms = norm_back(
        grad_normed_one, first_norm_gain, scaled_one, inverse_one
    )

    gain_latent = jnp.sum(gain_latent_terms, axis=0).reshape(128, 1, 4)
    final_out = last_rows(
        normed_one,
        normed_two,
        gain_first_terms.astype(BF),
        gain_second_terms.astype(BF),
        jnp.pad(grad_latent_all, ((0, 0), (0, PACKED - KV_RANK - ROPE))),
        jnp.pad(grad_logits, ((0, 0), (64, 48))),
        jnp.pad(gain_latent, ((0, 0), (0, 15), (96, 28))).reshape(length, 128),
    )

    down_in = down_in.reshape(16, 40, width)
    grad_output_w = jnp.sum(down_in[:, :16].astype(F32), axis=0)
    grad_sdown_w = jnp.sum(down_in[:, 16 : 16 + down_count].astype(F32), axis=0)
    final_out, heads_in, parted, grad_output_w, grad_sdown_w = tie(
        final_out, heads_in, parted, grad_output_w, grad_sdown_w
    )
    final_in = lax.all_to_all(
        final_out.reshape(length, PACKED), XYX, split_axis=0, concat_axis=0, tiled=True
    )

    grad_inputs = grad_middle + grad_input_norm
    result = middle + shared_out.astype(F32) + routed
    first_half = jnp.where(xh_at == 0, parted[0], parted[1])
    second_half = jnp.where(xh_at == 0, parted[1], parted[0])
    repeated = 2 * HALF - expert_gate.shape[2]
    expert_results = [
        jnp.concatenate(
            [
                first_half[:, k * HALF : (k + 1) * HALF],
                second_half[:, k * HALF + repeated : (k + 1) * HALF],
            ],
            axis=-1,
        ).astype(F32)
        for k in range(3)
    ]
    expert_results[2] = expert_results[2].T
    heads_sum = jnp.sum(heads_in.reshape(16, 128, 512).astype(F32), axis=0).astype(BF)
    beside = (grad_inputs, result, expert_results, grad_output_w, grad_sdown_w, unit_results)
    final_in, heads_sum, beside = tie(final_in, heads_sum, beside)
    grad_inputs, result, expert_results, grad_output_w, grad_sdown_w, unit_results = beside
    common_part = jnp.sum(final_in.reshape(16, 128, PACKED).astype(F32), axis=0).astype(BF)
    groups_in = lax.all_to_all(
        jnp.concatenate([heads_sum, common_part], axis=-1),
        ZC,
        split_axis=0,
        concat_axis=0,
        tiled=True,
    ).reshape(8, 16, 512 + PACKED)
    grad_query_weight, grad_expand_weight = head_sums(groups_in[..., :512])
    common_sum = jnp.sum(groups_in[..., 512:].astype(F32), axis=0)
    return (
        result.astype(BF)[None],
        grad_inputs.astype(BF)[None],
        common_sum[:, 592],
        grad_query_weight,
        common_sum[:, :576],
        common_sum[0, 608:612],
        grad_expand_weight,
        grad_output_w,
        common_sum[:, 593],
        common_sum[:, 576:592],
        unit_results[0],
        unit_results[1],
        grad_sdown_w,
        expert_results[0][None],
        expert_results[1][None],
        expert_results[2][None],
    )


def solution(mesh):
    fine = Mesh(mesh.devices.reshape(4, 2, 2, 4, 2), ALL)
    return jax.shard_map(
        on_device,
        mesh=fine,
        in_specs=(
            P(FSDP, SEQ, None),
            P(FSDP, None),
            P(FSDP, SEQ, None),
            P(ALL),
            P(ALL, None),
            P(ALL, None),
            P(ALL),
            P(ALL, None),
            P(ALL, None),
            P(ALL),
            P(ALL, None),
            P(ALL, None),
            P(ALL, None),
            P(ALL, None),
            P(SEQ, FSDP, None),
            P(SEQ, FSDP, None),
            P(SEQ, None, FSDP),
            P(FSDP, SEQ, None),
        ),
        out_specs=(
            P(FSDP, SEQ, None),
            P(FSDP, SEQ, None),
            P(ALL),
            P(ALL, None),
            P(ALL, None),
            P(ALL),
            P(ALL, None),
            P(ALL, None),
            P(ALL),
            P(ALL, None),
            P(ALL, None),
            P(ALL, None),
            P(ALL, None),
            P(SEQ, FSDP, None),
            P(SEQ, FSDP, None),
            P(SEQ, None, FSDP),
        ),
        check_vma=False,
    )
```

```python
import math

import jax
import jax.numpy as jnp
from jax import lax
from jax.experimental import pallas as pl
from jax.experimental.pallas import tpu as pltpu
from jax.sharding import Mesh
from jax.sharding import PartitionSpec as P

NOPE = 128
ROPE = 64
VDIM = 128
KV_RANK = 512
TOP = 2
UNIT_PAD = 384
SLOTS = 24
HALF = 768
PACKED = 640
QUERY = 384
EPSILON = 1e-06
VMEM_BYTES = 60 * 2**20
LESS_VMEM = 40 * 2**20
SMALL = pl.CostEstimate(flops=1024, bytes_accessed=2**18, transcendentals=0)

SEQ = ("z", "xl", "c")
FSDP = ("y", "xh")
ZC = ("z", "c")
XYX = ("xl", "y", "xh")
ZXX = ("z", "xl", "xh")
ALL = ("z", "xl", "c", "y", "xh")
BF = jnp.bfloat16
F32 = jnp.float32


def matmul(left_side, right_side):
    return jnp.dot(left_side, right_side, preferred_element_type=F32)


def contract_rows(left_side, right_side):
    return lax.dot_general(
        left_side, right_side, (((0,), (0,)), ((), ())), preferred_element_type=F32
    )


def contract_cols(left_side, right_side):
    return lax.dot_general(
        left_side, right_side, (((1,), (1,)), ((), ())), preferred_element_type=F32
    )


def normalize(values):
    inverse = lax.rsqrt(jnp.mean(values * values, axis=-1, keepdims=True) + EPSILON)
    return (values * inverse, inverse)


def norm_back(grad_normed, gain_vector, scaled, inverse):
    grad_scaled = grad_normed * gain_vector
    grad_input = inverse * (
        grad_scaled - scaled * jnp.mean(grad_scaled * scaled, axis=-1, keepdims=True)
    )
    return (grad_input, grad_normed * scaled)


def rotary_tables(position_list):
    half_rope = ROPE // 2
    frequency = jnp.exp(-(2.0 * jnp.arange(half_rope, dtype=F32) / ROPE) * math.log(10000.0))
    angles = position_list.astype(F32)[:, None] * frequency[None, :]
    return (jnp.cos(angles), jnp.sin(angles))


def wide_tables(cosine_table, sine_table):
    return (
        jnp.concatenate([cosine_table, cosine_table], axis=-1),
        jnp.concatenate([-sine_table, sine_table], axis=-1),
    )


def places(kind, rows, head, swapped):
    row = lax.broadcasted_iota(jnp.int32, (rows, ROPE), 0)
    col = lax.broadcasted_iota(jnp.int32, (rows, ROPE), 1)
    if swapped:
        col = (col + ROPE // 2) % ROPE
    return (row == col + head * ROPE).astype(kind)


def shift(values, axis_name, step):
    count = lax.axis_size(axis_name)
    return lax.ppermute(values, axis_name, [((i + step) % count, i) for i in range(count)])


def front_body(
    rows_ref, gain_ref, weight_ref, latent_gain_ref, packed_ref, normed_ref, latent_ref
):
    scaled, _ = normalize(rows_ref[...].astype(F32))
    normed = (scaled * gain_ref[...]).astype(BF)
    latent = matmul(normed, weight_ref[...])
    normed_ref[...] = normed
    latent_ref[...] = latent
    scaled_latent, _ = normalize(latent[:, :KV_RANK])
    packed_ref[:, :KV_RANK] = (scaled_latent * latent_gain_ref[...]).astype(BF)
    packed_ref[:, KV_RANK : KV_RANK + ROPE] = latent[:, KV_RANK:].astype(BF)
    packed_ref[:, KV_RANK + ROPE :] = jnp.zeros((latent.shape[0], PACKED - KV_RANK - ROPE), BF)


def front(rows, gain, weight, latent_gain):
    count, width = rows.shape
    columns, tile = weight.shape[1], 256
    outs = (
        jax.ShapeDtypeStruct((count, PACKED), BF),
        jax.ShapeDtypeStruct((count, width), BF),
        jax.ShapeDtypeStruct((count, columns), F32),
    )
    return pl.pallas_call(
        front_body,
        grid=(count // tile,),
        out_shape=outs,
        in_specs=[
            row_tiles(rows.shape, tile),
            whole_block((1, width)),
            whole_block(weight.shape),
            whole_block((1, KV_RANK)),
        ],
        out_specs=tuple(row_tiles(out.shape, tile) for out in outs),
        compiler_params=pltpu.CompilerParams(vmem_limit_bytes=LESS_VMEM),
        cost_estimate=SMALL,
    )(rows, gain[None], weight, latent_gain[None])


def key_values(packed_ref, expand_ref, cosine, sine, keys_ref, values_ref):
    expanded = matmul(packed_ref[:, :KV_RANK], expand_ref[...]).astype(BF)
    rope = packed_ref[:, KV_RANK : KV_RANK + ROPE]
    turned = (
        rope.astype(F32) * cosine + matmul(rope, places(BF, ROPE, 0, True)) * sine
    ).astype(BF)
    for head in range(2):
        at = head * (NOPE + VDIM)
        keys_ref[head, :, :NOPE] = expanded[:, at : at + NOPE]
        keys_ref[head, :, NOPE:] = turned
        values_ref[head] = expanded[:, at + NOPE : at + NOPE + VDIM]


def own_heads_body(
    normed_ref, query_weight_ref, packed_ref, expand_ref, cosine_ref, sine_ref,
    queries_ref, keys_ref, values_ref,
):
    cosine, sine = cosine_ref[...], sine_ref[...]
    flat = matmul(normed_ref[...], query_weight_ref[...]).astype(BF)
    for head in range(2):
        queries_ref[head, :, :NOPE] = flat[:, head * NOPE : (head + 1) * NOPE]
        ropes = flat[:, 2 * NOPE :]
        queries_ref[head, :, NOPE:] = (
            matmul(ropes, places(BF, 2 * ROPE, head, False)) * cosine
            + matmul(ropes, places(BF, 2 * ROPE, head, True)) * sine
        ).astype(BF)
    key_values(packed_ref, expand_ref, cosine, sine, keys_ref, values_ref)


def other_heads_body(packed_ref, expand_ref, cosine_ref, sine_ref, keys_ref, values_ref):
    key_values(packed_ref, expand_ref, cosine_ref[...], sine_ref[...], keys_ref, values_ref)


def row_tiles(shape, tile):
    if len(shape) == 2:
        return pl.BlockSpec((tile, shape[1]), lambda i: (i, 0))
    return pl.BlockSpec((shape[0], tile, shape[2]), lambda i: (0, i, 0))


def whole_block(shape):
    return pl.BlockSpec(shape, lambda i: (0,) * len(shape))


def heads_of(packed, expand_own, tables, normed=None, query_own=None):
    rows, tile = packed.shape[0], 256
    keys = jax.ShapeDtypeStruct((2, rows, NOPE + ROPE), BF)
    values = jax.ShapeDtypeStruct((2, rows, VDIM), BF)
    outs = (keys, values) if normed is None else (keys, keys, values)
    args, specs = [packed, expand_own, *tables], []
    specs = [
        row_tiles(packed.shape, tile),
        whole_block(expand_own.shape),
        row_tiles(tables[0].shape, tile),
        row_tiles(tables[1].shape, tile),
    ]
    if normed is not None:
        args = [normed, query_own] + args
        specs = [row_tiles(normed.shape, tile), whole_block((normed.shape[1], QUERY))] + specs
    return pl.pallas_call(
        other_heads_body if normed is None else own_heads_body,
        grid=(rows // tile,),
        out_shape=outs,
        in_specs=specs,
        out_specs=tuple(row_tiles(out.shape, tile) for out in outs),
        compiler_params=pltpu.CompilerParams(vmem_limit_bytes=LESS_VMEM),
        cost_estimate=SMALL,
    )(*args)


def back_rows_body(
    at_ref, nope_ref, rope_ref, pair_ref, pair_other_ref, key_rope_ref, key_rope_other_ref,
    cosine_ref, sine_ref, cosine_other_ref, sine_other_ref, query_weight_ref, expand_ref,
    flat_ref, part_ref, kept_ref, given_ref, terms_ref,
):
    swap = places(F32, ROPE, 0, True)

    def turned_back(values, cosine, sine):
        swapped = jnp.dot(
            values, swap, precision=lax.Precision.HIGHEST, preferred_element_type=F32
        )
        return (values * cosine - swapped * sine).astype(BF)

    cosine, sine = cosine_ref[...], sine_ref[...]
    flat_ref[:, : 2 * NOPE] = nope_ref[...]
    for head in range(2):
        at = 2 * NOPE + head * ROPE
        flat_ref[:, at : at + ROPE] = turned_back(rope_ref[head], cosine, sine)
    part_ref[...] = contract_cols(flat_ref[...], query_weight_ref[...]).astype(BF)
    rows = nope_ref.shape[0] // 2
    core = at_ref[1]
    for i, (pairs, ropes, cosine, sine) in enumerate(
        (
            (pair_ref, key_rope_ref, cosine, sine),
            (pair_other_ref, key_rope_other_ref, cosine_other_ref[...], sine_other_ref[...]),
        )
    ):
        terms = contract_cols(pairs[...], expand_ref[...]).astype(BF)
        rope = (
            turned_back(ropes[0], cosine, sine).astype(F32)
            + turned_back(ropes[1], cosine, sine).astype(F32)
        ).astype(BF)
        for c in range(2):
            terms_ref[c, :, :KV_RANK] = terms[c * rows : (c + 1) * rows]
            terms_ref[c, :, KV_RANK : KV_RANK + ROPE] = rope[c * rows : (c + 1) * rows]
            terms_ref[c, :, KV_RANK + ROPE :] = jnp.zeros((rows, PACKED - KV_RANK - ROPE), BF)
        place = pl.ds(at_ref[0] if i == 0 else 1 - at_ref[0], 1)
        kept_ref[place] = terms_ref[pl.ds(core, 1)]
        given_ref[place] = terms_ref[pl.ds(1 - core, 1)]


def back_rows(at, grads, tables, query_own, expand_own):
    nope, rope, pair, pair_other, key_rope, key_rope_other = grads
    rows, tile = nope.shape[0], 256
    args = [nope, rope, pair, pair_other, key_rope, key_rope_other, *tables]
    terms = jax.ShapeDtypeStruct((8, tile // 2, PACKED), BF)
    terms_spec = pl.BlockSpec((2, tile // 2, PACKED), lambda i: (i, 0, 0))
    outs = (
        jax.ShapeDtypeStruct((rows, QUERY), BF),
        jax.ShapeDtypeStruct((rows, query_own.shape[0]), BF),
    )
    return pl.pallas_call(
        back_rows_body,
        grid=(rows // tile,),
        out_shape=outs + (terms, terms),
        in_specs=[pl.BlockSpec(memory_space=pltpu.SMEM)]
        + [row_tiles(arg.shape, tile) for arg in args]
        + [whole_block((query_own.shape[0], QUERY)), whole_block(expand_own.shape)],
        out_specs=tuple(row_tiles(out.shape, tile) for out in outs) + (terms_spec, terms_spec),
        scratch_shapes=[pltpu.VMEM((2, tile // 2, PACKED), BF)],
        compiler_params=pltpu.CompilerParams(vmem_limit_bytes=VMEM_BYTES),
        cost_estimate=SMALL,
    )(at, *args, query_own, expand_own)


def scores_of(query, keys, own, other_first, t, block):
    scores = contract_cols(query, keys) * (NOPE + ROPE) ** (-0.5)
    count = scores.shape[0]
    row = lax.broadcasted_iota(jnp.int32, scores.shape, 0)
    col = lax.broadcasted_iota(jnp.int32, scores.shape, 1)
    if own:
        reach = jnp.where(t < block, count, 0)
    else:
        reach = jnp.where((t < block) | other_first, count, -count)
    return jnp.where(col <= row + reach, scores, -1e30)


def attend_body(
    at_ref, query_ref, key_ref, key_other_ref, value_ref, value_other_ref, out_ref, lse_ref, scores_ref
):
    count = query_ref.shape[1]
    block = pl.program_id(1)
    query = query_ref[0]
    other_first = at_ref[0] == 1
    sets = ((key_ref, value_ref, True, 0), (key_other_ref, value_other_ref, False, count))

    def score(t, top):
        at = pl.ds(pl.multiple_of(t * count, count), count)
        for keys, _, own, place in sets:
            scores = scores_of(query, keys[0, at, :], own, other_first, t, block)
            scores_ref[:, pl.ds(pl.multiple_of(2 * t * count + place, count), count)] = scores
            top = jnp.maximum(top, jnp.max(scores, axis=-1, keepdims=True))
        return top

    top = lax.fori_loop(0, block + 1, score, jnp.full((count, 1), -1e30, F32))

    def weigh(t, carry):
        row_total, summed = carry
        at = pl.ds(pl.multiple_of(t * count, count), count)
        for _, values, _, place in sets:
            scores = scores_ref[:, pl.ds(pl.multiple_of(2 * t * count + place, count), count)]
            exponent = jnp.exp(scores - top)
            row_total = row_total + jnp.sum(exponent, axis=-1, keepdims=True)
            summed = summed + matmul(exponent.astype(BF), values[0, at, :])
        return row_total, summed

    row_total, summed = lax.fori_loop(
        0, block + 1, weigh, (jnp.zeros((count, 1), F32), jnp.zeros((count, VDIM), F32))
    )
    out_ref[...] = (summed / row_total).astype(BF)
    lse_ref[0] = top + jnp.log(row_total)


def attend(xl_at, queries, keys, keys_other, values, values_other):
    heads, rows, depth = queries.shape
    count = rows // 4
    key_spec = pl.BlockSpec((1, rows, depth), lambda h, j: (h, 0, 0))
    value_spec = pl.BlockSpec((1, rows, VDIM), lambda h, j: (h, 0, 0))
    return pl.pallas_call(
        attend_body,
        grid=(heads, 4),
        out_shape=(
            jax.ShapeDtypeStruct((rows, heads * VDIM), BF),
            jax.ShapeDtypeStruct((heads, rows, 1), F32),
        ),
        in_specs=[
            pl.BlockSpec(memory_space=pltpu.SMEM),
            pl.BlockSpec((1, count, depth), lambda h, j: (h, j, 0)),
            key_spec,
            key_spec,
            value_spec,
            value_spec,
        ],
        out_specs=(
            pl.BlockSpec((count, VDIM), lambda h, j: (j, h)),
            pl.BlockSpec((1, count, 1), lambda h, j: (h, j, 0)),
        ),
        scratch_shapes=[pltpu.VMEM((count, 2 * rows), F32)],
        compiler_params=pltpu.CompilerParams(vmem_limit_bytes=LESS_VMEM),
        cost_estimate=SMALL,
    )(xl_at.reshape(1), queries, keys, keys_other, values, values_other)


def attend_back_body(
    at_ref, query_ref, key_ref, key_other_ref, value_ref, value_other_ref, grad_ref, lse_ref,
    nope_ref, rope_ref, pair_ref, pair_other_ref, key_rope_ref, key_rope_other_ref,
    probs_ref, grad_probs_ref, key_sum, key_other_sum, value_sum, value_other_sum,
):
    count = query_ref.shape[1]
    block = pl.program_id(1)
    query, grad = query_ref[0], grad_ref[...]
    other_first = at_ref[0] == 1
    scale = (NOPE + ROPE) ** (-0.5)
    sets = (
        (key_ref, value_ref, key_sum, value_sum, True, 0),
        (key_other_ref, value_other_ref, key_other_sum, value_other_sum, False, count),
    )

    @pl.when(block == 0)
    def _():
        for _, _, keys_to, values_to, _, _ in sets:
            keys_to[...] = jnp.zeros_like(keys_to)
            values_to[...] = jnp.zeros_like(values_to)

    def score(t, centered):
        at = pl.ds(pl.multiple_of(t * count, count), count)
        for keys, values, _, _, own, place in sets:
            to = pl.ds(pl.multiple_of(2 * t * count + place, count), count)
            scores = scores_of(query, keys[0, at, :], own, other_first, t, block)
            probs = jnp.exp(scores - lse_ref[0])
            grad_probs = contract_cols(grad, values[0, at, :])
            probs_ref[:, to] = probs
            grad_probs_ref[:, to] = grad_probs
            centered = centered + jnp.sum(probs * grad_probs, axis=-1, keepdims=True)
        return centered

    centered = lax.fori_loop(0, block + 1, score, jnp.zeros((count, 1), F32))

    def give(t, summed):
        at = pl.ds(pl.multiple_of(t * count, count), count)
        for keys, _, keys_to, values_to, _, place in sets:
            to = pl.ds(pl.multiple_of(2 * t * count + place, count), count)
            probs = probs_ref[:, to]
            grad_scores = (probs * (grad_probs_ref[:, to] - centered)).astype(BF)
            keys_to[at, :] += contract_rows(grad_scores, query)
            values_to[at, :] += contract_rows(probs.astype(BF), grad)
            summed = summed + matmul(grad_scores, keys[0, at, :])
        return summed

    grad_query = scale * lax.fori_loop(0, block + 1, give, jnp.zeros(query.shape, F32))
    nope_ref[...] = grad_query[:, :NOPE].astype(BF)
    rope_ref[0] = grad_query[:, NOPE:]

    @pl.when(block == 3)
    def _():
        for keys_from, values_from, to, rope_to in (
            (key_sum, value_sum, pair_ref, key_rope_ref),
            (key_other_sum, value_other_sum, pair_other_ref, key_rope_other_ref),
        ):
            to[:, :NOPE] = (scale * keys_from[:, :NOPE]).astype(BF)
            to[:, NOPE:] = values_from[...].astype(BF)
            rope_to[0] = scale * keys_from[:, NOPE:]


def attend_back(xl_at, queries, keys, keys_other, values, values_other, grads, lse):
    heads, rows, depth = queries.shape
    count = rows // 4
    key_spec = pl.BlockSpec((1, rows, depth), lambda h, j: (h, 0, 0))
    value_spec = pl.BlockSpec((1, rows, VDIM), lambda h, j: (h, 0, 0))
    pair = jax.ShapeDtypeStruct((rows, heads * (NOPE + VDIM)), BF)
    rope = jax.ShapeDtypeStruct((heads, rows, ROPE), F32)
    pair_spec = pl.BlockSpec((rows, NOPE + VDIM), lambda h, j: (0, h))
    rope_spec = pl.BlockSpec((1, rows, ROPE), lambda h, j: (h, 0, 0))
    return pl.pallas_call(
        attend_back_body,
        grid=(heads, 4),
        out_shape=(
            jax.ShapeDtypeStruct((rows, heads * NOPE), BF),
            rope,
            pair,
            pair,
            rope,
            rope,
        ),
        in_specs=[
            pl.BlockSpec(memory_space=pltpu.SMEM),
            pl.BlockSpec((1, count, depth), lambda h, j: (h, j, 0)),
            key_spec,
            key_spec,
            value_spec,
            value_spec,
            pl.BlockSpec((count, VDIM), lambda h, j: (j, h)),
            pl.BlockSpec((1, count, 1), lambda h, j: (h, j, 0)),
        ],
        out_specs=(
            pl.BlockSpec((count, NOPE), lambda h, j: (j, h)),
            pl.BlockSpec((1, count, ROPE), lambda h, j: (h, j, 0)),
            pair_spec,
            pair_spec,
            rope_spec,
            rope_spec,
        ),
        scratch_shapes=[pltpu.VMEM((count, 2 * rows), F32)] * 2
        + [pltpu.VMEM((rows, depth), F32)] * 2
        + [pltpu.VMEM((rows, VDIM), F32)] * 2,
        compiler_params=pltpu.CompilerParams(vmem_limit_bytes=VMEM_BYTES),
        cost_estimate=SMALL,
    )(xl_at.reshape(1), queries, keys, keys_other, values, values_other, grads, lse)


def group_columns(weight):
    rows, width = weight.shape[0], weight.shape[1] // 16
    return weight.reshape(rows, 4, 2, 2, width).transpose(1, 3, 0, 2, 4).reshape(8, rows, 2, width)


def ungroup_columns(parts):
    rows, width = parts.shape[1], parts.shape[3]
    return parts.reshape(4, 2, rows, 2, width).transpose(2, 0, 3, 1, 4).reshape(rows, 16 * width)


def spread_groups(parts):
    rows, width = parts.shape[1:]
    blocks = jnp.broadcast_to(
        parts.reshape(4, 1, 2, 1, 1, rows, width), (4, 2, 2, 4, 2, rows, width)
    )
    return blocks.reshape(128 * rows, width)


def to_replicas(rows):
    count, width = rows.shape
    blocks = jnp.broadcast_to(rows[None], (16, count, width)).reshape(16 * count, width)
    return lax.all_to_all(blocks, XYX, split_axis=0, concat_axis=0, tiled=True)


def in_row_order(rows):
    width = rows.shape[-1]
    blocks = rows.reshape(2, 8, 4, 2, 16, width).transpose(2, 0, 3, 1, 4, 5)
    return blocks.reshape(-1, width)


def exchange_all(blocks):
    return lax.all_to_all(blocks, ALL, split_axis=0, concat_axis=0, tiled=True)


def tie(*values):
    return lax.optimization_barrier(values)


def halves(gate, up, down):
    turned = down.T
    units = gate.shape[1]
    first = [part[:, :HALF] for part in (gate, up, turned)]
    second = [part[:, units - HALF :] for part in (gate, up, turned)]
    repeated = 2 * HALF - units
    keep = lax.broadcasted_iota(jnp.int32, second[0].shape, 1) >= repeated
    second = [jnp.where(keep, second[0], 0), jnp.where(keep, second[1], 0), second[2]]
    return jnp.concatenate(first, axis=-1), jnp.concatenate(second, axis=-1)


def meet(values, turn):
    pairs = [(2 * c + xh, 2 * (xh ^ turn) + c) for c in range(2) for xh in range(2)]
    pairs = [(source, target) for source, target in pairs if source != target]
    return lax.ppermute(values, ("c", "xh"), pairs)


def part(values, turn):
    pairs = [(2 * c + xh, 2 * xh + (c ^ turn)) for c in range(2) for xh in range(2)]
    pairs = [(source, target) for source, target in pairs if source != target]
    return lax.ppermute(values, ("c", "xh"), pairs)


def total(*terms):
    return sum(term.astype(F32) for term in terms).astype(BF)


def expert_body(at_ref, *refs):
    pieces, (own_ref, other_ref) = refs[:8], refs[8:10]
    own_out, other_out, own_kept, other_kept = refs[10:14]
    weights, sem = refs[14:]
    copies = [
        pltpu.make_async_copy(
            pieces[i], weights.at[pl.ds(pl.multiple_of(at_ref[i] * 256, 256), 256)], sem.at[i]
        )
        for i in range(8)
    ]
    for copy in copies:
        copy.start()
    for copy in copies:
        copy.wait()
    width = own_ref.shape[1] // 2
    for given, result, kept in (
        (own_ref, own_out, own_kept),
        (other_ref, other_out, other_kept),
    ):

        @pl.loop(0, HALF // 256)
        def _(n, given=given, kept=kept):
            def columns(k):
                return pl.ds(pl.multiple_of(k * HALF + n * 256, 256), 256)

            rows, grads = given[:, :width], given[:, width:]
            pre = matmul(rows, weights[:, columns(0)])
            lin = matmul(rows, weights[:, columns(1)])
            grad = matmul(grads, weights[:, columns(2)])
            sigmoid = jax.nn.sigmoid(pre)
            silu = pre * sigmoid
            kept[:, columns(0)] = (grad * lin * sigmoid * (1.0 + pre * (1.0 - sigmoid))).astype(BF)
            kept[:, columns(1)] = (grad * silu).astype(BF)
            kept[:, columns(2)] = (silu * lin).astype(BF)

        @pl.loop(0, width // 256)
        def _(f, kept=kept, result=result):
            block = weights[pl.ds(pl.multiple_of(f * 256, 256), 256), :]
            out = contract_cols(kept[:, 2 * HALF :], block[:, 2 * HALF :])
            back = contract_cols(kept[:, : 2 * HALF], block[:, : 2 * HALF])
            result[:, pl.ds(pl.multiple_of(f * 256, 256), 256)] = out.astype(BF)
            result[:, pl.ds(pl.multiple_of(width + f * 256, 256), 256)] = back.astype(BF)


def expert_rows(order, pieces, own, other):
    rows, width = own.shape
    kept = jax.ShapeDtypeStruct((rows, 3 * HALF), BF)
    result = jax.ShapeDtypeStruct((rows, width), BF)
    whole = pl.BlockSpec(memory_space=pltpu.VMEM)
    return pl.pallas_call(
        expert_body,
        out_shape=(result, result, kept, kept),
        in_specs=[pl.BlockSpec(memory_space=pltpu.SMEM)]
        + [pl.BlockSpec(memory_space=pl.ANY)] * 8
        + [whole] * 2,
        out_specs=(whole,) * 4,
        scratch_shapes=[pltpu.VMEM((width // 2, 3 * HALF), BF), pltpu.SemaphoreType.DMA((8,))],
        compiler_params=pltpu.CompilerParams(vmem_limit_bytes=VMEM_BYTES),
        cost_estimate=SMALL,
    )(order, *pieces, own, other)


def expert_grad_body(
    at_ref, own_rows, own_grads, other_rows, other_grads, own_kept, other_kept, *outs
):
    first = contract_rows(own_rows[...], own_kept[:, : 2 * HALF]) + contract_rows(
        other_rows[...], other_kept[:, : 2 * HALF]
    )
    last = contract_rows(own_grads[...], own_kept[:, 2 * HALF :]) + contract_rows(
        other_grads[...], other_kept[:, 2 * HALF :]
    )
    for i, out in enumerate(outs):

        @pl.when(pl.program_id(0) == i)
        def _(out=out):
            out[:, : 2 * HALF] = first.astype(BF)
            out[:, 2 * HALF :] = last.astype(BF)


def expert_grads(order, own, other, own_kept, other_kept):
    rows, width = own.shape
    blocks, count = width // 512, order.shape[0]
    row_spec = pl.BlockSpec((rows, 256), lambda i, at: (0, at[i]))
    grad_spec = pl.BlockSpec((rows, 256), lambda i, at: (0, blocks + at[i]))
    kept_spec = pl.BlockSpec((rows, 3 * HALF), lambda i, at: (0, 0))
    return pl.pallas_call(
        expert_grad_body,
        out_shape=(jax.ShapeDtypeStruct((256, 3 * HALF), BF),) * count,
        grid_spec=pltpu.PrefetchScalarGridSpec(
            num_scalar_prefetch=1,
            grid=(count,),
            in_specs=[row_spec, grad_spec, row_spec, grad_spec, kept_spec, kept_spec],
            out_specs=(pl.BlockSpec((256, 3 * HALF), lambda i, at: (0, 0)),) * count,
        ),
        compiler_params=pltpu.CompilerParams(vmem_limit_bytes=LESS_VMEM),
        cost_estimate=SMALL,
    )(order, own, own, other, other, own_kept, other_kept)


def shared_body(rows_ref, grads_ref, gate_up_ref, down_ref, back_ref, out_ref, kept_ref):
    both = matmul(rows_ref[...], gate_up_ref[...])
    pre, lin = both[:, :UNIT_PAD], both[:, UNIT_PAD:]
    grad = contract_cols(grads_ref[...], down_ref[...])
    sigmoid = jax.nn.sigmoid(pre)
    silu = pre * sigmoid
    hidden = (silu * lin).astype(BF)
    grad_pre = (grad * lin * sigmoid * (1.0 + pre * (1.0 - sigmoid))).astype(BF)
    grad_lin = (grad * silu).astype(BF)
    kept_ref[:, :UNIT_PAD] = grad_pre
    kept_ref[:, UNIT_PAD : 2 * UNIT_PAD] = grad_lin
    kept_ref[:, 2 * UNIT_PAD :] = hidden
    back_ref[...] = contract_cols(kept_ref[:, : 2 * UNIT_PAD], gate_up_ref[...]).astype(BF)
    out_ref[...] = matmul(hidden, down_ref[...]).astype(BF)


def shared_rows(rows, grads, gate_up, down):
    count, width = rows.shape
    tile = 256
    row_spec = pl.BlockSpec((tile, width), lambda i: (i, 0))
    return pl.pallas_call(
        shared_body,
        grid=(count // tile,),
        out_shape=(
            jax.ShapeDtypeStruct((count, width), BF),
            jax.ShapeDtypeStruct((count, width), BF),
            jax.ShapeDtypeStruct((count, 3 * UNIT_PAD), BF),
        ),
        in_specs=[
            row_spec,
            row_spec,
            pl.BlockSpec(gate_up.shape, lambda i: (0, 0)),
            pl.BlockSpec(down.shape, lambda i: (0, 0)),
        ],
        out_specs=(row_spec, row_spec, pl.BlockSpec((tile, 3 * UNIT_PAD), lambda i: (i, 0))),
        compiler_params=pltpu.CompilerParams(vmem_limit_bytes=VMEM_BYTES),
        cost_estimate=SMALL,
    )(rows, grads, gate_up, down)


def last_rows_body(
    one_ref, two_ref, first_terms_ref, second_terms_ref, latent_ref, logits_ref, extra_ref, out_ref
):
    column = lax.broadcasted_iota(jnp.int32, logits_ref.shape, 1)
    latent = contract_rows(one_ref[...], latent_ref[...])
    out_ref[:, :KV_RANK] = latent[:, :KV_RANK].astype(BF)
    last = latent[:, KV_RANK:] + contract_rows(two_ref[...], logits_ref[...])
    last = last + contract_rows(first_terms_ref[...], (column == 80).astype(BF))
    last = last + contract_rows(second_terms_ref[...], (column == 81).astype(BF))
    out_ref[:, KV_RANK:] = (last + extra_ref[...]).astype(BF)


def last_rows(normed_one, normed_two, first_terms, second_terms, latent, logits, extra):
    rows, length = normed_one.shape
    tile = 256
    column_spec = pl.BlockSpec((rows, tile), lambda i: (0, i))
    out = jax.ShapeDtypeStruct((length, PACKED), BF)
    return pl.pallas_call(
        last_rows_body,
        grid=(length // tile,),
        out_shape=out,
        in_specs=[column_spec] * 4
        + [whole_block(latent.shape), whole_block(logits.shape), row_tiles(extra.shape, tile)],
        out_specs=row_tiles(out.shape, tile),
        compiler_params=pltpu.CompilerParams(vmem_limit_bytes=VMEM_BYTES),
        cost_estimate=SMALL,
    )(normed_one, normed_two, first_terms, second_terms, latent, logits, extra)


def head_sums_body(in_ref, query_ref, expand_ref):
    for z in range(4):
        for c in range(2):

            def add(f, summed, z=z, c=c):
                for xl in range(2):
                    summed = summed + in_ref[((z * 2 + xl) * 2 + c) * 8 + f].astype(F32)
                return summed

            summed = lax.fori_loop(0, 8, add, jnp.zeros(in_ref.shape[1:], F32))
            for xl in range(2):
                part = z * 4 + xl * 2 + c
                at = part * (NOPE + ROPE)
                query_ref[:, at : at + NOPE] = summed[:, xl * NOPE : (xl + 1) * NOPE]
                rope_at = 2 * NOPE + xl * ROPE
                query_ref[:, at + NOPE : at + NOPE + ROPE] = summed[:, rope_at : rope_at + ROPE]
                for half in range(2):
                    j = 2 * xl + half
                    at = part * 256 + half * 128
                    expand_ref[:, at : at + 128] = summed[4 * j : 4 * j + 4, 384:]


def head_sums(arrived):
    whole = pl.BlockSpec(memory_space=pltpu.VMEM)
    return pl.pallas_call(
        head_sums_body,
        out_shape=(
            jax.ShapeDtypeStruct((16, 16 * (NOPE + ROPE)), F32),
            jax.ShapeDtypeStruct((4, 4096), F32),
        ),
        in_specs=[whole],
        out_specs=(whole,) * 2,
        compiler_params=pltpu.CompilerParams(vmem_limit_bytes=LESS_VMEM),
        cost_estimate=SMALL,
    )(arrived)


def query_grads_body(normed_ref, flat_ref, out_ref):
    out_ref[...] = contract_rows(normed_ref[...], flat_ref[...]).astype(BF)


def query_grads(normed, flat):
    tile = 256
    return pl.pallas_call(
        query_grads_body,
        grid=(normed.shape[1] // tile,),
        out_shape=jax.ShapeDtypeStruct((normed.shape[1], flat.shape[1]), BF),
        in_specs=[
            pl.BlockSpec((normed.shape[0], tile), lambda i: (0, i)),
            whole_block(flat.shape),
        ],
        out_specs=pl.BlockSpec((tile, flat.shape[1]), lambda i: (i, 0)),
        compiler_params=pltpu.CompilerParams(vmem_limit_bytes=LESS_VMEM),
        cost_estimate=SMALL,
    )(normed, flat)


def unit_columns_out(weight):
    runs = group_columns(weight).reshape(8, 16, 16, -1)
    return jnp.pad(runs, ((0, 0), (0, 0), (0, 0), (0, 24 - runs.shape[-1]))).reshape(8, 16, -1)


def unit_columns_back(parts, units):
    runs = parts.reshape(8, 16, 16, 24)[..., : units // 8]
    return ungroup_columns(runs.reshape(8, 16, 2, units))


def on_device(
    tokens,
    positions,
    routes,
    first_gain,
    query_weight,
    latent_weight,
    latent_gain,
    expand_weight,
    output_weight,
    second_gain,
    router_weight,
    shared_gate,
    shared_up,
    shared_down,
    expert_gate,
    expert_up,
    expert_down,
    cotangent,
):
    z_at, xl_at, c_at = lax.axis_index("z"), lax.axis_index("xl"), lax.axis_index("c")
    y_at, xh_at = lax.axis_index("y"), lax.axis_index("xh")
    own_tokens = tokens[0]
    row_count, width = own_tokens.shape
    length = 16 * row_count
    expert_count = router_weight.shape[1]
    units = shared_gate.shape[1] // 16

    half_tokens = lax.all_gather(own_tokens, ZC, axis=0, tiled=True)

    cosine_table, sine_table = rotary_tables(positions[0])

    def half_rows(table, at):
        return lax.dynamic_index_in_dim(
            table.reshape(4, 2, 2 * row_count, -1), at, axis=1, keepdims=False
        ).reshape(length // 2, -1)

    wide = wide_tables(cosine_table, sine_table)
    tables = [half_rows(table, at) for at in (xl_at, 1 - xl_at) for table in wide]
    route_ids = routes[0]
    route_hot = (
        route_ids[:, :, None] == jnp.arange(expert_count, dtype=jnp.int32)[None, None, :]
    ).astype(F32)
    grad_result = cotangent[0]
    grad_float = grad_result.astype(F32)
    route_total = row_count * TOP
    flat_hot = route_hot.reshape(route_total, expert_count).astype(BF)
    earlier = (
        jnp.arange(route_total, dtype=jnp.int32)[:, None]
        > jnp.arange(route_total, dtype=jnp.int32)[None, :]
    ).astype(BF)
    before = matmul(earlier, flat_hot)
    slot_place = jnp.sum(before * flat_hot.astype(F32), axis=-1).astype(jnp.int32)
    slot_ids = (route_ids.reshape(route_total) * SLOTS + slot_place).reshape(row_count, TOP)
    slot_match = (
        jnp.arange(expert_count * SLOTS, dtype=jnp.int32)[:, None, None] == slot_ids[None, :, :]
    )
    dispatch = jnp.any(slot_match, axis=-1).astype(BF)
    picks = (
        jnp.arange(expert_count * SLOTS, dtype=jnp.int32)[None, :]
        == slot_ids.T.reshape(-1)[:, None]
    ).astype(BF)
    dispatch_grads = matmul(dispatch, grad_result)
    first_half, second_half = halves(expert_gate[0], expert_up[0], expert_down[0])
    met = [jnp.where((xh_at ^ turn) == 0, first_half, second_half) for turn in range(2)]

    query_group = group_columns(query_weight)
    expand_group = group_columns(expand_weight).reshape(8, 16, 128)
    head_group = jnp.concatenate(
        [
            query_group[..., :NOPE].reshape(8, 16, 2 * NOPE),
            query_group[..., NOPE:].reshape(8, 16, 2 * ROPE),
            expand_group,
        ],
        axis=-1,
    )
    common = jnp.concatenate(
        [
            latent_weight,
            router_weight,
            first_gain[:, None],
            second_gain[:, None],
            jnp.pad(latent_gain, (0, 12))[:, None],
            jnp.zeros((16, 45), BF),
        ],
        axis=-1,
    )
    unit_group = jnp.concatenate(
        [unit_columns_out(weight) for weight in (shared_gate, shared_up)], axis=-1
    ).reshape(128, 768)
    common_in = exchange_all(jnp.broadcast_to(common[None], (128, 16, 640)).reshape(2048, 640))
    met_own = met[0]
    met = [meet(met[turn], turn) for turn in range(2)]
    met[0] = jnp.where(c_at == xh_at, met_own, met[0])
    head_group = spread_groups(head_group)
    unit_group, common_in = tie(unit_group, common_in)
    unit_group = lax.all_to_all(unit_group, ZC, split_axis=0, concat_axis=0, tiled=True)

    half_tokens, common_in, met, head_group = tie(half_tokens, common_in, met, head_group)
    above, below = [None, None], [None, None]
    above[0], below[0] = shift(met[0], "y", 1), shift(met[0], "y", -1)
    gains = common_in[:, 512:640].T.astype(F32)
    first_norm_gain, second_norm_gain = gains[80], gains[81]
    latent_norm_gain = gains[82].reshape(128, 16)[:, :4].reshape(KV_RANK)
    latent_full = common_in[:, :576]
    router_full = common_in[:, 576:592]
    latent_mine, normed_half, latent_half = front(
        half_tokens, first_norm_gain, latent_full, latent_norm_gain
    )
    latent_mine, head_group = tie(latent_mine, head_group)
    latent_other = shift(latent_mine, "xl", 1)
    head_in = exchange_all(head_group)

    down_count = shared_down.shape[0]
    down_rows = jnp.concatenate(
        [output_weight, jnp.pad(shared_down, ((0, 24 - down_count), (0, 0)))], axis=0
    )
    latent_other, latent_mine, normed_half, head_in, met, down_rows, grad_result, tables, unit_group, above[0], below[0], dispatch, dispatch_grads, picks = tie(
        latent_other, latent_mine, normed_half, head_in, met, down_rows, grad_result, tables, unit_group, above[0], below[0], dispatch, dispatch_grads, picks
    )
    down_all = to_replicas(down_rows).reshape(16, 40, width)
    seq_grad = lax.all_gather(grad_result, ZC, axis=0, tiled=True)
    expand_own = head_in[:, 384:].reshape(KV_RANK, 512)
    queries, keys, values = heads_of(latent_mine, expand_own, tables[:2], normed_half, head_in)

    keys_other, values_other = heads_of(latent_other, expand_own, tables[2:])

    attended_own, row_lse = attend(xl_at, queries, keys, keys_other, values, values_other)

    attended_own, row_lse, seq_grad, unit_group, down_all = tie(
        attended_own, row_lse, seq_grad, unit_group, down_all
    )
    output_own = down_all[:, :16].reshape(256, width)
    attended_part = matmul(attended_own, output_own).astype(BF)
    attended_sum = lax.psum_scatter(attended_part, ZC, scatter_dimension=0, tiled=True)
    unit_columns = to_replicas(unit_group)

    attended_sum, unit_columns, met[1], above[0], down_all = tie(
        attended_sum, unit_columns, met[1], above[0], down_all
    )
    unit_columns = in_row_order(unit_columns)
    sdown_own = down_all[:, 16:].reshape(UNIT_PAD, width)
    above[1], below[1] = shift(met[1], "y", 1), shift(met[1], "y", -1)
    input_rows = own_tokens.astype(F32)
    middle = input_rows + attended_sum.astype(F32)
    scaled_two, inverse_two = normalize(middle)
    normed_two = (scaled_two * second_norm_gain).astype(BF)
    seq_normed_two = lax.all_gather(normed_two, ZC, axis=0, tiled=True)
    logits = matmul(normed_two, router_full)
    chosen = jnp.sum(route_hot * logits[:, None, :], axis=-1)
    gate_values = jax.nn.softmax(chosen, axis=-1)
    slot_gates = jnp.sum(jnp.where(slot_match, gate_values[None], 0.0), axis=(1, 2))
    sent_rows = matmul(dispatch, normed_two).astype(BF)
    sent_grads = (dispatch_grads * slot_gates[:, None]).astype(BF)
    sent = jnp.concatenate([sent_rows, sent_grads], axis=-1)

    sent, seq_normed_two, above[0], above[1], below[1], unit_columns, sdown_own = tie(
        sent, seq_normed_two, above[0], above[1], below[1], unit_columns, sdown_own
    )
    own_in = lax.all_to_all(sent, ZXX, split_axis=0, concat_axis=0, tiled=True)
    far = [shift(above[0], "y", 1), shift(below[1], "y", -1)]

    back_part, out_part, shared_kept = shared_rows(
        seq_normed_two, seq_grad, unit_columns, sdown_own
    )
    grad_units = contract_rows(seq_normed_two, shared_kept[:, : 2 * UNIT_PAD]).astype(BF)
    grad_sdown = contract_rows(shared_kept[:, 2 * UNIT_PAD :], seq_grad).astype(BF)

    own_in, back_part, out_part, grad_units, grad_sdown, far = tie(
        own_in, back_part, out_part, grad_units, grad_sdown, far
    )
    shared_back = lax.psum_scatter(back_part, ZC, scatter_dimension=0, tiled=True)
    units_in = exchange_all(grad_units)
    other_in = shift(own_in, "c", 1)
    pieces = [met[0], met[1], above[0], above[1], far[0], far[1], below[0], below[1]]
    order = jnp.stack(
        [((y_at + step) % 4) * 2 + (c_at ^ turn) for step in range(4) for turn in range(2)]
    ).astype(jnp.int32)
    own_back, other_back, own_kept, other_kept = expert_rows(order, pieces, own_in, other_in)
    other_back, units_in = tie(other_back, units_in)
    back = total(own_back, shift(other_back, "c", 1))

    back, own_kept, other_kept = tie(back, own_kept, other_kept)
    returned = lax.all_to_all(back, ZXX, split_axis=0, concat_axis=0, tiled=True)
    blocks = [None] * 8
    blocks[4], blocks[5] = expert_grads(
        jnp.stack([order[4], order[5]]), own_in, other_in, own_kept, other_kept
    )
    from_below = shift(blocks[4], "y", -1)
    from_above = shift(blocks[5], "y", 1)
    own_kept, blocks[4] = tie(own_kept, blocks[4])
    blocks[3], blocks[6] = expert_grads(
        jnp.stack([order[3], order[6]]), own_in, other_in, own_kept, other_kept
    )
    upward_free, downward_free = shift(blocks[3], "y", -1), shift(blocks[6], "y", 1)
    own_kept, blocks[3] = tie(own_kept, blocks[3])
    blocks[2], blocks[7], blocks[0], blocks[1] = expert_grads(
        jnp.stack([order[2], order[7], order[0], order[1]]), own_in, other_in, own_kept, other_kept
    )

    returned, shared_back, from_below, from_above, blocks[0], blocks[2], blocks[7] = tie(
        returned, shared_back, from_below, from_above, blocks[0], blocks[2], blocks[7]
    )
    upward_last = total(blocks[2], from_below)
    downward_last = total(blocks[7], from_above)
    picked = matmul(picks, returned).reshape(TOP, row_count, 2 * width)
    picked_out = picked[:, :, :width]
    grad_normed_routed = picked[0, :, width:] + picked[1, :, width:]
    routed = gate_values[:, :1] * picked_out[0] + gate_values[:, 1:] * picked_out[1]
    grad_gates = jnp.stack(
        [jnp.sum(grad_float * picked_out[k], axis=-1) for k in range(TOP)], axis=-1
    )
    centered_gates = grad_gates - jnp.sum(gate_values * grad_gates, axis=-1, keepdims=True)
    grad_chosen = gate_values * centered_gates
    grad_logits = jnp.sum(route_hot * grad_chosen[:, :, None], axis=1).astype(BF)
    grad_normed_router = contract_cols(grad_logits, router_full)
    grad_normed_two = shared_back.astype(F32) + grad_normed_routed + grad_normed_router
    grad_from_norm, gain_second_terms = norm_back(
        grad_normed_two, second_norm_gain, scaled_two, inverse_two
    )
    grad_middle = grad_float + grad_from_norm

    grad_middle, upward_last, downward_last, upward_free, downward_free, units_in = tie(
        grad_middle, upward_last, downward_last, upward_free, downward_free, units_in
    )
    seq_grad_middle = lax.all_gather(grad_middle.astype(BF), ZC, axis=0, tiled=True)
    upward_last = shift(upward_last, "y", -1)
    downward_last = shift(downward_last, "y", 1)

    units_sum = jnp.sum(
        units_in.reshape(4, 2, 2, 8, 16, 2 * UNIT_PAD).astype(F32), axis=(1, 3)
    ).reshape(8, 16, 2 * UNIT_PAD)
    unit_results = [
        unit_columns_back(units_sum[..., :UNIT_PAD], units),
        unit_columns_back(units_sum[..., UNIT_PAD:], units),
    ]
    seq_grad_middle, upward_last, downward_last, out_part, unit_results = tie(
        seq_grad_middle, upward_last, downward_last, out_part, unit_results
    )
    shared_out = lax.psum_scatter(out_part, ZC, scatter_dimension=0, tiled=True)
    grad_output = contract_rows(attended_own, seq_grad_middle).astype(BF)
    down_grads = jnp.concatenate(
        [grad_output.reshape(16, 16, width), grad_sdown.reshape(16, 24, width)], axis=1
    ).reshape(640, width)
    down_in = lax.all_to_all(down_grads, XYX, split_axis=0, concat_axis=0, tiled=True)
    grad_heads = contract_cols(seq_grad_middle, output_own).astype(BF)
    attention_grads = attend_back(
        xl_at, queries, keys, keys_other, values, values_other, grad_heads, row_lse
    )

    attention_grads, shared_out = tie(attention_grads, shared_out)
    _, _, pair, pair_other, _, _ = attention_grads
    grad_query_flat, normed_part, latent_kept, latent_given = back_rows(
        jnp.stack([xl_at, c_at]), attention_grads, tables, head_in, expand_own
    )
    grad_query_flat, normed_part, latent_kept, latent_given, down_in = tie(
        grad_query_flat, normed_part, latent_kept, latent_given, down_in
    )
    latent_sums = total(latent_kept, shift(latent_given, "c", 1)).reshape(8 * row_count, -1)
    latent_in = lax.all_to_all(latent_sums, ("z", "xl"), split_axis=0, concat_axis=0, tiled=True)
    grad_normed_part = lax.psum_scatter(normed_part, ZC, scatter_dimension=0, tiled=True)
    grad_expand = (
        contract_rows(latent_mine[:, :KV_RANK], pair)
        + contract_rows(latent_other[:, :KV_RANK], pair_other)
    ).astype(BF)
    grad_query_w = query_grads(normed_half, grad_query_flat)
    grad_expand = grad_expand.reshape(128, 4, 4, 128).transpose(0, 2, 1, 3).reshape(length, 128)
    head_grads = jnp.concatenate([grad_query_w, grad_expand], axis=-1)

    summed = [
        total(blocks[0], upward_last, downward_free),
        total(blocks[1], upward_free, downward_last),
    ]
    latent_in, head_grads, summed = tie(latent_in, head_grads, summed)
    heads_in = exchange_all(head_grads)
    parted = [part(summed[turn], turn) for turn in range(2)]
    grad_latent_sum = jnp.sum(latent_in.reshape(8, row_count, -1).astype(F32), axis=0)
    scaled_one, inverse_one = normalize(input_rows)
    normed_one = (scaled_one * first_norm_gain).astype(BF)
    latent_own = lax.dynamic_slice_in_dim(
        latent_half, (z_at * 2 + c_at) * row_count, row_count, axis=0
    )
    scaled_latent, inverse_latent = normalize(latent_own[:, :KV_RANK])
    grad_latent, gain_latent_terms = norm_back(
        grad_latent_sum[:, :KV_RANK], latent_norm_gain, scaled_latent, inverse_latent
    )
    grad_latent_all = jnp.concatenate(
        [grad_latent, grad_latent_sum[:, KV_RANK : KV_RANK + ROPE]], axis=-1
    ).astype(BF)
    grad_normed_one = grad_normed_part.astype(F32) + contract_cols(grad_latent_all, latent_full)
    grad_input_norm, gain_first_terms = norm_back(
        grad_normed_one, first_norm_gain, scaled_one, inverse_one
    )

    gain_latent = jnp.sum(gain_latent_terms, axis=0).reshape(128, 1, 4)
    final_out = last_rows(
        normed_one,
        normed_two,
        gain_first_terms.astype(BF),
        gain_second_terms.astype(BF),
        jnp.pad(grad_latent_all, ((0, 0), (0, PACKED - KV_RANK - ROPE))),
        jnp.pad(grad_logits, ((0, 0), (64, 48))),
        jnp.pad(gain_latent, ((0, 0), (0, 15), (96, 28))).reshape(length, 128),
    )

    down_in = down_in.reshape(16, 40, width)
    grad_output_w = jnp.sum(down_in[:, :16].astype(F32), axis=0)
    grad_sdown_w = jnp.sum(down_in[:, 16 : 16 + down_count].astype(F32), axis=0)
    final_out, heads_in, parted, grad_output_w, grad_sdown_w = tie(
        final_out, heads_in, parted, grad_output_w, grad_sdown_w
    )
    parted[0] = jnp.where(c_at == xh_at, summed[0], parted[0])
    final_in = exchange_all(final_out)

    grad_inputs = grad_middle + grad_input_norm
    result = middle + shared_out.astype(F32) + routed
    first_half = jnp.where(xh_at == 0, parted[0], parted[1])
    second_half = jnp.where(xh_at == 0, parted[1], parted[0])
    repeated = 2 * HALF - expert_gate.shape[2]
    expert_results = [
        jnp.concatenate(
            [
                first_half[:, k * HALF : (k + 1) * HALF],
                second_half[:, k * HALF + repeated : (k + 1) * HALF],
            ],
            axis=-1,
        ).astype(F32)
        for k in range(3)
    ]
    expert_results[2] = expert_results[2].T
    grad_query_weight, grad_expand_weight = head_sums(heads_in.reshape(128, 16, 512))
    beside = (grad_inputs, result, grad_query_weight, grad_expand_weight)
    final_in, beside = tie(final_in, beside)
    grad_inputs, result, grad_query_weight, grad_expand_weight = beside
    common_sum = jnp.sum(final_in.reshape(128, 16, PACKED).astype(F32), axis=0)
    return (
        result.astype(BF)[None],
        grad_inputs.astype(BF)[None],
        common_sum[:, 592],
        grad_query_weight,
        common_sum[:, :576],
        common_sum[0, 608:612],
        grad_expand_weight,
        grad_output_w,
        common_sum[:, 593],
        common_sum[:, 576:592],
        unit_results[0],
        unit_results[1],
        grad_sdown_w,
        expert_results[0][None],
        expert_results[1][None],
        expert_results[2][None],
    )


def solution(mesh):
    fine = Mesh(mesh.devices.reshape(4, 2, 2, 4, 2), ALL)
    return jax.shard_map(
        on_device,
        mesh=fine,
        in_specs=(
            P(FSDP, SEQ, None),
            P(FSDP, None),
            P(FSDP, SEQ, None),
            P(ALL),
            P(ALL, None),
            P(ALL, None),
            P(ALL),
            P(ALL, None),
            P(ALL, None),
            P(ALL),
            P(ALL, None),
            P(ALL, None),
            P(ALL, None),
            P(ALL, None),
            P(SEQ, FSDP, None),
            P(SEQ, FSDP, None),
            P(SEQ, None, FSDP),
            P(FSDP, SEQ, None),
        ),
        out_specs=(
            P(FSDP, SEQ, None),
            P(FSDP, SEQ, None),
            P(ALL),
            P(ALL, None),
            P(ALL, None),
            P(ALL),
            P(ALL, None),
            P(ALL, None),
            P(ALL),
            P(ALL, None),
            P(ALL, None),
            P(ALL, None),
            P(ALL, None),
            P(SEQ, FSDP, None),
            P(SEQ, FSDP, None),
            P(SEQ, None, FSDP),
        ),
        check_vma=False,
    )
```

```python
import math

import jax
import jax.numpy as jnp
from jax import lax
from jax.experimental import pallas as pl
from jax.experimental.pallas import tpu as pltpu
from jax.sharding import Mesh
from jax.sharding import PartitionSpec as P

NOPE = 128
ROPE = 64
VDIM = 128
KV_RANK = 512
TOP = 2
UNIT_PAD = 384
SLOTS = 24
HALF = 768
PACKED = 640
QUERY = 384
EPSILON = 1e-06
VMEM_BYTES = 60 * 2**20
LESS_VMEM = 40 * 2**20
SMALL = pl.CostEstimate(flops=1024, bytes_accessed=2**18, transcendentals=0)

SEQ = ("z", "xl", "c")
FSDP = ("y", "xh")
ZC = ("z", "c")
XYX = ("xl", "y", "xh")
ZXX = ("z", "xl", "xh")
ALL = ("z", "xl", "c", "y", "xh")
BF = jnp.bfloat16
F32 = jnp.float32


def matmul(left_side, right_side):
    return jnp.dot(left_side, right_side, preferred_element_type=F32)


def contract_rows(left_side, right_side):
    return lax.dot_general(
        left_side, right_side, (((0,), (0,)), ((), ())), preferred_element_type=F32
    )


def contract_cols(left_side, right_side):
    return lax.dot_general(
        left_side, right_side, (((1,), (1,)), ((), ())), preferred_element_type=F32
    )


def normalize(values):
    inverse = lax.rsqrt(jnp.mean(values * values, axis=-1, keepdims=True) + EPSILON)
    return (values * inverse, inverse)


def norm_back(grad_normed, gain_vector, scaled, inverse):
    grad_scaled = grad_normed * gain_vector
    grad_input = inverse * (
        grad_scaled - scaled * jnp.mean(grad_scaled * scaled, axis=-1, keepdims=True)
    )
    return (grad_input, grad_normed * scaled)


def rotary_tables(position_list):
    half_rope = ROPE // 2
    frequency = jnp.exp(-(2.0 * jnp.arange(half_rope, dtype=F32) / ROPE) * math.log(10000.0))
    angles = position_list.astype(F32)[:, None] * frequency[None, :]
    return (jnp.cos(angles), jnp.sin(angles))


def wide_tables(cosine_table, sine_table):
    return (
        jnp.concatenate([cosine_table, cosine_table], axis=-1),
        jnp.concatenate([-sine_table, sine_table], axis=-1),
    )


def places(kind, rows, head, swapped):
    row = lax.broadcasted_iota(jnp.int32, (rows, ROPE), 0)
    col = lax.broadcasted_iota(jnp.int32, (rows, ROPE), 1)
    if swapped:
        col = (col + ROPE // 2) % ROPE
    return (row == col + head * ROPE).astype(kind)


def shift(values, axis_name, step):
    count = lax.axis_size(axis_name)
    return lax.ppermute(values, axis_name, [((i + step) % count, i) for i in range(count)])


def front_body(
    rows_ref, gain_ref, weight_ref, latent_gain_ref, packed_ref, normed_ref, latent_ref
):
    scaled, _ = normalize(rows_ref[...].astype(F32))
    normed = (scaled * gain_ref[...]).astype(BF)
    latent = matmul(normed, weight_ref[...])
    normed_ref[...] = normed
    latent_ref[...] = latent
    scaled_latent, _ = normalize(latent[:, :KV_RANK])
    packed_ref[:, :KV_RANK] = (scaled_latent * latent_gain_ref[...]).astype(BF)
    packed_ref[:, KV_RANK : KV_RANK + ROPE] = latent[:, KV_RANK:].astype(BF)
    packed_ref[:, KV_RANK + ROPE :] = jnp.zeros((latent.shape[0], PACKED - KV_RANK - ROPE), BF)


def front(rows, gain, weight, latent_gain):
    count, width = rows.shape
    columns, tile = weight.shape[1], 256
    outs = (
        jax.ShapeDtypeStruct((count, PACKED), BF),
        jax.ShapeDtypeStruct((count, width), BF),
        jax.ShapeDtypeStruct((count, columns), F32),
    )
    return pl.pallas_call(
        front_body,
        grid=(count // tile,),
        out_shape=outs,
        in_specs=[
            row_tiles(rows.shape, tile),
            whole_block((1, width)),
            whole_block(weight.shape),
            whole_block((1, KV_RANK)),
        ],
        out_specs=tuple(row_tiles(out.shape, tile) for out in outs),
        compiler_params=pltpu.CompilerParams(vmem_limit_bytes=LESS_VMEM),
        cost_estimate=SMALL,
    )(rows, gain[None], weight, latent_gain[None])


def key_values(packed_ref, expand_ref, cosine, sine, keys_ref, values_ref):
    expanded = matmul(packed_ref[:, :KV_RANK], expand_ref[...]).astype(BF)
    rope = packed_ref[:, KV_RANK : KV_RANK + ROPE]
    turned = (
        rope.astype(F32) * cosine + matmul(rope, places(BF, ROPE, 0, True)) * sine
    ).astype(BF)
    for head in range(2):
        at = head * (NOPE + VDIM)
        keys_ref[head, :, :NOPE] = expanded[:, at : at + NOPE]
        keys_ref[head, :, NOPE:] = turned
        values_ref[head] = expanded[:, at + NOPE : at + NOPE + VDIM]


def own_heads_body(
    normed_ref, query_weight_ref, packed_ref, expand_ref, cosine_ref, sine_ref,
    queries_ref, keys_ref, values_ref,
):
    cosine, sine = cosine_ref[...], sine_ref[...]
    flat = matmul(normed_ref[...], query_weight_ref[...]).astype(BF)
    for head in range(2):
        queries_ref[head, :, :NOPE] = flat[:, head * NOPE : (head + 1) * NOPE]
        ropes = flat[:, 2 * NOPE :]
        queries_ref[head, :, NOPE:] = (
            matmul(ropes, places(BF, 2 * ROPE, head, False)) * cosine
            + matmul(ropes, places(BF, 2 * ROPE, head, True)) * sine
        ).astype(BF)
    key_values(packed_ref, expand_ref, cosine, sine, keys_ref, values_ref)


def other_heads_body(packed_ref, expand_ref, cosine_ref, sine_ref, keys_ref, values_ref):
    key_values(packed_ref, expand_ref, cosine_ref[...], sine_ref[...], keys_ref, values_ref)


def row_tiles(shape, tile):
    if len(shape) == 2:
        return pl.BlockSpec((tile, shape[1]), lambda i: (i, 0))
    return pl.BlockSpec((shape[0], tile, shape[2]), lambda i: (0, i, 0))


def whole_block(shape):
    return pl.BlockSpec(shape, lambda i: (0,) * len(shape))


def heads_of(packed, expand_own, tables, normed=None, query_own=None):
    rows, tile = packed.shape[0], 256
    keys = jax.ShapeDtypeStruct((2, rows, NOPE + ROPE), BF)
    values = jax.ShapeDtypeStruct((2, rows, VDIM), BF)
    outs = (keys, values) if normed is None else (keys, keys, values)
    args, specs = [packed, expand_own, *tables], []
    specs = [
        row_tiles(packed.shape, tile),
        whole_block(expand_own.shape),
        row_tiles(tables[0].shape, tile),
        row_tiles(tables[1].shape, tile),
    ]
    if normed is not None:
        args = [normed, query_own] + args
        specs = [row_tiles(normed.shape, tile), whole_block((normed.shape[1], QUERY))] + specs
    return pl.pallas_call(
        other_heads_body if normed is None else own_heads_body,
        grid=(rows // tile,),
        out_shape=outs,
        in_specs=specs,
        out_specs=tuple(row_tiles(out.shape, tile) for out in outs),
        compiler_params=pltpu.CompilerParams(vmem_limit_bytes=LESS_VMEM),
        cost_estimate=SMALL,
    )(*args)


def back_rows_body(
    at_ref, nope_ref, rope_ref, pair_ref, pair_other_ref, key_rope_ref, key_rope_other_ref,
    cosine_ref, sine_ref, cosine_other_ref, sine_other_ref, query_weight_ref, expand_ref,
    flat_ref, part_ref, kept_ref, given_ref, terms_ref,
):
    swap = places(F32, ROPE, 0, True)

    def turned_back(values, cosine, sine):
        swapped = jnp.dot(
            values, swap, precision=lax.Precision.HIGHEST, preferred_element_type=F32
        )
        return (values * cosine - swapped * sine).astype(BF)

    cosine, sine = cosine_ref[...], sine_ref[...]
    flat_ref[:, : 2 * NOPE] = nope_ref[...]
    for head in range(2):
        at = 2 * NOPE + head * ROPE
        flat_ref[:, at : at + ROPE] = turned_back(rope_ref[head], cosine, sine)
    part_ref[...] = contract_cols(flat_ref[...], query_weight_ref[...]).astype(BF)
    rows = nope_ref.shape[0] // 2
    core = at_ref[1]
    for i, (pairs, ropes, cosine, sine) in enumerate(
        (
            (pair_ref, key_rope_ref, cosine, sine),
            (pair_other_ref, key_rope_other_ref, cosine_other_ref[...], sine_other_ref[...]),
        )
    ):
        terms = contract_cols(pairs[...], expand_ref[...]).astype(BF)
        rope = (
            turned_back(ropes[0], cosine, sine).astype(F32)
            + turned_back(ropes[1], cosine, sine).astype(F32)
        ).astype(BF)
        for c in range(2):
            terms_ref[c, :, :KV_RANK] = terms[c * rows : (c + 1) * rows]
            terms_ref[c, :, KV_RANK : KV_RANK + ROPE] = rope[c * rows : (c + 1) * rows]
            terms_ref[c, :, KV_RANK + ROPE :] = jnp.zeros((rows, PACKED - KV_RANK - ROPE), BF)
        place = pl.ds(at_ref[0] if i == 0 else 1 - at_ref[0], 1)
        kept_ref[place] = terms_ref[pl.ds(core, 1)]
        given_ref[place] = terms_ref[pl.ds(1 - core, 1)]


def back_rows(at, grads, tables, query_own, expand_own):
    nope, rope, pair, pair_other, key_rope, key_rope_other = grads
    rows, tile = nope.shape[0], 256
    args = [nope, rope, pair, pair_other, key_rope, key_rope_other, *tables]
    terms = jax.ShapeDtypeStruct((8, tile // 2, PACKED), BF)
    terms_spec = pl.BlockSpec((2, tile // 2, PACKED), lambda i: (i, 0, 0))
    outs = (
        jax.ShapeDtypeStruct((rows, QUERY), BF),
        jax.ShapeDtypeStruct((rows, query_own.shape[0]), BF),
    )
    return pl.pallas_call(
        back_rows_body,
        grid=(rows // tile,),
        out_shape=outs + (terms, terms),
        in_specs=[pl.BlockSpec(memory_space=pltpu.SMEM)]
        + [row_tiles(arg.shape, tile) for arg in args]
        + [whole_block((query_own.shape[0], QUERY)), whole_block(expand_own.shape)],
        out_specs=tuple(row_tiles(out.shape, tile) for out in outs) + (terms_spec, terms_spec),
        scratch_shapes=[pltpu.VMEM((2, tile // 2, PACKED), BF)],
        compiler_params=pltpu.CompilerParams(vmem_limit_bytes=VMEM_BYTES),
        cost_estimate=SMALL,
    )(at, *args, query_own, expand_own)


def scores_of(query, keys, own, other_first, t, block):
    scores = contract_cols(query, keys) * (NOPE + ROPE) ** (-0.5)
    count = scores.shape[0]
    row = lax.broadcasted_iota(jnp.int32, scores.shape, 0)
    col = lax.broadcasted_iota(jnp.int32, scores.shape, 1)
    if own:
        reach = jnp.where(t < block, count, 0)
    else:
        reach = jnp.where((t < block) | other_first, count, -count)
    return jnp.where(col <= row + reach, scores, -1e30)


def attend_body(
    at_ref, query_ref, key_ref, key_other_ref, value_ref, value_other_ref, out_ref, lse_ref, scores_ref
):
    count = query_ref.shape[1]
    block = pl.program_id(1)
    query = query_ref[0]
    other_first = at_ref[0] == 1
    sets = ((key_ref, value_ref, True, 0), (key_other_ref, value_other_ref, False, count))

    def score(t, top):
        at = pl.ds(pl.multiple_of(t * count, count), count)
        for keys, _, own, place in sets:
            scores = scores_of(query, keys[0, at, :], own, other_first, t, block)
            scores_ref[:, pl.ds(pl.multiple_of(2 * t * count + place, count), count)] = scores
            top = jnp.maximum(top, jnp.max(scores, axis=-1, keepdims=True))
        return top

    top = lax.fori_loop(0, block + 1, score, jnp.full((count, 1), -1e30, F32))

    def weigh(t, carry):
        row_total, summed = carry
        at = pl.ds(pl.multiple_of(t * count, count), count)
        for _, values, _, place in sets:
            scores = scores_ref[:, pl.ds(pl.multiple_of(2 * t * count + place, count), count)]
            exponent = jnp.exp(scores - top)
            row_total = row_total + jnp.sum(exponent, axis=-1, keepdims=True)
            summed = summed + matmul(exponent.astype(BF), values[0, at, :])
        return row_total, summed

    row_total, summed = lax.fori_loop(
        0, block + 1, weigh, (jnp.zeros((count, 1), F32), jnp.zeros((count, VDIM), F32))
    )
    out_ref[...] = (summed / row_total).astype(BF)
    lse_ref[0] = top + jnp.log(row_total)


def attend(xl_at, queries, keys, keys_other, values, values_other):
    heads, rows, depth = queries.shape
    count = rows // 4
    key_spec = pl.BlockSpec((1, rows, depth), lambda h, j: (h, 0, 0))
    value_spec = pl.BlockSpec((1, rows, VDIM), lambda h, j: (h, 0, 0))
    return pl.pallas_call(
        attend_body,
        grid=(heads, 4),
        out_shape=(
            jax.ShapeDtypeStruct((rows, heads * VDIM), BF),
            jax.ShapeDtypeStruct((heads, rows, 1), F32),
        ),
        in_specs=[
            pl.BlockSpec(memory_space=pltpu.SMEM),
            pl.BlockSpec((1, count, depth), lambda h, j: (h, j, 0)),
            key_spec,
            key_spec,
            value_spec,
            value_spec,
        ],
        out_specs=(
            pl.BlockSpec((count, VDIM), lambda h, j: (j, h)),
            pl.BlockSpec((1, count, 1), lambda h, j: (h, j, 0)),
        ),
        scratch_shapes=[pltpu.VMEM((count, 2 * rows), F32)],
        compiler_params=pltpu.CompilerParams(vmem_limit_bytes=LESS_VMEM),
        cost_estimate=SMALL,
    )(xl_at.reshape(1), queries, keys, keys_other, values, values_other)


def attend_back_body(
    at_ref, query_ref, key_ref, key_other_ref, value_ref, value_other_ref, grad_ref, lse_ref,
    nope_ref, rope_ref, pair_ref, pair_other_ref, key_rope_ref, key_rope_other_ref,
    probs_ref, grad_probs_ref, key_sum, key_other_sum, value_sum, value_other_sum,
):
    count = query_ref.shape[1]
    block = pl.program_id(1)
    query, grad = query_ref[0], grad_ref[...]
    other_first = at_ref[0] == 1
    scale = (NOPE + ROPE) ** (-0.5)
    sets = (
        (key_ref, value_ref, key_sum, value_sum, True, 0),
        (key_other_ref, value_other_ref, key_other_sum, value_other_sum, False, count),
    )

    @pl.when(block == 0)
    def _():
        for _, _, keys_to, values_to, _, _ in sets:
            keys_to[...] = jnp.zeros_like(keys_to)
            values_to[...] = jnp.zeros_like(values_to)

    def score(t, centered):
        at = pl.ds(pl.multiple_of(t * count, count), count)
        for keys, values, _, _, own, place in sets:
            to = pl.ds(pl.multiple_of(2 * t * count + place, count), count)
            scores = scores_of(query, keys[0, at, :], own, other_first, t, block)
            probs = jnp.exp(scores - lse_ref[0])
            grad_probs = contract_cols(grad, values[0, at, :])
            probs_ref[:, to] = probs
            grad_probs_ref[:, to] = grad_probs
            centered = centered + jnp.sum(probs * grad_probs, axis=-1, keepdims=True)
        return centered

    centered = lax.fori_loop(0, block + 1, score, jnp.zeros((count, 1), F32))

    def give(t, summed):
        at = pl.ds(pl.multiple_of(t * count, count), count)
        for keys, _, keys_to, values_to, _, place in sets:
            to = pl.ds(pl.multiple_of(2 * t * count + place, count), count)
            probs = probs_ref[:, to]
            grad_scores = (probs * (grad_probs_ref[:, to] - centered)).astype(BF)
            keys_to[at, :] += contract_rows(grad_scores, query)
            values_to[at, :] += contract_rows(probs.astype(BF), grad)
            summed = summed + matmul(grad_scores, keys[0, at, :])
        return summed

    grad_query = scale * lax.fori_loop(0, block + 1, give, jnp.zeros(query.shape, F32))
    nope_ref[...] = grad_query[:, :NOPE].astype(BF)
    rope_ref[0] = grad_query[:, NOPE:]

    @pl.when(block == 3)
    def _():
        for keys_from, values_from, to, rope_to in (
            (key_sum, value_sum, pair_ref, key_rope_ref),
            (key_other_sum, value_other_sum, pair_other_ref, key_rope_other_ref),
        ):
            to[:, :NOPE] = (scale * keys_from[:, :NOPE]).astype(BF)
            to[:, NOPE:] = values_from[...].astype(BF)
            rope_to[0] = scale * keys_from[:, NOPE:]


def attend_back(xl_at, queries, keys, keys_other, values, values_other, grads, lse):
    heads, rows, depth = queries.shape
    count = rows // 4
    key_spec = pl.BlockSpec((1, rows, depth), lambda h, j: (h, 0, 0))
    value_spec = pl.BlockSpec((1, rows, VDIM), lambda h, j: (h, 0, 0))
    pair = jax.ShapeDtypeStruct((rows, heads * (NOPE + VDIM)), BF)
    rope = jax.ShapeDtypeStruct((heads, rows, ROPE), F32)
    pair_spec = pl.BlockSpec((rows, NOPE + VDIM), lambda h, j: (0, h))
    rope_spec = pl.BlockSpec((1, rows, ROPE), lambda h, j: (h, 0, 0))
    return pl.pallas_call(
        attend_back_body,
        grid=(heads, 4),
        out_shape=(
            jax.ShapeDtypeStruct((rows, heads * NOPE), BF),
            rope,
            pair,
            pair,
            rope,
            rope,
        ),
        in_specs=[
            pl.BlockSpec(memory_space=pltpu.SMEM),
            pl.BlockSpec((1, count, depth), lambda h, j: (h, j, 0)),
            key_spec,
            key_spec,
            value_spec,
            value_spec,
            pl.BlockSpec((count, VDIM), lambda h, j: (j, h)),
            pl.BlockSpec((1, count, 1), lambda h, j: (h, j, 0)),
        ],
        out_specs=(
            pl.BlockSpec((count, NOPE), lambda h, j: (j, h)),
            pl.BlockSpec((1, count, ROPE), lambda h, j: (h, j, 0)),
            pair_spec,
            pair_spec,
            rope_spec,
            rope_spec,
        ),
        scratch_shapes=[pltpu.VMEM((count, 2 * rows), F32)] * 2
        + [pltpu.VMEM((rows, depth), F32)] * 2
        + [pltpu.VMEM((rows, VDIM), F32)] * 2,
        compiler_params=pltpu.CompilerParams(vmem_limit_bytes=VMEM_BYTES),
        cost_estimate=SMALL,
    )(xl_at.reshape(1), queries, keys, keys_other, values, values_other, grads, lse)


def group_columns(weight):
    rows, width = weight.shape[0], weight.shape[1] // 16
    return weight.reshape(rows, 4, 2, 2, width).transpose(1, 3, 0, 2, 4).reshape(8, rows, 2, width)


def ungroup_columns(parts):
    rows, width = parts.shape[1], parts.shape[3]
    return parts.reshape(4, 2, rows, 2, width).transpose(2, 0, 3, 1, 4).reshape(rows, 16 * width)


def spread_groups(parts):
    rows, width = parts.shape[1:]
    blocks = jnp.broadcast_to(
        parts.reshape(4, 1, 2, 1, 1, rows, width), (4, 2, 2, 4, 2, rows, width)
    )
    return blocks.reshape(128 * rows, width)


def to_replicas(rows):
    count, width = rows.shape
    blocks = jnp.broadcast_to(rows[None], (16, count, width)).reshape(16 * count, width)
    return lax.all_to_all(blocks, XYX, split_axis=0, concat_axis=0, tiled=True)


def in_row_order(rows):
    width = rows.shape[-1]
    blocks = rows.reshape(2, 8, 4, 2, 16, width).transpose(2, 0, 3, 1, 4, 5)
    return blocks.reshape(-1, width)


def exchange_all(blocks):
    return lax.all_to_all(blocks, ALL, split_axis=0, concat_axis=0, tiled=True)


def tie(*values):
    return lax.optimization_barrier(values)


def halves(gate, up, down):
    turned = down.T
    units = gate.shape[1]
    first = [part[:, :HALF] for part in (gate, up, turned)]
    second = [part[:, units - HALF :] for part in (gate, up, turned)]
    repeated = 2 * HALF - units
    keep = lax.broadcasted_iota(jnp.int32, second[0].shape, 1) >= repeated
    second = [jnp.where(keep, second[0], 0), jnp.where(keep, second[1], 0), second[2]]
    return jnp.concatenate(first, axis=-1), jnp.concatenate(second, axis=-1)


def meet(values, turn):
    pairs = [(2 * c + xh, 2 * (xh ^ turn) + c) for c in range(2) for xh in range(2)]
    pairs = [(source, target) for source, target in pairs if source != target]
    return lax.ppermute(values, ("c", "xh"), pairs)


def part(values, turn):
    pairs = [(2 * c + xh, 2 * xh + (c ^ turn)) for c in range(2) for xh in range(2)]
    pairs = [(source, target) for source, target in pairs if source != target]
    return lax.ppermute(values, ("c", "xh"), pairs)


def total(*terms):
    return sum(term.astype(F32) for term in terms).astype(BF)


def expert_body(at_ref, *refs):
    pieces, (own_ref, other_ref) = refs[:8], refs[8:10]
    own_out, other_out, own_kept, other_kept = refs[10:14]
    weights, sem = refs[14:]
    copies = [
        pltpu.make_async_copy(
            pieces[i], weights.at[pl.ds(pl.multiple_of(at_ref[i] * 256, 256), 256)], sem.at[i]
        )
        for i in range(8)
    ]
    for copy in copies:
        copy.start()
    for copy in copies:
        copy.wait()
    width = own_ref.shape[1] // 2
    for given, result, kept in (
        (own_ref, own_out, own_kept),
        (other_ref, other_out, other_kept),
    ):

        @pl.loop(0, HALF // 256)
        def _(n, given=given, kept=kept):
            def columns(k):
                return pl.ds(pl.multiple_of(k * HALF + n * 256, 256), 256)

            rows, grads = given[:, :width], given[:, width:]
            pre = matmul(rows, weights[:, columns(0)])
            lin = matmul(rows, weights[:, columns(1)])
            grad = matmul(grads, weights[:, columns(2)])
            sigmoid = jax.nn.sigmoid(pre)
            silu = pre * sigmoid
            kept[:, columns(0)] = (grad * lin * sigmoid * (1.0 + pre * (1.0 - sigmoid))).astype(BF)
            kept[:, columns(1)] = (grad * silu).astype(BF)
            kept[:, columns(2)] = (silu * lin).astype(BF)

        @pl.loop(0, width // 256)
        def _(f, kept=kept, result=result):
            block = weights[pl.ds(pl.multiple_of(f * 256, 256), 256), :]
            out = contract_cols(kept[:, 2 * HALF :], block[:, 2 * HALF :])
            back = contract_cols(kept[:, : 2 * HALF], block[:, : 2 * HALF])
            result[:, pl.ds(pl.multiple_of(f * 256, 256), 256)] = out.astype(BF)
            result[:, pl.ds(pl.multiple_of(width + f * 256, 256), 256)] = back.astype(BF)


def expert_rows(order, pieces, own, other):
    rows, width = own.shape
    kept = jax.ShapeDtypeStruct((rows, 3 * HALF), BF)
    result = jax.ShapeDtypeStruct((rows, width), BF)
    whole = pl.BlockSpec(memory_space=pltpu.VMEM)
    return pl.pallas_call(
        expert_body,
        out_shape=(result, result, kept, kept),
        in_specs=[pl.BlockSpec(memory_space=pltpu.SMEM)]
        + [pl.BlockSpec(memory_space=pl.ANY)] * 8
        + [whole] * 2,
        out_specs=(whole,) * 4,
        scratch_shapes=[pltpu.VMEM((width // 2, 3 * HALF), BF), pltpu.SemaphoreType.DMA((8,))],
        compiler_params=pltpu.CompilerParams(vmem_limit_bytes=VMEM_BYTES),
        cost_estimate=SMALL,
    )(order, *pieces, own, other)


def expert_grad_body(
    at_ref, own_rows, own_grads, other_rows, other_grads, own_kept, other_kept, *outs
):
    first = contract_rows(own_rows[...], own_kept[:, : 2 * HALF]) + contract_rows(
        other_rows[...], other_kept[:, : 2 * HALF]
    )
    last = contract_rows(own_grads[...], own_kept[:, 2 * HALF :]) + contract_rows(
        other_grads[...], other_kept[:, 2 * HALF :]
    )
    for i, out in enumerate(outs):

        @pl.when(pl.program_id(0) == i)
        def _(out=out):
            out[:, : 2 * HALF] = first.astype(BF)
            out[:, 2 * HALF :] = last.astype(BF)


def expert_grads(order, own, other, own_kept, other_kept):
    rows, width = own.shape
    blocks, count = width // 512, order.shape[0]
    row_spec = pl.BlockSpec((rows, 256), lambda i, at: (0, at[i]))
    grad_spec = pl.BlockSpec((rows, 256), lambda i, at: (0, blocks + at[i]))
    kept_spec = pl.BlockSpec((rows, 3 * HALF), lambda i, at: (0, 0))
    return pl.pallas_call(
        expert_grad_body,
        out_shape=(jax.ShapeDtypeStruct((256, 3 * HALF), BF),) * count,
        grid_spec=pltpu.PrefetchScalarGridSpec(
            num_scalar_prefetch=1,
            grid=(count,),
            in_specs=[row_spec, grad_spec, row_spec, grad_spec, kept_spec, kept_spec],
            out_specs=(pl.BlockSpec((256, 3 * HALF), lambda i, at: (0, 0)),) * count,
        ),
        compiler_params=pltpu.CompilerParams(vmem_limit_bytes=LESS_VMEM),
        cost_estimate=SMALL,
    )(order, own, own, other, other, own_kept, other_kept)


def shared_body(rows_ref, grads_ref, gate_up_ref, down_ref, back_ref, out_ref, kept_ref):
    both = matmul(rows_ref[...], gate_up_ref[...])
    pre, lin = both[:, :UNIT_PAD], both[:, UNIT_PAD:]
    grad = contract_cols(grads_ref[...], down_ref[...])
    sigmoid = jax.nn.sigmoid(pre)
    silu = pre * sigmoid
    hidden = (silu * lin).astype(BF)
    grad_pre = (grad * lin * sigmoid * (1.0 + pre * (1.0 - sigmoid))).astype(BF)
    grad_lin = (grad * silu).astype(BF)
    kept_ref[:, :UNIT_PAD] = grad_pre
    kept_ref[:, UNIT_PAD : 2 * UNIT_PAD] = grad_lin
    kept_ref[:, 2 * UNIT_PAD :] = hidden
    back_ref[...] = contract_cols(kept_ref[:, : 2 * UNIT_PAD], gate_up_ref[...]).astype(BF)
    out_ref[...] = matmul(hidden, down_ref[...]).astype(BF)


def shared_rows(rows, grads, gate_up, down):
    count, width = rows.shape
    tile = 256
    row_spec = pl.BlockSpec((tile, width), lambda i: (i, 0))
    return pl.pallas_call(
        shared_body,
        grid=(count // tile,),
        out_shape=(
            jax.ShapeDtypeStruct((count, width), BF),
            jax.ShapeDtypeStruct((count, width), BF),
            jax.ShapeDtypeStruct((count, 3 * UNIT_PAD), BF),
        ),
        in_specs=[
            row_spec,
            row_spec,
            pl.BlockSpec(gate_up.shape, lambda i: (0, 0)),
            pl.BlockSpec(down.shape, lambda i: (0, 0)),
        ],
        out_specs=(row_spec, row_spec, pl.BlockSpec((tile, 3 * UNIT_PAD), lambda i: (i, 0))),
        compiler_params=pltpu.CompilerParams(vmem_limit_bytes=VMEM_BYTES),
        cost_estimate=SMALL,
    )(rows, grads, gate_up, down)


def last_rows_body(
    one_ref, two_ref, first_terms_ref, second_terms_ref, latent_ref, logits_ref, extra_ref, out_ref
):
    column = lax.broadcasted_iota(jnp.int32, logits_ref.shape, 1)
    latent = contract_rows(one_ref[...], latent_ref[...])
    out_ref[:, :KV_RANK] = latent[:, :KV_RANK].astype(BF)
    last = latent[:, KV_RANK:] + contract_rows(two_ref[...], logits_ref[...])
    last = last + contract_rows(first_terms_ref[...], (column == 80).astype(BF))
    last = last + contract_rows(second_terms_ref[...], (column == 81).astype(BF))
    out_ref[:, KV_RANK:] = (last + extra_ref[...]).astype(BF)


def last_rows(normed_one, normed_two, first_terms, second_terms, latent, logits, extra):
    rows, length = normed_one.shape
    tile = 256
    column_spec = pl.BlockSpec((rows, tile), lambda i: (0, i))
    out = jax.ShapeDtypeStruct((length, PACKED), BF)
    return pl.pallas_call(
        last_rows_body,
        grid=(length // tile,),
        out_shape=out,
        in_specs=[column_spec] * 4
        + [whole_block(latent.shape), whole_block(logits.shape), row_tiles(extra.shape, tile)],
        out_specs=row_tiles(out.shape, tile),
        compiler_params=pltpu.CompilerParams(vmem_limit_bytes=VMEM_BYTES),
        cost_estimate=SMALL,
    )(normed_one, normed_two, first_terms, second_terms, latent, logits, extra)


def head_sums_body(in_ref, query_ref, expand_ref):
    for z in range(4):
        for c in range(2):

            def add(f, summed, z=z, c=c):
                for xl in range(2):
                    summed = summed + in_ref[((z * 2 + xl) * 2 + c) * 8 + f].astype(F32)
                return summed

            summed = lax.fori_loop(0, 8, add, jnp.zeros(in_ref.shape[1:], F32))
            for xl in range(2):
                part = z * 4 + xl * 2 + c
                at = part * (NOPE + ROPE)
                query_ref[:, at : at + NOPE] = summed[:, xl * NOPE : (xl + 1) * NOPE]
                rope_at = 2 * NOPE + xl * ROPE
                query_ref[:, at + NOPE : at + NOPE + ROPE] = summed[:, rope_at : rope_at + ROPE]
                for half in range(2):
                    j = 2 * xl + half
                    at = part * 256 + half * 128
                    expand_ref[:, at : at + 128] = summed[4 * j : 4 * j + 4, 384:]


def head_sums(arrived):
    whole = pl.BlockSpec(memory_space=pltpu.VMEM)
    return pl.pallas_call(
        head_sums_body,
        out_shape=(
            jax.ShapeDtypeStruct((16, 16 * (NOPE + ROPE)), F32),
            jax.ShapeDtypeStruct((4, 4096), F32),
        ),
        in_specs=[whole],
        out_specs=(whole,) * 2,
        compiler_params=pltpu.CompilerParams(vmem_limit_bytes=LESS_VMEM),
        cost_estimate=SMALL,
    )(arrived)


def query_grads_body(normed_ref, flat_ref, out_ref):
    out_ref[...] = contract_rows(normed_ref[...], flat_ref[...]).astype(BF)


def query_grads(normed, flat):
    tile = 256
    return pl.pallas_call(
        query_grads_body,
        grid=(normed.shape[1] // tile,),
        out_shape=jax.ShapeDtypeStruct((normed.shape[1], flat.shape[1]), BF),
        in_specs=[
            pl.BlockSpec((normed.shape[0], tile), lambda i: (0, i)),
            whole_block(flat.shape),
        ],
        out_specs=pl.BlockSpec((tile, flat.shape[1]), lambda i: (i, 0)),
        compiler_params=pltpu.CompilerParams(vmem_limit_bytes=LESS_VMEM),
        cost_estimate=SMALL,
    )(normed, flat)


def unit_columns_out(weight):
    runs = group_columns(weight).reshape(8, 16, 16, -1)
    return jnp.pad(runs, ((0, 0), (0, 0), (0, 0), (0, 24 - runs.shape[-1]))).reshape(8, 16, -1)


def unit_columns_back(parts, units):
    runs = parts.reshape(8, 16, 16, 24)[..., : units // 8]
    return ungroup_columns(runs.reshape(8, 16, 2, units))


def on_device(
    tokens,
    positions,
    routes,
    first_gain,
    query_weight,
    latent_weight,
    latent_gain,
    expand_weight,
    output_weight,
    second_gain,
    router_weight,
    shared_gate,
    shared_up,
    shared_down,
    expert_gate,
    expert_up,
    expert_down,
    cotangent,
):
    z_at, xl_at, c_at = lax.axis_index("z"), lax.axis_index("xl"), lax.axis_index("c")
    y_at, xh_at = lax.axis_index("y"), lax.axis_index("xh")
    own_tokens = tokens[0]
    row_count, width = own_tokens.shape
    length = 16 * row_count
    expert_count = router_weight.shape[1]
    units = shared_gate.shape[1] // 16

    half_tokens = lax.all_gather(own_tokens, ZC, axis=0, tiled=True)

    cosine_table, sine_table = rotary_tables(positions[0])

    def half_rows(table, at):
        return lax.dynamic_index_in_dim(
            table.reshape(4, 2, 2 * row_count, -1), at, axis=1, keepdims=False
        ).reshape(length // 2, -1)

    wide = wide_tables(cosine_table, sine_table)
    tables = [half_rows(table, at) for at in (xl_at, 1 - xl_at) for table in wide]
    route_ids = routes[0]
    route_hot = (
        route_ids[:, :, None] == jnp.arange(expert_count, dtype=jnp.int32)[None, None, :]
    ).astype(F32)
    grad_result = cotangent[0]
    grad_float = grad_result.astype(F32)
    route_total = row_count * TOP
    flat_hot = route_hot.reshape(route_total, expert_count).astype(BF)
    earlier = (
        jnp.arange(route_total, dtype=jnp.int32)[:, None]
        > jnp.arange(route_total, dtype=jnp.int32)[None, :]
    ).astype(BF)
    before = matmul(earlier, flat_hot)
    slot_place = jnp.sum(before * flat_hot.astype(F32), axis=-1).astype(jnp.int32)
    slot_ids = (route_ids.reshape(route_total) * SLOTS + slot_place).reshape(row_count, TOP)
    slot_match = (
        jnp.arange(expert_count * SLOTS, dtype=jnp.int32)[:, None, None] == slot_ids[None, :, :]
    )
    dispatch = jnp.any(slot_match, axis=-1).astype(BF)
    picks = (
        jnp.arange(expert_count * SLOTS, dtype=jnp.int32)[None, :]
        == slot_ids.T.reshape(-1)[:, None]
    ).astype(BF)
    dispatch_grads = matmul(dispatch, grad_result)
    first_half, second_half = halves(expert_gate[0], expert_up[0], expert_down[0])
    met = [jnp.where((xh_at ^ turn) == 0, first_half, second_half) for turn in range(2)]

    query_group = group_columns(query_weight)
    expand_group = group_columns(expand_weight).reshape(8, 16, 128)
    head_group = jnp.concatenate(
        [
            query_group[..., :NOPE].reshape(8, 16, 2 * NOPE),
            query_group[..., NOPE:].reshape(8, 16, 2 * ROPE),
            expand_group,
        ],
        axis=-1,
    )
    common = jnp.concatenate(
        [
            latent_weight,
            router_weight,
            first_gain[:, None],
            second_gain[:, None],
            jnp.pad(latent_gain, (0, 12))[:, None],
            jnp.zeros((16, 45), BF),
        ],
        axis=-1,
    )
    unit_group = jnp.concatenate(
        [unit_columns_out(weight) for weight in (shared_gate, shared_up)], axis=-1
    ).reshape(128, 768)
    common_in = exchange_all(jnp.broadcast_to(common[None], (128, 16, 640)).reshape(2048, 640))
    met_own = met[0]
    met = [meet(met[turn], turn) for turn in range(2)]
    met[0] = jnp.where(c_at == xh_at, met_own, met[0])
    head_group = spread_groups(head_group)
    unit_group, common_in = tie(unit_group, common_in)
    unit_group = lax.all_to_all(unit_group, ZC, split_axis=0, concat_axis=0, tiled=True)

    half_tokens, common_in, met, head_group = tie(half_tokens, common_in, met, head_group)
    head_in = exchange_all(head_group)
    above, below = [None, None], [None, None]
    above[0], below[0] = shift(met[0], "y", 1), shift(met[0], "y", -1)
    gains = common_in[:, 512:640].T.astype(F32)
    first_norm_gain, second_norm_gain = gains[80], gains[81]
    latent_norm_gain = gains[82].reshape(128, 16)[:, :4].reshape(KV_RANK)
    latent_full = common_in[:, :576]
    router_full = common_in[:, 576:592]
    latent_mine, normed_half, latent_half = front(
        half_tokens, first_norm_gain, latent_full, latent_norm_gain
    )
    latent_other = shift(latent_mine, "xl", 1)

    down_count = shared_down.shape[0]
    down_rows = jnp.concatenate(
        [output_weight, jnp.pad(shared_down, ((0, 24 - down_count), (0, 0)))], axis=0
    )
    latent_other, latent_mine, normed_half, head_in, met, down_rows, grad_result, tables, unit_group, above[0], below[0], dispatch, dispatch_grads, picks = tie(
        latent_other, latent_mine, normed_half, head_in, met, down_rows, grad_result, tables, unit_group, above[0], below[0], dispatch, dispatch_grads, picks
    )
    down_all = to_replicas(down_rows).reshape(16, 40, width)
    seq_grad = lax.all_gather(grad_result, ZC, axis=0, tiled=True)
    expand_own = head_in[:, 384:].reshape(KV_RANK, 512)
    queries, keys, values = heads_of(latent_mine, expand_own, tables[:2], normed_half, head_in)

    keys_other, values_other = heads_of(latent_other, expand_own, tables[2:])

    attended_own, row_lse = attend(xl_at, queries, keys, keys_other, values, values_other)

    attended_own, row_lse, seq_grad, unit_group, down_all = tie(
        attended_own, row_lse, seq_grad, unit_group, down_all
    )
    output_own = down_all[:, :16].reshape(256, width)
    attended_part = matmul(attended_own, output_own).astype(BF)
    attended_sum = lax.psum_scatter(attended_part, ZC, scatter_dimension=0, tiled=True)
    unit_columns = to_replicas(unit_group)

    attended_sum, unit_columns, met[1], above[0], down_all = tie(
        attended_sum, unit_columns, met[1], above[0], down_all
    )
    unit_columns = in_row_order(unit_columns)
    sdown_own = down_all[:, 16:].reshape(UNIT_PAD, width)
    above[1], below[1] = shift(met[1], "y", 1), shift(met[1], "y", -1)
    input_rows = own_tokens.astype(F32)
    middle = input_rows + attended_sum.astype(F32)
    scaled_two, inverse_two = normalize(middle)
    normed_two = (scaled_two * second_norm_gain).astype(BF)
    seq_normed_two = lax.all_gather(normed_two, ZC, axis=0, tiled=True)
    logits = matmul(normed_two, router_full)
    chosen = jnp.sum(route_hot * logits[:, None, :], axis=-1)
    gate_values = jax.nn.softmax(chosen, axis=-1)
    slot_gates = jnp.sum(jnp.where(slot_match, gate_values[None], 0.0), axis=(1, 2))
    sent_rows = matmul(dispatch, normed_two).astype(BF)
    sent_grads = (dispatch_grads * slot_gates[:, None]).astype(BF)
    sent = jnp.concatenate([sent_rows, sent_grads], axis=-1)

    sent, seq_normed_two, above[0], above[1], below[1], unit_columns, sdown_own = tie(
        sent, seq_normed_two, above[0], above[1], below[1], unit_columns, sdown_own
    )
    own_in = lax.all_to_all(sent, ZXX, split_axis=0, concat_axis=0, tiled=True)
    far = [shift(above[0], "y", 1), shift(below[1], "y", -1)]

    back_part, out_part, shared_kept = shared_rows(
        seq_normed_two, seq_grad, unit_columns, sdown_own
    )
    grad_units = contract_rows(seq_normed_two, shared_kept[:, : 2 * UNIT_PAD]).astype(BF)
    grad_sdown = contract_rows(shared_kept[:, 2 * UNIT_PAD :], seq_grad).astype(BF)

    own_in, back_part, out_part, grad_units, grad_sdown, far = tie(
        own_in, back_part, out_part, grad_units, grad_sdown, far
    )
    shared_back = lax.psum_scatter(back_part, ZC, scatter_dimension=0, tiled=True)
    units_in = exchange_all(grad_units)
    other_in = shift(own_in, "c", 1)
    pieces = [met[0], met[1], above[0], above[1], far[0], far[1], below[0], below[1]]
    order = jnp.stack(
        [((y_at + step) % 4) * 2 + (c_at ^ turn) for step in range(4) for turn in range(2)]
    ).astype(jnp.int32)
    own_back, other_back, own_kept, other_kept = expert_rows(order, pieces, own_in, other_in)
    other_back, units_in = tie(other_back, units_in)
    back = total(own_back, shift(other_back, "c", 1))

    back, own_kept, other_kept = tie(back, own_kept, other_kept)
    returned = lax.all_to_all(back, ZXX, split_axis=0, concat_axis=0, tiled=True)
    blocks = [None] * 8
    blocks[4], blocks[5] = expert_grads(
        jnp.stack([order[4], order[5]]), own_in, other_in, own_kept, other_kept
    )
    from_below = shift(blocks[4], "y", -1)
    from_above = shift(blocks[5], "y", 1)
    own_kept, blocks[4] = tie(own_kept, blocks[4])
    blocks[3], blocks[6] = expert_grads(
        jnp.stack([order[3], order[6]]), own_in, other_in, own_kept, other_kept
    )
    upward_free, downward_free = shift(blocks[3], "y", -1), shift(blocks[6], "y", 1)
    own_kept, blocks[3] = tie(own_kept, blocks[3])
    blocks[2], blocks[7], blocks[0], blocks[1] = expert_grads(
        jnp.stack([order[2], order[7], order[0], order[1]]), own_in, other_in, own_kept, other_kept
    )

    returned, shared_back, from_below, from_above, blocks[0], blocks[2], blocks[7] = tie(
        returned, shared_back, from_below, from_above, blocks[0], blocks[2], blocks[7]
    )
    upward_last = total(blocks[2], from_below)
    downward_last = total(blocks[7], from_above)
    picked = matmul(picks, returned).reshape(TOP, row_count, 2 * width)
    picked_out = picked[:, :, :width]
    grad_normed_routed = picked[0, :, width:] + picked[1, :, width:]
    routed = gate_values[:, :1] * picked_out[0] + gate_values[:, 1:] * picked_out[1]
    grad_gates = jnp.stack(
        [jnp.sum(grad_float * picked_out[k], axis=-1) for k in range(TOP)], axis=-1
    )
    centered_gates = grad_gates - jnp.sum(gate_values * grad_gates, axis=-1, keepdims=True)
    grad_chosen = gate_values * centered_gates
    grad_logits = jnp.sum(route_hot * grad_chosen[:, :, None], axis=1).astype(BF)
    grad_normed_router = contract_cols(grad_logits, router_full)
    grad_normed_two = shared_back.astype(F32) + grad_normed_routed + grad_normed_router
    grad_from_norm, gain_second_terms = norm_back(
        grad_normed_two, second_norm_gain, scaled_two, inverse_two
    )
    grad_middle = grad_float + grad_from_norm

    grad_middle, upward_last, downward_last, upward_free, downward_free, units_in = tie(
        grad_middle, upward_last, downward_last, upward_free, downward_free, units_in
    )
    seq_grad_middle = lax.all_gather(grad_middle.astype(BF), ZC, axis=0, tiled=True)
    upward_last = shift(upward_last, "y", -1)
    downward_last = shift(downward_last, "y", 1)

    units_sum = jnp.sum(
        units_in.reshape(4, 2, 2, 8, 16, 2 * UNIT_PAD).astype(F32), axis=(1, 3)
    ).reshape(8, 16, 2 * UNIT_PAD)
    unit_results = [
        unit_columns_back(units_sum[..., :UNIT_PAD], units),
        unit_columns_back(units_sum[..., UNIT_PAD:], units),
    ]
    seq_grad_middle, upward_last, downward_last, out_part, unit_results = tie(
        seq_grad_middle, upward_last, downward_last, out_part, unit_results
    )
    shared_out = lax.psum_scatter(out_part, ZC, scatter_dimension=0, tiled=True)
    grad_output = contract_rows(attended_own, seq_grad_middle).astype(BF)
    down_grads = jnp.concatenate(
        [grad_output.reshape(16, 16, width), grad_sdown.reshape(16, 24, width)], axis=1
    ).reshape(640, width)
    down_in = lax.all_to_all(down_grads, XYX, split_axis=0, concat_axis=0, tiled=True)
    grad_heads = contract_cols(seq_grad_middle, output_own).astype(BF)
    attention_grads = attend_back(
        xl_at, queries, keys, keys_other, values, values_other, grad_heads, row_lse
    )

    attention_grads, shared_out = tie(attention_grads, shared_out)
    _, _, pair, pair_other, _, _ = attention_grads
    grad_query_flat, normed_part, latent_kept, latent_given = back_rows(
        jnp.stack([xl_at, c_at]), attention_grads, tables, head_in, expand_own
    )
    grad_query_flat, normed_part, latent_kept, latent_given, down_in = tie(
        grad_query_flat, normed_part, latent_kept, latent_given, down_in
    )
    latent_sums = total(latent_kept, shift(latent_given, "c", 1)).reshape(8 * row_count, -1)
    latent_in = lax.all_to_all(latent_sums, ("z", "xl"), split_axis=0, concat_axis=0, tiled=True)
    grad_normed_part = lax.psum_scatter(normed_part, ZC, scatter_dimension=0, tiled=True)
    grad_expand = (
        contract_rows(latent_mine[:, :KV_RANK], pair)
        + contract_rows(latent_other[:, :KV_RANK], pair_other)
    ).astype(BF)
    grad_query_w = query_grads(normed_half, grad_query_flat)
    grad_expand = grad_expand.reshape(128, 4, 4, 128).transpose(0, 2, 1, 3).reshape(length, 128)
    head_grads = jnp.concatenate([grad_query_w, grad_expand], axis=-1)

    summed = [
        total(blocks[0], upward_last, downward_free),
        total(blocks[1], upward_free, downward_last),
    ]
    latent_in, head_grads, summed = tie(latent_in, head_grads, summed)
    heads_in = exchange_all(head_grads)
    parted = [part(summed[turn], turn) for turn in range(2)]
    grad_latent_sum = jnp.sum(latent_in.reshape(8, row_count, -1).astype(F32), axis=0)
    scaled_one, inverse_one = normalize(input_rows)
    normed_one = (scaled_one * first_norm_gain).astype(BF)
    latent_own = lax.dynamic_slice_in_dim(
        latent_half, (z_at * 2 + c_at) * row_count, row_count, axis=0
    )
    scaled_latent, inverse_latent = normalize(latent_own[:, :KV_RANK])
    grad_latent, gain_latent_terms = norm_back(
        grad_latent_sum[:, :KV_RANK], latent_norm_gain, scaled_latent, inverse_latent
    )
    grad_latent_all = jnp.concatenate(
        [grad_latent, grad_latent_sum[:, KV_RANK : KV_RANK + ROPE]], axis=-1
    ).astype(BF)
    grad_normed_one = grad_normed_part.astype(F32) + contract_cols(grad_latent_all, latent_full)
    grad_input_norm, gain_first_terms = norm_back(
        grad_normed_one, first_norm_gain, scaled_one, inverse_one
    )

    gain_latent = jnp.sum(gain_latent_terms, axis=0).reshape(128, 1, 4)
    final_out = last_rows(
        normed_one,
        normed_two,
        gain_first_terms.astype(BF),
        gain_second_terms.astype(BF),
        jnp.pad(grad_latent_all, ((0, 0), (0, PACKED - KV_RANK - ROPE))),
        jnp.pad(grad_logits, ((0, 0), (64, 48))),
        jnp.pad(gain_latent, ((0, 0), (0, 15), (96, 28))).reshape(length, 128),
    )

    down_in = down_in.reshape(16, 40, width)
    grad_output_w = jnp.sum(down_in[:, :16].astype(F32), axis=0)
    grad_sdown_w = jnp.sum(down_in[:, 16 : 16 + down_count].astype(F32), axis=0)
    final_out, heads_in, parted, grad_output_w, grad_sdown_w = tie(
        final_out, heads_in, parted, grad_output_w, grad_sdown_w
    )
    parted[0] = jnp.where(c_at == xh_at, summed[0], parted[0])
    final_in = exchange_all(final_out)

    grad_inputs = grad_middle + grad_input_norm
    result = middle + shared_out.astype(F32) + routed
    first_half = jnp.where(xh_at == 0, parted[0], parted[1])
    second_half = jnp.where(xh_at == 0, parted[1], parted[0])
    repeated = 2 * HALF - expert_gate.shape[2]
    expert_results = [
        jnp.concatenate(
            [
                first_half[:, k * HALF : (k + 1) * HALF],
                second_half[:, k * HALF + repeated : (k + 1) * HALF],
            ],
            axis=-1,
        ).astype(F32)
        for k in range(3)
    ]
    expert_results[2] = expert_results[2].T
    grad_query_weight, grad_expand_weight = head_sums(heads_in.reshape(128, 16, 512))
    beside = (grad_inputs, result, grad_query_weight, grad_expand_weight)
    final_in, beside = tie(final_in, beside)
    grad_inputs, result, grad_query_weight, grad_expand_weight = beside
    common_sum = jnp.sum(final_in.reshape(128, 16, PACKED).astype(F32), axis=0)
    return (
        result.astype(BF)[None],
        grad_inputs.astype(BF)[None],
        common_sum[:, 592],
        grad_query_weight,
        common_sum[:, :576],
        common_sum[0, 608:612],
        grad_expand_weight,
        grad_output_w,
        common_sum[:, 593],
        common_sum[:, 576:592],
        unit_results[0],
        unit_results[1],
        grad_sdown_w,
        expert_results[0][None],
        expert_results[1][None],
        expert_results[2][None],
    )


def solution(mesh):
    fine = Mesh(mesh.devices.reshape(4, 2, 2, 4, 2), ALL)
    return jax.shard_map(
        on_device,
        mesh=fine,
        in_specs=(
            P(FSDP, SEQ, None),
            P(FSDP, None),
            P(FSDP, SEQ, None),
            P(ALL),
            P(ALL, None),
            P(ALL, None),
            P(ALL),
            P(ALL, None),
            P(ALL, None),
            P(ALL),
            P(ALL, None),
            P(ALL, None),
            P(ALL, None),
            P(ALL, None),
            P(SEQ, FSDP, None),
            P(SEQ, FSDP, None),
            P(SEQ, None, FSDP),
            P(FSDP, SEQ, None),
        ),
        out_specs=(
            P(FSDP, SEQ, None),
            P(FSDP, SEQ, None),
            P(ALL),
            P(ALL, None),
            P(ALL, None),
            P(ALL),
            P(ALL, None),
            P(ALL, None),
            P(ALL),
            P(ALL, None),
            P(ALL, None),
            P(ALL, None),
            P(ALL, None),
            P(SEQ, FSDP, None),
            P(SEQ, FSDP, None),
            P(SEQ, None, FSDP),
        ),
        check_vma=False,
    )
```

```python
import math

import jax
import jax.numpy as jnp
from jax import lax
from jax.experimental import pallas as pl
from jax.experimental.pallas import tpu as pltpu
from jax.sharding import Mesh
from jax.sharding import PartitionSpec as P

NOPE = 128
ROPE = 64
VDIM = 128
KV_RANK = 512
TOP = 2
UNIT_PAD = 384
SLOTS = 24
HALF = 768
PACKED = 640
QUERY = 384
EPSILON = 1e-06
VMEM_BYTES = 60 * 2**20
LESS_VMEM = 40 * 2**20
SMALL = pl.CostEstimate(flops=1024, bytes_accessed=2**18, transcendentals=0)

SEQ = ("z", "xl", "c")
FSDP = ("y", "xh")
ZC = ("z", "c")
XYX = ("xl", "y", "xh")
ZXX = ("z", "xl", "xh")
ALL = ("z", "xl", "c", "y", "xh")
BF = jnp.bfloat16
F32 = jnp.float32


def matmul(left_side, right_side):
    return jnp.dot(left_side, right_side, preferred_element_type=F32)


def contract_rows(left_side, right_side):
    return lax.dot_general(
        left_side, right_side, (((0,), (0,)), ((), ())), preferred_element_type=F32
    )


def contract_cols(left_side, right_side):
    return lax.dot_general(
        left_side, right_side, (((1,), (1,)), ((), ())), preferred_element_type=F32
    )


def normalize(values):
    inverse = lax.rsqrt(jnp.mean(values * values, axis=-1, keepdims=True) + EPSILON)
    return (values * inverse, inverse)


def norm_back(grad_normed, gain_vector, scaled, inverse):
    grad_scaled = grad_normed * gain_vector
    grad_input = inverse * (
        grad_scaled - scaled * jnp.mean(grad_scaled * scaled, axis=-1, keepdims=True)
    )
    return (grad_input, grad_normed * scaled)


def rotary_tables(position_list):
    half_rope = ROPE // 2
    frequency = jnp.exp(-(2.0 * jnp.arange(half_rope, dtype=F32) / ROPE) * math.log(10000.0))
    angles = position_list.astype(F32)[:, None] * frequency[None, :]
    return (jnp.cos(angles), jnp.sin(angles))


def wide_tables(cosine_table, sine_table):
    return (
        jnp.concatenate([cosine_table, cosine_table], axis=-1),
        jnp.concatenate([-sine_table, sine_table], axis=-1),
    )


def places(kind, rows, head, swapped):
    row = lax.broadcasted_iota(jnp.int32, (rows, ROPE), 0)
    col = lax.broadcasted_iota(jnp.int32, (rows, ROPE), 1)
    if swapped:
        col = (col + ROPE // 2) % ROPE
    return (row == col + head * ROPE).astype(kind)


def shift(values, axis_name, step):
    count = lax.axis_size(axis_name)
    return lax.ppermute(values, axis_name, [((i + step) % count, i) for i in range(count)])


def front_body(
    rows_ref, gain_ref, weight_ref, latent_gain_ref, packed_ref, normed_ref, latent_ref
):
    scaled, _ = normalize(rows_ref[...].astype(F32))
    normed = (scaled * gain_ref[...]).astype(BF)
    latent = matmul(normed, weight_ref[...])
    normed_ref[...] = normed
    latent_ref[...] = latent
    scaled_latent, _ = normalize(latent[:, :KV_RANK])
    packed_ref[:, :KV_RANK] = (scaled_latent * latent_gain_ref[...]).astype(BF)
    packed_ref[:, KV_RANK : KV_RANK + ROPE] = latent[:, KV_RANK:].astype(BF)
    packed_ref[:, KV_RANK + ROPE :] = jnp.zeros((latent.shape[0], PACKED - KV_RANK - ROPE), BF)


def front(rows, gain, weight, latent_gain):
    count, width = rows.shape
    columns, tile = weight.shape[1], 256
    outs = (
        jax.ShapeDtypeStruct((count, PACKED), BF),
        jax.ShapeDtypeStruct((count, width), BF),
        jax.ShapeDtypeStruct((count, columns), F32),
    )
    return pl.pallas_call(
        front_body,
        grid=(count // tile,),
        out_shape=outs,
        in_specs=[
            row_tiles(rows.shape, tile),
            whole_block((1, width)),
            whole_block(weight.shape),
            whole_block((1, KV_RANK)),
        ],
        out_specs=tuple(row_tiles(out.shape, tile) for out in outs),
        compiler_params=pltpu.CompilerParams(vmem_limit_bytes=LESS_VMEM),
        cost_estimate=SMALL,
    )(rows, gain[None], weight, latent_gain[None])


def key_values(packed_ref, expand_ref, cosine, sine, keys_ref, values_ref):
    expanded = matmul(packed_ref[:, :KV_RANK], expand_ref[...]).astype(BF)
    rope = packed_ref[:, KV_RANK : KV_RANK + ROPE]
    turned = (
        rope.astype(F32) * cosine + matmul(rope, places(BF, ROPE, 0, True)) * sine
    ).astype(BF)
    for head in range(2):
        at = head * (NOPE + VDIM)
        keys_ref[head, :, :NOPE] = expanded[:, at : at + NOPE]
        keys_ref[head, :, NOPE:] = turned
        values_ref[head] = expanded[:, at + NOPE : at + NOPE + VDIM]


def own_heads_body(
    normed_ref, query_weight_ref, packed_ref, expand_ref, cosine_ref, sine_ref,
    queries_ref, keys_ref, values_ref,
):
    cosine, sine = cosine_ref[...], sine_ref[...]
    flat = matmul(normed_ref[...], query_weight_ref[...]).astype(BF)
    for head in range(2):
        queries_ref[head, :, :NOPE] = flat[:, head * NOPE : (head + 1) * NOPE]
        ropes = flat[:, 2 * NOPE :]
        queries_ref[head, :, NOPE:] = (
            matmul(ropes, places(BF, 2 * ROPE, head, False)) * cosine
            + matmul(ropes, places(BF, 2 * ROPE, head, True)) * sine
        ).astype(BF)
    key_values(packed_ref, expand_ref, cosine, sine, keys_ref, values_ref)


def other_heads_body(packed_ref, expand_ref, cosine_ref, sine_ref, keys_ref, values_ref):
    key_values(packed_ref, expand_ref, cosine_ref[...], sine_ref[...], keys_ref, values_ref)


def row_tiles(shape, tile):
    if len(shape) == 2:
        return pl.BlockSpec((tile, shape[1]), lambda i: (i, 0))
    return pl.BlockSpec((shape[0], tile, shape[2]), lambda i: (0, i, 0))


def whole_block(shape):
    return pl.BlockSpec(shape, lambda i: (0,) * len(shape))


def heads_of(packed, expand_own, tables, normed=None, query_own=None):
    rows, tile = packed.shape[0], 256
    keys = jax.ShapeDtypeStruct((2, rows, NOPE + ROPE), BF)
    values = jax.ShapeDtypeStruct((2, rows, VDIM), BF)
    outs = (keys, values) if normed is None else (keys, keys, values)
    args, specs = [packed, expand_own, *tables], []
    specs = [
        row_tiles(packed.shape, tile),
        whole_block(expand_own.shape),
        row_tiles(tables[0].shape, tile),
        row_tiles(tables[1].shape, tile),
    ]
    if normed is not None:
        args = [normed, query_own] + args
        specs = [row_tiles(normed.shape, tile), whole_block((normed.shape[1], QUERY))] + specs
    return pl.pallas_call(
        other_heads_body if normed is None else own_heads_body,
        grid=(rows // tile,),
        out_shape=outs,
        in_specs=specs,
        out_specs=tuple(row_tiles(out.shape, tile) for out in outs),
        compiler_params=pltpu.CompilerParams(vmem_limit_bytes=LESS_VMEM),
        cost_estimate=SMALL,
    )(*args)


def back_rows_body(
    at_ref, nope_ref, rope_ref, pair_ref, pair_other_ref, key_rope_ref, key_rope_other_ref,
    cosine_ref, sine_ref, cosine_other_ref, sine_other_ref, query_weight_ref, expand_ref,
    flat_ref, part_ref, kept_ref, given_ref, terms_ref,
):
    swap = places(F32, ROPE, 0, True)

    def turned_back(values, cosine, sine):
        swapped = jnp.dot(
            values, swap, precision=lax.Precision.HIGHEST, preferred_element_type=F32
        )
        return (values * cosine - swapped * sine).astype(BF)

    cosine, sine = cosine_ref[...], sine_ref[...]
    flat_ref[:, : 2 * NOPE] = nope_ref[...]
    for head in range(2):
        at = 2 * NOPE + head * ROPE
        flat_ref[:, at : at + ROPE] = turned_back(rope_ref[head], cosine, sine)
    part_ref[...] = contract_cols(flat_ref[...], query_weight_ref[...]).astype(BF)
    rows = nope_ref.shape[0] // 2
    core = at_ref[1]
    for i, (pairs, ropes, cosine, sine) in enumerate(
        (
            (pair_ref, key_rope_ref, cosine, sine),
            (pair_other_ref, key_rope_other_ref, cosine_other_ref[...], sine_other_ref[...]),
        )
    ):
        terms = contract_cols(pairs[...], expand_ref[...]).astype(BF)
        rope = (
            turned_back(ropes[0], cosine, sine).astype(F32)
            + turned_back(ropes[1], cosine, sine).astype(F32)
        ).astype(BF)
        for c in range(2):
            terms_ref[c, :, :KV_RANK] = terms[c * rows : (c + 1) * rows]
            terms_ref[c, :, KV_RANK : KV_RANK + ROPE] = rope[c * rows : (c + 1) * rows]
            terms_ref[c, :, KV_RANK + ROPE :] = jnp.zeros((rows, PACKED - KV_RANK - ROPE), BF)
        place = pl.ds(at_ref[0] if i == 0 else 1 - at_ref[0], 1)
        kept_ref[place] = terms_ref[pl.ds(core, 1)]
        given_ref[place] = terms_ref[pl.ds(1 - core, 1)]


def back_rows(at, grads, tables, query_own, expand_own):
    nope, rope, pair, pair_other, key_rope, key_rope_other = grads
    rows, tile = nope.shape[0], 256
    args = [nope, rope, pair, pair_other, key_rope, key_rope_other, *tables]
    terms = jax.ShapeDtypeStruct((8, tile // 2, PACKED), BF)
    terms_spec = pl.BlockSpec((2, tile // 2, PACKED), lambda i: (i, 0, 0))
    outs = (
        jax.ShapeDtypeStruct((rows, QUERY), BF),
        jax.ShapeDtypeStruct((rows, query_own.shape[0]), BF),
    )
    return pl.pallas_call(
        back_rows_body,
        grid=(rows // tile,),
        out_shape=outs + (terms, terms),
        in_specs=[pl.BlockSpec(memory_space=pltpu.SMEM)]
        + [row_tiles(arg.shape, tile) for arg in args]
        + [whole_block((query_own.shape[0], QUERY)), whole_block(expand_own.shape)],
        out_specs=tuple(row_tiles(out.shape, tile) for out in outs) + (terms_spec, terms_spec),
        scratch_shapes=[pltpu.VMEM((2, tile // 2, PACKED), BF)],
        compiler_params=pltpu.CompilerParams(vmem_limit_bytes=VMEM_BYTES),
        cost_estimate=SMALL,
    )(at, *args, query_own, expand_own)


def scores_of(query, keys, own, other_first, diagonal):
    scores = contract_cols(query, keys) * (NOPE + ROPE) ** (-0.5)
    if not diagonal:
        return scores
    if not own:
        return jnp.where(other_first, scores, -1e30)
    row = lax.broadcasted_iota(jnp.int32, scores.shape, 0)
    col = lax.broadcasted_iota(jnp.int32, scores.shape, 1)
    return jnp.where(col <= row, scores, -1e30)


def attend_body(
    at_ref, query_ref, key_ref, key_other_ref, value_ref, value_other_ref, out_ref, lse_ref, scores_ref
):
    count = query_ref.shape[1]
    block = pl.program_id(1)
    query = query_ref[0]
    other_first = at_ref[0] == 1
    sets = ((key_ref, value_ref, True, 0), (key_other_ref, value_other_ref, False, count))

    def score(t, top, diagonal=False):
        at = pl.ds(pl.multiple_of(t * count, count), count)
        for keys, _, own, place in sets:
            scores = scores_of(query, keys[0, at, :], own, other_first, diagonal)
            scores_ref[:, pl.ds(pl.multiple_of(2 * t * count + place, count), count)] = scores
            top = jnp.maximum(top, jnp.max(scores, axis=-1, keepdims=True))
        return top

    top = lax.fori_loop(0, block, score, jnp.full((count, 1), -1e30, F32))
    top = score(block, top, True)

    def weigh(t, carry):
        row_total, summed = carry
        at = pl.ds(pl.multiple_of(t * count, count), count)
        for _, values, _, place in sets:
            scores = scores_ref[:, pl.ds(pl.multiple_of(2 * t * count + place, count), count)]
            exponent = jnp.exp(scores - top)
            row_total = row_total + jnp.sum(exponent, axis=-1, keepdims=True)
            summed = summed + matmul(exponent.astype(BF), values[0, at, :])
        return row_total, summed

    row_total, summed = lax.fori_loop(
        0, block + 1, weigh, (jnp.zeros((count, 1), F32), jnp.zeros((count, VDIM), F32))
    )
    out_ref[...] = (summed / row_total).astype(BF)
    lse_ref[0] = top + jnp.log(row_total)


def attend(xl_at, queries, keys, keys_other, values, values_other):
    heads, rows, depth = queries.shape
    count = rows // 4
    key_spec = pl.BlockSpec((1, rows, depth), lambda h, j: (h, 0, 0))
    value_spec = pl.BlockSpec((1, rows, VDIM), lambda h, j: (h, 0, 0))
    return pl.pallas_call(
        attend_body,
        grid=(heads, 4),
        out_shape=(
            jax.ShapeDtypeStruct((rows, heads * VDIM), BF),
            jax.ShapeDtypeStruct((heads, rows, 1), F32),
        ),
        in_specs=[
            pl.BlockSpec(memory_space=pltpu.SMEM),
            pl.BlockSpec((1, count, depth), lambda h, j: (h, j, 0)),
            key_spec,
            key_spec,
            value_spec,
            value_spec,
        ],
        out_specs=(
            pl.BlockSpec((count, VDIM), lambda h, j: (j, h)),
            pl.BlockSpec((1, count, 1), lambda h, j: (h, j, 0)),
        ),
        scratch_shapes=[pltpu.VMEM((count, 2 * rows), F32)],
        compiler_params=pltpu.CompilerParams(vmem_limit_bytes=LESS_VMEM),
        cost_estimate=SMALL,
    )(xl_at.reshape(1), queries, keys, keys_other, values, values_other)


def attend_back_body(
    at_ref, query_ref, key_ref, key_other_ref, value_ref, value_other_ref, grad_ref, lse_ref,
    nope_ref, rope_ref, pair_ref, pair_other_ref, key_rope_ref, key_rope_other_ref,
    probs_ref, grad_probs_ref, key_sum, key_other_sum, value_sum, value_other_sum,
):
    count = query_ref.shape[1]
    block = pl.program_id(1)
    query, grad = query_ref[0], grad_ref[...]
    other_first = at_ref[0] == 1
    scale = (NOPE + ROPE) ** (-0.5)
    sets = (
        (key_ref, value_ref, key_sum, value_sum, True, 0),
        (key_other_ref, value_other_ref, key_other_sum, value_other_sum, False, count),
    )

    @pl.when(block == 0)
    def _():
        for _, _, keys_to, values_to, _, _ in sets:
            keys_to[...] = jnp.zeros_like(keys_to)
            values_to[...] = jnp.zeros_like(values_to)

    def score(t, centered, diagonal=False):
        at = pl.ds(pl.multiple_of(t * count, count), count)
        for keys, values, _, _, own, place in sets:
            to = pl.ds(pl.multiple_of(2 * t * count + place, count), count)
            scores = scores_of(query, keys[0, at, :], own, other_first, diagonal)
            probs = jnp.exp(scores - lse_ref[0])
            grad_probs = contract_cols(grad, values[0, at, :])
            probs_ref[:, to] = probs
            grad_probs_ref[:, to] = grad_probs
            centered = centered + jnp.sum(probs * grad_probs, axis=-1, keepdims=True)
        return centered

    centered = lax.fori_loop(0, block, score, jnp.zeros((count, 1), F32))
    centered = score(block, centered, True)

    def give(t, summed):
        at = pl.ds(pl.multiple_of(t * count, count), count)
        for keys, _, keys_to, values_to, _, place in sets:
            to = pl.ds(pl.multiple_of(2 * t * count + place, count), count)
            probs = probs_ref[:, to]
            grad_scores = (probs * (grad_probs_ref[:, to] - centered)).astype(BF)
            keys_to[at, :] += contract_rows(grad_scores, query)
            values_to[at, :] += contract_rows(probs.astype(BF), grad)
            summed = summed + matmul(grad_scores, keys[0, at, :])
        return summed

    grad_query = scale * lax.fori_loop(0, block + 1, give, jnp.zeros(query.shape, F32))
    nope_ref[...] = grad_query[:, :NOPE].astype(BF)
    rope_ref[0] = grad_query[:, NOPE:]

    @pl.when(block == 3)
    def _():
        for keys_from, values_from, to, rope_to in (
            (key_sum, value_sum, pair_ref, key_rope_ref),
            (key_other_sum, value_other_sum, pair_other_ref, key_rope_other_ref),
        ):
            to[:, :NOPE] = (scale * keys_from[:, :NOPE]).astype(BF)
            to[:, NOPE:] = values_from[...].astype(BF)
            rope_to[0] = scale * keys_from[:, NOPE:]


def attend_back(xl_at, queries, keys, keys_other, values, values_other, grads, lse):
    heads, rows, depth = queries.shape
    count = rows // 4
    key_spec = pl.BlockSpec((1, rows, depth), lambda h, j: (h, 0, 0))
    value_spec = pl.BlockSpec((1, rows, VDIM), lambda h, j: (h, 0, 0))
    pair = jax.ShapeDtypeStruct((rows, heads * (NOPE + VDIM)), BF)
    rope = jax.ShapeDtypeStruct((heads, rows, ROPE), F32)
    pair_spec = pl.BlockSpec((rows, NOPE + VDIM), lambda h, j: (0, h))
    rope_spec = pl.BlockSpec((1, rows, ROPE), lambda h, j: (h, 0, 0))
    return pl.pallas_call(
        attend_back_body,
        grid=(heads, 4),
        out_shape=(
            jax.ShapeDtypeStruct((rows, heads * NOPE), BF),
            rope,
            pair,
            pair,
            rope,
            rope,
        ),
        in_specs=[
            pl.BlockSpec(memory_space=pltpu.SMEM),
            pl.BlockSpec((1, count, depth), lambda h, j: (h, j, 0)),
            key_spec,
            key_spec,
            value_spec,
            value_spec,
            pl.BlockSpec((count, VDIM), lambda h, j: (j, h)),
            pl.BlockSpec((1, count, 1), lambda h, j: (h, j, 0)),
        ],
        out_specs=(
            pl.BlockSpec((count, NOPE), lambda h, j: (j, h)),
            pl.BlockSpec((1, count, ROPE), lambda h, j: (h, j, 0)),
            pair_spec,
            pair_spec,
            rope_spec,
            rope_spec,
        ),
        scratch_shapes=[pltpu.VMEM((count, 2 * rows), F32)] * 2
        + [pltpu.VMEM((rows, depth), F32)] * 2
        + [pltpu.VMEM((rows, VDIM), F32)] * 2,
        compiler_params=pltpu.CompilerParams(vmem_limit_bytes=VMEM_BYTES),
        cost_estimate=SMALL,
    )(xl_at.reshape(1), queries, keys, keys_other, values, values_other, grads, lse)


def group_columns(weight):
    rows, width = weight.shape[0], weight.shape[1] // 16
    return weight.reshape(rows, 4, 2, 2, width).transpose(1, 3, 0, 2, 4).reshape(8, rows, 2, width)


def ungroup_columns(parts):
    rows, width = parts.shape[1], parts.shape[3]
    return parts.reshape(4, 2, rows, 2, width).transpose(2, 0, 3, 1, 4).reshape(rows, 16 * width)


def spread_groups(parts):
    rows, width = parts.shape[1:]
    blocks = jnp.broadcast_to(
        parts.reshape(4, 1, 2, 1, 1, rows, width), (4, 2, 2, 4, 2, rows, width)
    )
    return blocks.reshape(128 * rows, width)


def to_replicas(rows):
    count, width = rows.shape
    blocks = jnp.broadcast_to(rows[None], (16, count, width)).reshape(16 * count, width)
    return lax.all_to_all(blocks, XYX, split_axis=0, concat_axis=0, tiled=True)


def in_row_order(rows):
    width = rows.shape[-1]
    blocks = rows.reshape(2, 8, 4, 2, 16, width).transpose(2, 0, 3, 1, 4, 5)
    return blocks.reshape(-1, width)


def exchange_all(blocks):
    return lax.all_to_all(blocks, ALL, split_axis=0, concat_axis=0, tiled=True)


def tie(*values):
    return lax.optimization_barrier(values)


def halves(gate, up, down):
    turned = down.T
    units = gate.shape[1]
    first = [part[:, :HALF] for part in (gate, up, turned)]
    second = [part[:, units - HALF :] for part in (gate, up, turned)]
    repeated = 2 * HALF - units
    keep = lax.broadcasted_iota(jnp.int32, second[0].shape, 1) >= repeated
    second = [jnp.where(keep, second[0], 0), jnp.where(keep, second[1], 0), second[2]]
    return jnp.concatenate(first, axis=-1), jnp.concatenate(second, axis=-1)


def meet(values, turn):
    pairs = [(2 * c + xh, 2 * (xh ^ turn) + c) for c in range(2) for xh in range(2)]
    pairs = [(source, target) for source, target in pairs if source != target]
    return lax.ppermute(values, ("c", "xh"), pairs)


def part(values, turn):
    pairs = [(2 * c + xh, 2 * xh + (c ^ turn)) for c in range(2) for xh in range(2)]
    pairs = [(source, target) for source, target in pairs if source != target]
    return lax.ppermute(values, ("c", "xh"), pairs)


def total(*terms):
    return sum(term.astype(F32) for term in terms).astype(BF)


def expert_body(at_ref, *refs):
    pieces, (own_ref, other_ref) = refs[:8], refs[8:10]
    own_out, other_out, own_kept, other_kept = refs[10:14]
    weights, sem = refs[14:]
    copies = [
        pltpu.make_async_copy(
            pieces[i], weights.at[pl.ds(pl.multiple_of(at_ref[i] * 256, 256), 256)], sem.at[i]
        )
        for i in range(8)
    ]
    for copy in copies:
        copy.start()
    for copy in copies:
        copy.wait()
    width = own_ref.shape[1] // 2
    for given, result, kept in (
        (own_ref, own_out, own_kept),
        (other_ref, other_out, other_kept),
    ):

        @pl.loop(0, HALF // 256)
        def _(n, given=given, kept=kept):
            def columns(k):
                return pl.ds(pl.multiple_of(k * HALF + n * 256, 256), 256)

            rows, grads = given[:, :width], given[:, width:]
            pre = matmul(rows, weights[:, columns(0)])
            lin = matmul(rows, weights[:, columns(1)])
            grad = matmul(grads, weights[:, columns(2)])
            sigmoid = jax.nn.sigmoid(pre)
            silu = pre * sigmoid
            kept[:, columns(0)] = (grad * lin * sigmoid * (1.0 + pre * (1.0 - sigmoid))).astype(BF)
            kept[:, columns(1)] = (grad * silu).astype(BF)
            kept[:, columns(2)] = (silu * lin).astype(BF)

        @pl.loop(0, width // 256)
        def _(f, kept=kept, result=result):
            block = weights[pl.ds(pl.multiple_of(f * 256, 256), 256), :]
            out = contract_cols(kept[:, 2 * HALF :], block[:, 2 * HALF :])
            back = contract_cols(kept[:, : 2 * HALF], block[:, : 2 * HALF])
            result[:, pl.ds(pl.multiple_of(f * 256, 256), 256)] = out.astype(BF)
            result[:, pl.ds(pl.multiple_of(width + f * 256, 256), 256)] = back.astype(BF)


def expert_rows(order, pieces, own, other):
    rows, width = own.shape
    kept = jax.ShapeDtypeStruct((rows, 3 * HALF), BF)
    result = jax.ShapeDtypeStruct((rows, width), BF)
    whole = pl.BlockSpec(memory_space=pltpu.VMEM)
    return pl.pallas_call(
        expert_body,
        out_shape=(result, result, kept, kept),
        in_specs=[pl.BlockSpec(memory_space=pltpu.SMEM)]
        + [pl.BlockSpec(memory_space=pl.ANY)] * 8
        + [whole] * 2,
        out_specs=(whole,) * 4,
        scratch_shapes=[pltpu.VMEM((width // 2, 3 * HALF), BF), pltpu.SemaphoreType.DMA((8,))],
        compiler_params=pltpu.CompilerParams(vmem_limit_bytes=VMEM_BYTES),
        cost_estimate=SMALL,
    )(order, *pieces, own, other)


def expert_grad_body(
    at_ref, own_rows, own_grads, other_rows, other_grads, own_kept, other_kept, *outs
):
    first = contract_rows(own_rows[...], own_kept[:, : 2 * HALF]) + contract_rows(
        other_rows[...], other_kept[:, : 2 * HALF]
    )
    last = contract_rows(own_grads[...], own_kept[:, 2 * HALF :]) + contract_rows(
        other_grads[...], other_kept[:, 2 * HALF :]
    )
    for i, out in enumerate(outs):

        @pl.when(pl.program_id(0) == i)
        def _(out=out):
            out[:, : 2 * HALF] = first.astype(BF)
            out[:, 2 * HALF :] = last.astype(BF)


def expert_grads(order, own, other, own_kept, other_kept):
    rows, width = own.shape
    blocks, count = width // 512, order.shape[0]
    row_spec = pl.BlockSpec((rows, 256), lambda i, at: (0, at[i]))
    grad_spec = pl.BlockSpec((rows, 256), lambda i, at: (0, blocks + at[i]))
    kept_spec = pl.BlockSpec((rows, 3 * HALF), lambda i, at: (0, 0))
    return pl.pallas_call(
        expert_grad_body,
        out_shape=(jax.ShapeDtypeStruct((256, 3 * HALF), BF),) * count,
        grid_spec=pltpu.PrefetchScalarGridSpec(
            num_scalar_prefetch=1,
            grid=(count,),
            in_specs=[row_spec, grad_spec, row_spec, grad_spec, kept_spec, kept_spec],
            out_specs=(pl.BlockSpec((256, 3 * HALF), lambda i, at: (0, 0)),) * count,
        ),
        compiler_params=pltpu.CompilerParams(vmem_limit_bytes=LESS_VMEM),
        cost_estimate=SMALL,
    )(order, own, own, other, other, own_kept, other_kept)


def shared_body(rows_ref, grads_ref, gate_up_ref, down_ref, back_ref, out_ref, kept_ref):
    both = matmul(rows_ref[...], gate_up_ref[...])
    pre, lin = both[:, :UNIT_PAD], both[:, UNIT_PAD:]
    grad = contract_cols(grads_ref[...], down_ref[...])
    sigmoid = jax.nn.sigmoid(pre)
    silu = pre * sigmoid
    hidden = (silu * lin).astype(BF)
    grad_pre = (grad * lin * sigmoid * (1.0 + pre * (1.0 - sigmoid))).astype(BF)
    grad_lin = (grad * silu).astype(BF)
    kept_ref[:, :UNIT_PAD] = grad_pre
    kept_ref[:, UNIT_PAD : 2 * UNIT_PAD] = grad_lin
    kept_ref[:, 2 * UNIT_PAD :] = hidden
    back_ref[...] = contract_cols(kept_ref[:, : 2 * UNIT_PAD], gate_up_ref[...]).astype(BF)
    out_ref[...] = matmul(hidden, down_ref[...]).astype(BF)


def shared_rows(rows, grads, gate_up, down):
    count, width = rows.shape
    tile = 256
    row_spec = pl.BlockSpec((tile, width), lambda i: (i, 0))
    return pl.pallas_call(
        shared_body,
        grid=(count // tile,),
        out_shape=(
            jax.ShapeDtypeStruct((count, width), BF),
            jax.ShapeDtypeStruct((count, width), BF),
            jax.ShapeDtypeStruct((count, 3 * UNIT_PAD), BF),
        ),
        in_specs=[
            row_spec,
            row_spec,
            pl.BlockSpec(gate_up.shape, lambda i: (0, 0)),
            pl.BlockSpec(down.shape, lambda i: (0, 0)),
        ],
        out_specs=(row_spec, row_spec, pl.BlockSpec((tile, 3 * UNIT_PAD), lambda i: (i, 0))),
        compiler_params=pltpu.CompilerParams(vmem_limit_bytes=VMEM_BYTES),
        cost_estimate=SMALL,
    )(rows, grads, gate_up, down)


def last_rows_body(
    one_ref, two_ref, first_terms_ref, second_terms_ref, latent_ref, logits_ref, extra_ref, out_ref
):
    column = lax.broadcasted_iota(jnp.int32, logits_ref.shape, 1)
    latent = contract_rows(one_ref[...], latent_ref[...])
    out_ref[:, :KV_RANK] = latent[:, :KV_RANK].astype(BF)
    last = latent[:, KV_RANK:] + contract_rows(two_ref[...], logits_ref[...])
    last = last + contract_rows(first_terms_ref[...], (column == 80).astype(BF))
    last = last + contract_rows(second_terms_ref[...], (column == 81).astype(BF))
    out_ref[:, KV_RANK:] = (last + extra_ref[...]).astype(BF)


def last_rows(normed_one, normed_two, first_terms, second_terms, latent, logits, extra):
    rows, length = normed_one.shape
    tile = 256
    column_spec = pl.BlockSpec((rows, tile), lambda i: (0, i))
    out = jax.ShapeDtypeStruct((length, PACKED), BF)
    return pl.pallas_call(
        last_rows_body,
        grid=(length // tile,),
        out_shape=out,
        in_specs=[column_spec] * 4
        + [whole_block(latent.shape), whole_block(logits.shape), row_tiles(extra.shape, tile)],
        out_specs=row_tiles(out.shape, tile),
        compiler_params=pltpu.CompilerParams(vmem_limit_bytes=VMEM_BYTES),
        cost_estimate=SMALL,
    )(normed_one, normed_two, first_terms, second_terms, latent, logits, extra)


def head_sums_body(in_ref, query_ref, expand_ref):
    for z in range(4):
        for c in range(2):

            def add(f, summed, z=z, c=c):
                for xl in range(2):
                    summed = summed + in_ref[((z * 2 + xl) * 2 + c) * 8 + f].astype(F32)
                return summed

            summed = lax.fori_loop(0, 8, add, jnp.zeros(in_ref.shape[1:], F32))
            for xl in range(2):
                part = z * 4 + xl * 2 + c
                at = part * (NOPE + ROPE)
                query_ref[:, at : at + NOPE] = summed[:, xl * NOPE : (xl + 1) * NOPE]
                rope_at = 2 * NOPE + xl * ROPE
                query_ref[:, at + NOPE : at + NOPE + ROPE] = summed[:, rope_at : rope_at + ROPE]
                for half in range(2):
                    j = 2 * xl + half
                    at = part * 256 + half * 128
                    expand_ref[:, at : at + 128] = summed[4 * j : 4 * j + 4, 384:]


def head_sums(arrived):
    whole = pl.BlockSpec(memory_space=pltpu.VMEM)
    return pl.pallas_call(
        head_sums_body,
        out_shape=(
            jax.ShapeDtypeStruct((16, 16 * (NOPE + ROPE)), F32),
            jax.ShapeDtypeStruct((4, 4096), F32),
        ),
        in_specs=[whole],
        out_specs=(whole,) * 2,
        compiler_params=pltpu.CompilerParams(vmem_limit_bytes=LESS_VMEM),
        cost_estimate=SMALL,
    )(arrived)


def query_grads_body(normed_ref, flat_ref, out_ref):
    out_ref[...] = contract_rows(normed_ref[...], flat_ref[...]).astype(BF)


def query_grads(normed, flat):
    tile = 256
    return pl.pallas_call(
        query_grads_body,
        grid=(normed.shape[1] // tile,),
        out_shape=jax.ShapeDtypeStruct((normed.shape[1], flat.shape[1]), BF),
        in_specs=[
            pl.BlockSpec((normed.shape[0], tile), lambda i: (0, i)),
            whole_block(flat.shape),
        ],
        out_specs=pl.BlockSpec((tile, flat.shape[1]), lambda i: (i, 0)),
        compiler_params=pltpu.CompilerParams(vmem_limit_bytes=LESS_VMEM),
        cost_estimate=SMALL,
    )(normed, flat)


def unit_columns_out(weight):
    runs = group_columns(weight).reshape(8, 16, 16, -1)
    return jnp.pad(runs, ((0, 0), (0, 0), (0, 0), (0, 24 - runs.shape[-1]))).reshape(8, 16, -1)


def unit_columns_back(parts, units):
    runs = parts.reshape(8, 16, 16, 24)[..., : units // 8]
    return ungroup_columns(runs.reshape(8, 16, 2, units))


def on_device(
    tokens,
    positions,
    routes,
    first_gain,
    query_weight,
    latent_weight,
    latent_gain,
    expand_weight,
    output_weight,
    second_gain,
    router_weight,
    shared_gate,
    shared_up,
    shared_down,
    expert_gate,
    expert_up,
    expert_down,
    cotangent,
):
    z_at, xl_at, c_at = lax.axis_index("z"), lax.axis_index("xl"), lax.axis_index("c")
    y_at, xh_at = lax.axis_index("y"), lax.axis_index("xh")
    own_tokens = tokens[0]
    row_count, width = own_tokens.shape
    length = 16 * row_count
    expert_count = router_weight.shape[1]
    units = shared_gate.shape[1] // 16

    half_tokens = lax.all_gather(own_tokens, ZC, axis=0, tiled=True)

    cosine_table, sine_table = rotary_tables(positions[0])

    def half_rows(table, at):
        return lax.dynamic_index_in_dim(
            table.reshape(4, 2, 2 * row_count, -1), at, axis=1, keepdims=False
        ).reshape(length // 2, -1)

    wide = wide_tables(cosine_table, sine_table)
    tables = [half_rows(table, at) for at in (xl_at, 1 - xl_at) for table in wide]
    route_ids = routes[0]
    route_hot = (
        route_ids[:, :, None] == jnp.arange(expert_count, dtype=jnp.int32)[None, None, :]
    ).astype(F32)
    grad_result = cotangent[0]
    grad_float = grad_result.astype(F32)
    route_total = row_count * TOP
    flat_hot = route_hot.reshape(route_total, expert_count).astype(BF)
    earlier = (
        jnp.arange(route_total, dtype=jnp.int32)[:, None]
        > jnp.arange(route_total, dtype=jnp.int32)[None, :]
    ).astype(BF)
    before = matmul(earlier, flat_hot)
    slot_place = jnp.sum(before * flat_hot.astype(F32), axis=-1).astype(jnp.int32)
    slot_ids = (route_ids.reshape(route_total) * SLOTS + slot_place).reshape(row_count, TOP)
    slot_match = (
        jnp.arange(expert_count * SLOTS, dtype=jnp.int32)[:, None, None] == slot_ids[None, :, :]
    )
    dispatch = jnp.any(slot_match, axis=-1).astype(BF)
    picks = (
        jnp.arange(expert_count * SLOTS, dtype=jnp.int32)[None, :]
        == slot_ids.T.reshape(-1)[:, None]
    ).astype(BF)
    dispatch_grads = matmul(dispatch, grad_result)
    first_half, second_half = halves(expert_gate[0], expert_up[0], expert_down[0])
    met = [jnp.where((xh_at ^ turn) == 0, first_half, second_half) for turn in range(2)]

    query_group = group_columns(query_weight)
    expand_group = group_columns(expand_weight).reshape(8, 16, 128)
    head_group = jnp.concatenate(
        [
            query_group[..., :NOPE].reshape(8, 16, 2 * NOPE),
            query_group[..., NOPE:].reshape(8, 16, 2 * ROPE),
            expand_group,
        ],
        axis=-1,
    )
    common = jnp.concatenate(
        [
            latent_weight,
            router_weight,
            first_gain[:, None],
            second_gain[:, None],
            jnp.pad(latent_gain, (0, 12))[:, None],
            jnp.zeros((16, 45), BF),
        ],
        axis=-1,
    )
    unit_group = jnp.concatenate(
        [unit_columns_out(weight) for weight in (shared_gate, shared_up)], axis=-1
    ).reshape(128, 768)
    common_in = exchange_all(jnp.broadcast_to(common[None], (128, 16, 640)).reshape(2048, 640))
    met_own = met[0]
    met = [meet(met[turn], turn) for turn in range(2)]
    met[0] = jnp.where(c_at == xh_at, met_own, met[0])
    head_group = spread_groups(head_group)
    unit_group, common_in = tie(unit_group, common_in)
    unit_group = lax.all_to_all(unit_group, ZC, split_axis=0, concat_axis=0, tiled=True)

    half_tokens, common_in, met, head_group = tie(half_tokens, common_in, met, head_group)
    head_in = exchange_all(head_group)
    above, below = [None, None], [None, None]
    above[0], below[0] = shift(met[0], "y", 1), shift(met[0], "y", -1)
    gains = common_in[:, 512:640].T.astype(F32)
    first_norm_gain, second_norm_gain = gains[80], gains[81]
    latent_norm_gain = gains[82].reshape(128, 16)[:, :4].reshape(KV_RANK)
    latent_full = common_in[:, :576]
    router_full = common_in[:, 576:592]
    latent_mine, normed_half, latent_half = front(
        half_tokens, first_norm_gain, latent_full, latent_norm_gain
    )
    latent_other = shift(latent_mine, "xl", 1)

    down_count = shared_down.shape[0]
    down_rows = jnp.concatenate(
        [output_weight, jnp.pad(shared_down, ((0, 24 - down_count), (0, 0)))], axis=0
    )
    latent_other, latent_mine, normed_half, head_in, met, down_rows, grad_result, tables, unit_group, above[0], below[0], dispatch, dispatch_grads, picks = tie(
        latent_other, latent_mine, normed_half, head_in, met, down_rows, grad_result, tables, unit_group, above[0], below[0], dispatch, dispatch_grads, picks
    )
    down_all = to_replicas(down_rows).reshape(16, 40, width)
    seq_grad = lax.all_gather(grad_result, ZC, axis=0, tiled=True)
    expand_own = head_in[:, 384:].reshape(KV_RANK, 512)
    queries, keys, values = heads_of(latent_mine, expand_own, tables[:2], normed_half, head_in)

    keys_other, values_other = heads_of(latent_other, expand_own, tables[2:])

    attended_own, row_lse = attend(xl_at, queries, keys, keys_other, values, values_other)

    attended_own, row_lse, seq_grad, unit_group, down_all = tie(
        attended_own, row_lse, seq_grad, unit_group, down_all
    )
    output_own = down_all[:, :16].reshape(256, width)
    attended_part = matmul(attended_own, output_own).astype(BF)
    attended_sum = lax.psum_scatter(attended_part, ZC, scatter_dimension=0, tiled=True)
    unit_columns = to_replicas(unit_group)

    attended_sum, unit_columns, met[1], above[0], down_all = tie(
        attended_sum, unit_columns, met[1], above[0], down_all
    )
    unit_columns = in_row_order(unit_columns)
    sdown_own = down_all[:, 16:].reshape(UNIT_PAD, width)
    above[1], below[1] = shift(met[1], "y", 1), shift(met[1], "y", -1)
    input_rows = own_tokens.astype(F32)
    middle = input_rows + attended_sum.astype(F32)
    scaled_two, inverse_two = normalize(middle)
    normed_two = (scaled_two * second_norm_gain).astype(BF)
    seq_normed_two = lax.all_gather(normed_two, ZC, axis=0, tiled=True)
    logits = matmul(normed_two, router_full)
    chosen = jnp.sum(route_hot * logits[:, None, :], axis=-1)
    gate_values = jax.nn.softmax(chosen, axis=-1)
    slot_gates = jnp.sum(jnp.where(slot_match, gate_values[None], 0.0), axis=(1, 2))
    sent_rows = matmul(dispatch, normed_two).astype(BF)
    sent_grads = (dispatch_grads * slot_gates[:, None]).astype(BF)
    sent = jnp.concatenate([sent_rows, sent_grads], axis=-1)

    sent, seq_normed_two, above[0], above[1], below[1], unit_columns, sdown_own = tie(
        sent, seq_normed_two, above[0], above[1], below[1], unit_columns, sdown_own
    )
    own_in = lax.all_to_all(sent, ZXX, split_axis=0, concat_axis=0, tiled=True)
    far = [shift(above[0], "y", 1), shift(below[1], "y", -1)]

    back_part, out_part, shared_kept = shared_rows(
        seq_normed_two, seq_grad, unit_columns, sdown_own
    )
    grad_units = contract_rows(seq_normed_two, shared_kept[:, : 2 * UNIT_PAD]).astype(BF)
    grad_sdown = contract_rows(shared_kept[:, 2 * UNIT_PAD :], seq_grad).astype(BF)

    own_in, back_part, out_part, grad_units, grad_sdown, far = tie(
        own_in, back_part, out_part, grad_units, grad_sdown, far
    )
    shared_back = lax.psum_scatter(back_part, ZC, scatter_dimension=0, tiled=True)
    units_in = exchange_all(grad_units)
    other_in = shift(own_in, "c", 1)
    pieces = [met[0], met[1], above[0], above[1], far[0], far[1], below[0], below[1]]
    order = jnp.stack(
        [((y_at + step) % 4) * 2 + (c_at ^ turn) for step in range(4) for turn in range(2)]
    ).astype(jnp.int32)
    own_back, other_back, own_kept, other_kept = expert_rows(order, pieces, own_in, other_in)
    other_back, units_in = tie(other_back, units_in)
    back = total(own_back, shift(other_back, "c", 1))

    back, own_kept, other_kept = tie(back, own_kept, other_kept)
    returned = lax.all_to_all(back, ZXX, split_axis=0, concat_axis=0, tiled=True)
    blocks = [None] * 8
    blocks[4], blocks[5] = expert_grads(
        jnp.stack([order[4], order[5]]), own_in, other_in, own_kept, other_kept
    )
    from_below = shift(blocks[4], "y", -1)
    from_above = shift(blocks[5], "y", 1)
    own_kept, blocks[4] = tie(own_kept, blocks[4])
    blocks[3], blocks[6] = expert_grads(
        jnp.stack([order[3], order[6]]), own_in, other_in, own_kept, other_kept
    )
    upward_free, downward_free = shift(blocks[3], "y", -1), shift(blocks[6], "y", 1)
    own_kept, blocks[3] = tie(own_kept, blocks[3])
    blocks[2], blocks[7], blocks[0], blocks[1] = expert_grads(
        jnp.stack([order[2], order[7], order[0], order[1]]), own_in, other_in, own_kept, other_kept
    )

    returned, shared_back, from_below, from_above, blocks[0], blocks[2], blocks[7] = tie(
        returned, shared_back, from_below, from_above, blocks[0], blocks[2], blocks[7]
    )
    upward_last = total(blocks[2], from_below)
    downward_last = total(blocks[7], from_above)
    picked = matmul(picks, returned).reshape(TOP, row_count, 2 * width)
    picked_out = picked[:, :, :width]
    grad_normed_routed = picked[0, :, width:] + picked[1, :, width:]
    routed = gate_values[:, :1] * picked_out[0] + gate_values[:, 1:] * picked_out[1]
    grad_gates = jnp.stack(
        [jnp.sum(grad_float * picked_out[k], axis=-1) for k in range(TOP)], axis=-1
    )
    centered_gates = grad_gates - jnp.sum(gate_values * grad_gates, axis=-1, keepdims=True)
    grad_chosen = gate_values * centered_gates
    grad_logits = jnp.sum(route_hot * grad_chosen[:, :, None], axis=1).astype(BF)
    grad_normed_router = contract_cols(grad_logits, router_full)
    grad_normed_two = shared_back.astype(F32) + grad_normed_routed + grad_normed_router
    grad_from_norm, gain_second_terms = norm_back(
        grad_normed_two, second_norm_gain, scaled_two, inverse_two
    )
    grad_middle = grad_float + grad_from_norm

    grad_middle, upward_last, downward_last, upward_free, downward_free, units_in = tie(
        grad_middle, upward_last, downward_last, upward_free, downward_free, units_in
    )
    seq_grad_middle = lax.all_gather(grad_middle.astype(BF), ZC, axis=0, tiled=True)
    upward_last = shift(upward_last, "y", -1)
    downward_last = shift(downward_last, "y", 1)

    units_sum = jnp.sum(
        units_in.reshape(4, 2, 2, 8, 16, 2 * UNIT_PAD).astype(F32), axis=(1, 3)
    ).reshape(8, 16, 2 * UNIT_PAD)
    unit_results = [
        unit_columns_back(units_sum[..., :UNIT_PAD], units),
        unit_columns_back(units_sum[..., UNIT_PAD:], units),
    ]
    seq_grad_middle, upward_last, downward_last, out_part, unit_results = tie(
        seq_grad_middle, upward_last, downward_last, out_part, unit_results
    )
    shared_out = lax.psum_scatter(out_part, ZC, scatter_dimension=0, tiled=True)
    grad_output = contract_rows(attended_own, seq_grad_middle).astype(BF)
    down_grads = jnp.concatenate(
        [grad_output.reshape(16, 16, width), grad_sdown.reshape(16, 24, width)], axis=1
    ).reshape(640, width)
    down_in = lax.all_to_all(down_grads, XYX, split_axis=0, concat_axis=0, tiled=True)
    grad_heads = contract_cols(seq_grad_middle, output_own).astype(BF)
    attention_grads = attend_back(
        xl_at, queries, keys, keys_other, values, values_other, grad_heads, row_lse
    )

    attention_grads, shared_out = tie(attention_grads, shared_out)
    _, _, pair, pair_other, _, _ = attention_grads
    grad_query_flat, normed_part, latent_kept, latent_given = back_rows(
        jnp.stack([xl_at, c_at]), attention_grads, tables, head_in, expand_own
    )
    grad_query_flat, normed_part, latent_kept, latent_given, down_in = tie(
        grad_query_flat, normed_part, latent_kept, latent_given, down_in
    )
    latent_sums = total(latent_kept, shift(latent_given, "c", 1)).reshape(8 * row_count, -1)
    latent_in = lax.all_to_all(latent_sums, ("z", "xl"), split_axis=0, concat_axis=0, tiled=True)
    grad_normed_part = lax.psum_scatter(normed_part, ZC, scatter_dimension=0, tiled=True)
    grad_expand = (
        contract_rows(latent_mine[:, :KV_RANK], pair)
        + contract_rows(latent_other[:, :KV_RANK], pair_other)
    ).astype(BF)
    grad_query_w = query_grads(normed_half, grad_query_flat)
    grad_expand = grad_expand.reshape(128, 4, 4, 128).transpose(0, 2, 1, 3).reshape(length, 128)
    head_grads = jnp.concatenate([grad_query_w, grad_expand], axis=-1)

    summed = [
        total(blocks[0], upward_last, downward_free),
        total(blocks[1], upward_free, downward_last),
    ]
    latent_in, head_grads, summed = tie(latent_in, head_grads, summed)
    heads_in = exchange_all(head_grads)
    parted = [part(summed[turn], turn) for turn in range(2)]
    grad_latent_sum = jnp.sum(latent_in.reshape(8, row_count, -1).astype(F32), axis=0)
    scaled_one, inverse_one = normalize(input_rows)
    normed_one = (scaled_one * first_norm_gain).astype(BF)
    latent_own = lax.dynamic_slice_in_dim(
        latent_half, (z_at * 2 + c_at) * row_count, row_count, axis=0
    )
    scaled_latent, inverse_latent = normalize(latent_own[:, :KV_RANK])
    grad_latent, gain_latent_terms = norm_back(
        grad_latent_sum[:, :KV_RANK], latent_norm_gain, scaled_latent, inverse_latent
    )
    grad_latent_all = jnp.concatenate(
        [grad_latent, grad_latent_sum[:, KV_RANK : KV_RANK + ROPE]], axis=-1
    ).astype(BF)
    grad_normed_one = grad_normed_part.astype(F32) + contract_cols(grad_latent_all, latent_full)
    grad_input_norm, gain_first_terms = norm_back(
        grad_normed_one, first_norm_gain, scaled_one, inverse_one
    )

    gain_latent = jnp.sum(gain_latent_terms, axis=0).reshape(128, 1, 4)
    final_out = last_rows(
        normed_one,
        normed_two,
        gain_first_terms.astype(BF),
        gain_second_terms.astype(BF),
        jnp.pad(grad_latent_all, ((0, 0), (0, PACKED - KV_RANK - ROPE))),
        jnp.pad(grad_logits, ((0, 0), (64, 48))),
        jnp.pad(gain_latent, ((0, 0), (0, 15), (96, 28))).reshape(length, 128),
    )

    down_in = down_in.reshape(16, 40, width)
    grad_output_w = jnp.sum(down_in[:, :16].astype(F32), axis=0)
    grad_sdown_w = jnp.sum(down_in[:, 16 : 16 + down_count].astype(F32), axis=0)
    final_out, heads_in, parted, grad_output_w, grad_sdown_w = tie(
        final_out, heads_in, parted, grad_output_w, grad_sdown_w
    )
    parted[0] = jnp.where(c_at == xh_at, summed[0], parted[0])
    final_in = exchange_all(final_out)

    grad_inputs = grad_middle + grad_input_norm
    result = middle + shared_out.astype(F32) + routed
    first_half = jnp.where(xh_at == 0, parted[0], parted[1])
    second_half = jnp.where(xh_at == 0, parted[1], parted[0])
    repeated = 2 * HALF - expert_gate.shape[2]
    expert_results = [
        jnp.concatenate(
            [
                first_half[:, k * HALF : (k + 1) * HALF],
                second_half[:, k * HALF + repeated : (k + 1) * HALF],
            ],
            axis=-1,
        ).astype(F32)
        for k in range(3)
    ]
    expert_results[2] = expert_results[2].T
    grad_query_weight, grad_expand_weight = head_sums(heads_in.reshape(128, 16, 512))
    beside = (grad_inputs, result, grad_query_weight, grad_expand_weight)
    final_in, beside = tie(final_in, beside)
    grad_inputs, result, grad_query_weight, grad_expand_weight = beside
    common_sum = jnp.sum(final_in.reshape(128, 16, PACKED).astype(F32), axis=0)
    return (
        result.astype(BF)[None],
        grad_inputs.astype(BF)[None],
        common_sum[:, 592],
        grad_query_weight,
        common_sum[:, :576],
        common_sum[0, 608:612],
        grad_expand_weight,
        grad_output_w,
        common_sum[:, 593],
        common_sum[:, 576:592],
        unit_results[0],
        unit_results[1],
        grad_sdown_w,
        expert_results[0][None],
        expert_results[1][None],
        expert_results[2][None],
    )


def solution(mesh):
    fine = Mesh(mesh.devices.reshape(4, 2, 2, 4, 2), ALL)
    return jax.shard_map(
        on_device,
        mesh=fine,
        in_specs=(
            P(FSDP, SEQ, None),
            P(FSDP, None),
            P(FSDP, SEQ, None),
            P(ALL),
            P(ALL, None),
            P(ALL, None),
            P(ALL),
            P(ALL, None),
            P(ALL, None),
            P(ALL),
            P(ALL, None),
            P(ALL, None),
            P(ALL, None),
            P(ALL, None),
            P(SEQ, FSDP, None),
            P(SEQ, FSDP, None),
            P(SEQ, None, FSDP),
            P(FSDP, SEQ, None),
        ),
        out_specs=(
            P(FSDP, SEQ, None),
            P(FSDP, SEQ, None),
            P(ALL),
            P(ALL, None),
            P(ALL, None),
            P(ALL),
            P(ALL, None),
            P(ALL, None),
            P(ALL),
            P(ALL, None),
            P(ALL, None),
            P(ALL, None),
            P(ALL, None),
            P(SEQ, FSDP, None),
            P(SEQ, FSDP, None),
            P(SEQ, None, FSDP),
        ),
        check_vma=False,
    )
```
